32 devices in a mesh: groups: 2 (over x), shard: 16 (over z, y, core).
Axes of the slice: x: 2, y: 2, z: 4, core: 2. Of those that a mesh axis runs over, the one named last changes fastest.
Arguments:
- tokens: bfloat16 [8192, 8192], P(('groups', 'shard')), parts along dimension 0, may hold values from -6 to 6
- cotangent: bfloat16 [8192, 1024], P(('groups', 'shard')), parts along dimension 0, may hold values from -6 to 6
- response_loss_mask: int32 [8192], P(('groups', 'shard')), parts along dimension 0, may hold values 0 or 1
- adapter_down_weight: bfloat16 [64, 8192], P(None, 'shard'), may hold values from -0.0625 to 0.0625
- projection: bfloat16 [65536, 4096], P('shard'), may hold values from -0.0234375 to 0.0234375
- targets: float32 [256, 4096], P(('groups', 'shard')), parts along dimension 0, may hold values from -6 to 6
Outputs:
- scores: float32 [32, 128], P('groups', 'shard'), parts along dimension 0
The draws below stay inside these ranges and needn't reach their ends.
There are 2 independent parts, one for each index of `groups`. The reference program is written for one: setup_inputs(seed, part) draws one part's arguments, and reference() takes and returns one part's arrays. A program takes and returns all parts, laid end to end along the dimension named above; an argument that names none is the same for every part. Nothing has to cross between parts.
All inputs are finite; a program needn't handle non-finite values. No bound on the sum of `response_loss_mask` on one device may be relied on, other than what follows from the above.
Results may differ from the reference program's by a relative error of at most 0.004.
Values may be sent and summed in bfloat16 or wider, within the bound.
No kernel may reach another device: no remote copies, remote signals or barrier semaphores. Data moves between devices by JAX's collectives and lax.ppermute only.
A program may use at most 128 MiB of HBM per device.

```python
import jax
import jax.numpy as jnp
from jax import lax

MODEL_WIDTH = 8192
KV = 1024
ADAPTER_RANK = 64
PDIM = 4096
LENGTH = 256
TOKENS = 4096
GRADIENT_ENTRIES = 65536
TARGETS = 128


def touch_ends(entries, stream_key, smallest, high):
    dims = entries.shape
    place = [jax.random.randint(jax.random.fold_in(stream_key, axis), (), 0, dims[axis]) for axis in range(len(dims))]
    entries = entries.at[tuple(place)].set(smallest)
    longest = dims.index(max(dims))
    place[longest] = (place[longest] + 1) % dims[longest]
    return entries.at[tuple(place)].set(high)


def shard_levels(stream_key, extent, cuts, low, largest):
    def one(dim, blocks):
        steps = jax.random.uniform(jax.random.fold_in(jax.random.fold_in(stream_key, 6), dim), (blocks,), jnp.float32, low / len(cuts), largest / len(cuts))
        return jnp.repeat(jnp.exp(steps), extent[dim] // blocks).reshape((-1,) + (1,) * (len(extent) - dim - 1))

    factor_of = one(*cuts[0])
    for cut in cuts[1:]:
        factor_of = factor_of * one(*cut)
    return factor_of


def gaussian(key, extent, spread, bound, shards=(), kind=jnp.bfloat16):
    factor_of = shard_levels(key, extent, shards, -0.22, 0.18) if shards else 1.0
    drawn = jax.random.normal(key, extent, jnp.float32) * spread * factor_of
    return jnp.minimum(jnp.maximum(drawn, -bound), bound).astype(kind)


def setup_inputs(seed: int = 0, part: int = 0) -> dict:
    streams_of = jax.random.split(jax.random.key(seed), 7)
    part_splits = jax.random.split(jax.random.fold_in(streams_of[6], part), 7)
    return {
        "tokens": gaussian(part_splits[0], (TOKENS, MODEL_WIDTH), 1.0, 6.0, ((0, 16),)),
        "cotangent": gaussian(part_splits[1], (TOKENS, KV), 1.0, 6.0, ((0, 16),)),
        "response_loss_mask": touch_ends((jax.random.randint(part_splits[2], (TOKENS,), 0, 4) < 3).astype(jnp.int32), jax.random.fold_in(part_splits[2], 1), 0, 1),
        "adapter_down_weight": gaussian(streams_of[3], (ADAPTER_RANK, MODEL_WIDTH), MODEL_WIDTH ** -0.5, 0.0625, ((1, 16),)),
        "projection": gaussian(streams_of[4], (GRADIENT_ENTRIES, PDIM), GRADIENT_ENTRIES ** -0.5, 0.0234375, ((0, 16),)),
        "targets": gaussian(part_splits[5], (TARGETS, PDIM), 1.0, 6.0, ((0, 16),), jnp.float32),
    }


def unit_rows(values):
    return values * lax.rsqrt(lax.optimization_barrier(jnp.mean(values * values, axis=1, keepdims=True)) + 1e-06)

def reference(tokens, cotangent, response_loss_mask, adapter_down_weight, projection, targets):
    count = TOKENS // LENGTH
    low_rank_activations = jnp.dot(tokens, adapter_down_weight.T, preferred_element_type=jnp.float32).astype(jnp.bfloat16)
    weighted = cotangent * response_loss_mask.astype(jnp.bfloat16)[:, None]
    left = weighted.reshape(count, LENGTH, KV).astype(jnp.float32)
    right = low_rank_activations.reshape(count, LENGTH, ADAPTER_RANK).astype(jnp.float32)
    grads = jnp.einsum('elo,elr->eor', left, right)
    flat = grads.reshape(count, KV * ADAPTER_RANK).astype(jnp.bfloat16)
    features = jnp.dot(flat, projection, preferred_element_type=jnp.float32)
    unit_f = unit_rows(features)
    unit_t = unit_rows(targets)
    return jnp.dot(unit_f, unit_t.T, precision=lax.Precision.HIGHEST) / PDIM
```

```python
import functools

import jax
import jax.numpy as jnp
from jax import lax
from jax.experimental import pallas as pl
from jax.experimental.pallas import tpu as pltpu
from jax.sharding import PartitionSpec as P

PDIM = 4096
LENGTH = 256
MIB = 1 << 20
NT = (((1,), (1,)), ((), ()))
VMEM = pl.BlockSpec(memory_space=pltpu.VMEM)
SMEM = pl.BlockSpec(memory_space=pltpu.SMEM)


def split_axis(n):
    near = 2 if n >= 4 else 1
    core = 2 if n >= 2 else 1
    return n // (near * core), near, core


def permute(value, n, move):
    return lax.ppermute(value, "shard", [(s, move(s)) for s in range(n)])


def gather_blocks(block, n):
    far, near, core = split_axis(n)
    me = lax.axis_index("shard")
    z, y, c = me // (near * core), (me // core) % near, me % core
    held = [(block, z, y, c)]
    if near == 2:
        held.append((permute(block, n, lambda s: s ^ core), z, 1 - y, c))
    for d in range(1, far):
        for item, hz, hy, hc in list(held[:near]):
            moved = permute(item, n, lambda s: (s + d * near * core) % n)
            held.append((moved, (z - d + far) % far, hy, hc))
    if core == 2:
        held += [(permute(item, n, lambda s: s ^ 1), hz, hy, 1 - hc) for item, hz, hy, hc in list(held)]
    owners = jnp.stack([(hz * near + hy) * core + hc for _, hz, hy, hc in held])
    return [h[0] for h in held], owners.astype(jnp.int32)


def grads_kernel(count, owners, *refs):
    blocks = refs[:count]
    tokens, cotangent, mask, out, grads = refs[count:]
    depth = blocks[0].shape[1]
    rank = blocks[0].shape[0]
    total = jnp.zeros((rank, tokens.shape[0]), jnp.float32)
    for i, block in enumerate(blocks):
        start = pl.multiple_of(owners[i] * depth, depth)
        total += lax.dot_general(
            block[...], tokens[:, pl.ds(start, depth)], NT, preferred_element_type=jnp.float32
        )
    lowrank = total.astype(jnp.bfloat16) * mask[...].astype(jnp.bfloat16)
    turned = jnp.dot(lowrank, cotangent[...], preferred_element_type=jnp.float32)
    grads[...] = turned.T
    rows, lanes = out.shape
    pack = lanes // rank
    for q in range(pack):
        out[:, q * rank : (q + 1) * rank] = grads[pl.ds(q, rows, stride=pack), :].astype(jnp.bfloat16)


def packed_grads(blocks, owners, tokens, cotangent, mask):
    rank, width = blocks[0].shape[0], cotangent.shape[1]
    lanes = 256
    rows = width * rank // lanes
    return pl.pallas_call(
        functools.partial(grads_kernel, len(blocks)),
        out_shape=jax.ShapeDtypeStruct((rows, lanes), jnp.bfloat16),
        in_specs=[SMEM] + [VMEM] * (len(blocks) + 3),
        out_specs=VMEM,
        scratch_shapes=[pltpu.VMEM((width, rank), jnp.float32)],
        compiler_params=pltpu.CompilerParams(vmem_limit_bytes=24 * MIB),
        name="grads",
    )(owners, *blocks, tokens, cotangent, mask.reshape(1, -1))


def partial_kernel(devices, parts, targets, out):
    count = parts.shape[0] // devices
    width = parts.shape[1]
    features = jnp.zeros((count, width), jnp.float32)
    for s in range(devices):
        features += parts[s * count : (s + 1) * count, :].astype(jnp.float32)
    high = lax.Precision.HIGHEST
    dots = lax.dot_general(targets[...], features, NT, precision=high, preferred_element_type=jnp.float32)
    ones = jnp.ones(targets.shape, jnp.float32)
    squares = lax.dot_general(ones, features * features, NT, precision=high, preferred_element_type=jnp.float32)
    rest = jnp.zeros((targets.shape[0], out.shape[1] - 2 * count), jnp.float32)
    out[...] = jnp.concatenate([dots, squares, rest], axis=1) if rest.shape[1] else jnp.concatenate([dots, squares], axis=1)


def body(tokens, cotangent, response_loss_mask, adapter_down_weight, projection, targets):
    devices = lax.axis_size("shard")
    count = devices * (tokens.shape[0] // LENGTH)
    target_cols = lax.all_to_all(targets, "shard", split_axis=1, concat_axis=0, tiled=True)
    blocks, owners = gather_blocks(adapter_down_weight, devices)
    packed = packed_grads(blocks, owners, tokens, cotangent, response_loss_mask)
    rows = packed.reshape(devices, -1)
    rows = lax.all_to_all(rows, "shard", split_axis=0, concat_axis=0, tiled=True)
    partial = jnp.dot(rows, projection, preferred_element_type=jnp.float32).astype(jnp.bfloat16)
    parts = lax.all_to_all(partial, "shard", split_axis=1, concat_axis=0, tiled=True)
    sums = pl.pallas_call(
        functools.partial(partial_kernel, devices),
        out_shape=jax.ShapeDtypeStruct((target_cols.shape[0], 128), jnp.float32),
        in_specs=[VMEM, VMEM],
        out_specs=VMEM,
        name="partial_scores",
    )(parts, target_cols)
    arrived = lax.all_to_all(sums, "shard", split_axis=0, concat_axis=0, tiled=True)
    total = jnp.sum(arrived.reshape(devices, targets.shape[0], -1), axis=0)
    scale_f = lax.rsqrt(total[:, count : 2 * count] / PDIM + 1e-06)
    scale_t = lax.rsqrt(jnp.mean(targets * targets, axis=1, keepdims=True) + 1e-06)
    return (total[:, :count] * scale_f * scale_t / PDIM).T


def solution(mesh):
    in_specs = (
        P(("groups", "shard"), None),
        P(("groups", "shard"), None),
        P(("groups", "shard")),
        P(None, "shard"),
        P("shard", None),
        P(("groups", "shard"), None),
    )
    out_specs = P("groups", "shard")
    return jax.shard_map(body, mesh=mesh, in_specs=in_specs, out_specs=out_specs, check_vma=False)
```

```python
import functools

import jax
import jax.numpy as jnp
from jax import lax
from jax.experimental import pallas as pl
from jax.experimental.pallas import tpu as pltpu
from jax.sharding import PartitionSpec as P

PDIM = 4096
LENGTH = 256
LANES = 256
MIB = 1 << 20
NT = (((1,), (1,)), ((), ()))
VMEM = pl.BlockSpec(memory_space=pltpu.VMEM)
SMEM = pl.BlockSpec(memory_space=pltpu.SMEM)
ANY = pl.BlockSpec(memory_space=pl.ANY)


def swap(value, bit, n):
    return lax.ppermute(value, "shard", [(s, s ^ bit) for s in range(n)])


def gather_blocks(block, n):
    held = {0: block}
    bit = n // 2
    while bit >= 1:
        for k in list(held):
            held[k ^ bit] = swap(held[k], bit, n)
        bit //= 2
    return [held[k] for k in range(n)]


def grads_kernel(n, me, *refs):
    blocks = refs[:n]
    tokens_hbm, cotangent_hbm, mask = refs[n : n + 3]
    outs = refs[n + 3 : n + 3 + n // 2]
    tokens, cotangent, grads, sems = refs[n + 3 + n // 2 :]
    rank, depth = blocks[0].shape
    width = tokens.shape[1]
    pieces = 4
    piece = tokens.shape[0] // pieces
    copies = [
        pltpu.make_async_copy(tokens_hbm.at[pl.ds(i * piece, piece)], tokens.at[pl.ds(i * piece, piece)], sems.at[i])
        for i in range(pieces)
    ]
    copies.append(pltpu.make_async_copy(cotangent_hbm, cotangent, sems.at[pieces]))
    for copy in copies:
        copy.start()
    for copy in copies:
        copy.wait()
    total = jnp.zeros((rank, tokens.shape[0]), jnp.float32)
    for k, block in enumerate(blocks):
        start = pl.multiple_of((me[0] ^ k) * depth, depth)
        total += lax.dot_general(
            block[...], tokens[:, pl.ds(start, depth)], NT, preferred_element_type=jnp.float32
        )
    lowrank = total.astype(jnp.bfloat16) * mask[...].astype(jnp.bfloat16)
    turned = jnp.dot(lowrank, cotangent[...], preferred_element_type=jnp.float32)
    grads[...] = turned.T
    pack = LANES // rank
    share = outs[0].shape[1]
    for k in range(n):
        start = pl.multiple_of((me[0] ^ k) * (share * pack), share * pack)
        for q in range(pack):
            rows = grads[pl.ds(start + q, share, stride=pack), :]
            outs[k // 2][k % 2, :, q * rank : (q + 1) * rank] = rows.astype(jnp.bfloat16)


def packed_grads(me, blocks, tokens, cotangent, mask):
    n = len(blocks)
    rank, width = blocks[0].shape[0], cotangent.shape[1]
    rows = width * rank // LANES
    shape = jax.ShapeDtypeStruct((2, rows // n, LANES), jnp.bfloat16)
    return pl.pallas_call(
        functools.partial(grads_kernel, n),
        out_shape=[shape] * (n // 2),
        in_specs=[SMEM] + [VMEM] * n + [ANY, ANY, VMEM],
        out_specs=[VMEM] * (n // 2),
        scratch_shapes=[
            pltpu.VMEM(tokens.shape, tokens.dtype),
            pltpu.VMEM(cotangent.shape, cotangent.dtype),
            pltpu.VMEM((width, rank), jnp.float32),
            pltpu.SemaphoreType.DMA((5,)),
        ],
        compiler_params=pltpu.CompilerParams(vmem_limit_bytes=24 * MIB),
        cost_estimate=pl.CostEstimate(flops=300000000, bytes_accessed=5000000, transcendentals=0),
        name="grads",
    )(me, *blocks, tokens, cotangent, mask.reshape(1, -1))


def features_kernel(n, me, *refs):
    own = refs[: n // 2]
    other, weights_hbm, keep, send, x, weights, total, sems = refs[n // 2 :]
    share = own[0].shape[1]
    pitch = x.shape[1] // n
    copies = [
        pltpu.make_async_copy(weights_hbm.at[pl.ds(j * LANES, LANES)], weights.at[pl.ds(j * LANES, LANES)], sems.at[j])
        for j in range(share)
    ]
    for copy in copies:
        copy.start()
    for k in range(n):
        start = pl.multiple_of((me[0] ^ k) * pitch, pitch)
        rows = own[k // 2][0] if k % 2 == 0 else other[k // 2]
        for h in range(x.shape[0]):
            x[h, pl.ds(start, share), :] = rows[:, h * 128 : (h + 1) * 128].astype(jnp.float32)
    for j, copy in enumerate(copies):
        left = jnp.concatenate([x[h, pl.ds(j, n, stride=pitch), :] for h in range(x.shape[0])], axis=1)
        left = left.astype(jnp.bfloat16)
        copy.wait()
        term = jnp.dot(left, weights[pl.ds(j * LANES, LANES), :], preferred_element_type=jnp.float32)
        if j == 0:
            total[...] = term
        else:
            total[...] += term
    half = keep.shape[1]
    mine = pl.multiple_of((me[0] & 1) * half, half)
    partner = pl.multiple_of((1 - (me[0] & 1)) * half, half)
    keep[...] = total[:, pl.ds(mine, half)]
    send[...] = total[:, pl.ds(partner, half)].astype(jnp.bfloat16)


def partial_features(me, own, other, projection):
    n = 2 * len(own)
    depth, width = projection.shape
    half = (n, width // 2)
    return pl.pallas_call(
        functools.partial(features_kernel, n),
        out_shape=[jax.ShapeDtypeStruct(half, jnp.float32), jax.ShapeDtypeStruct(half, jnp.bfloat16)],
        in_specs=[SMEM] + [VMEM] * (n // 2 + 1) + [ANY],
        out_specs=[VMEM, VMEM],
        scratch_shapes=[
            pltpu.VMEM((LANES // 128, n * max(depth // LANES, 8), 128), jnp.float32),
            pltpu.VMEM(projection.shape, projection.dtype),
            pltpu.VMEM((n, width), jnp.float32),
            pltpu.SemaphoreType.DMA((depth // LANES,)),
        ],
        compiler_params=pltpu.CompilerParams(vmem_limit_bytes=44 * MIB),
        cost_estimate=pl.CostEstimate(flops=600000000, bytes_accessed=34000000, transcendentals=0),
        name="features",
    )(me, *own, other, projection)


def scores_kernel(me, kept, arrived, targets, partner_targets, mine, send):
    features = kept[...] + arrived[...].astype(jnp.float32)
    count, half = features.shape
    start = pl.multiple_of((me[0] & 1) * half, half)
    high = lax.Precision.HIGHEST
    ones = jnp.ones((targets.shape[0], half), jnp.float32)
    squares = lax.dot_general(ones, features * features, NT, precision=high, preferred_element_type=jnp.float32)
    rest = jnp.zeros((targets.shape[0], mine.shape[1] - 2 * count), jnp.float32)
    for source, out in ((targets, mine), (partner_targets, send)):
        scale = lax.rsqrt(jnp.sum(source[...] * source[...], axis=1, keepdims=True) / PDIM + 1e-06)
        dots = lax.dot_general(
            source[:, pl.ds(start, half)], features, NT, precision=high, preferred_element_type=jnp.float32
        )
        parts = [dots * scale, squares] + ([rest] if rest.shape[1] else [])
        out[...] = jnp.concatenate(parts, axis=1)


def partial_scores(me, kept, arrived, targets, partner_targets):
    shape = jax.ShapeDtypeStruct((targets.shape[0], 128), jnp.float32)
    return pl.pallas_call(
        scores_kernel,
        out_shape=[shape, shape],
        in_specs=[SMEM] + [VMEM] * 4,
        out_specs=[VMEM, VMEM],
        name="partial_scores",
    )(me, kept, arrived, targets, partner_targets)


def body(tokens, cotangent, response_loss_mask, adapter_down_weight, projection, targets):
    n = lax.axis_size("shard")
    me = lax.axis_index("shard").astype(jnp.int32).reshape(1)
    partner_targets = swap(targets, 1, n)
    blocks = gather_blocks(adapter_down_weight, n)
    groups = packed_grads(me, blocks, tokens, cotangent, response_loss_mask)
    arrived = [groups[0]] + [swap(groups[q], 2 * q, n) for q in range(1, n // 2)]
    other = swap(jnp.stack([rows[1] for rows in arrived]), 1, n)
    kept, send = partial_features(me, arrived, other, projection)
    kept = kept + swap(send, 1, n).astype(jnp.float32)
    bit = 2
    while bit < n:
        came = swap(kept.astype(jnp.bfloat16), bit, n)
        bit *= 2
        if bit < n:
            kept = kept + came.astype(jnp.float32)
    mine, send = partial_scores(me, kept, came, targets, partner_targets)
    total = mine + swap(send, 1, n)
    scale = lax.rsqrt(total[:, n : 2 * n] / PDIM + 1e-06)
    return (total[:, :n] * scale / PDIM).T


def solution(mesh):
    in_specs = (
        P(("groups", "shard"), None),
        P(("groups", "shard"), None),
        P(("groups", "shard")),
        P(None, "shard"),
        P("shard", None),
        P(("groups", "shard"), None),
    )
    out_specs = P("groups", "shard")
    return jax.shard_map(body, mesh=mesh, in_specs=in_specs, out_specs=out_specs, check_vma=False)
```

```python
import functools

import jax
import jax.numpy as jnp
from jax import lax
from jax.experimental import pallas as pl
from jax.experimental.pallas import tpu as pltpu
from jax.sharding import PartitionSpec as P

PDIM = 4096
LENGTH = 256
LANES = 256
NEAR = 4
MIB = 1 << 20
NT = (((1,), (1,)), ((), ()))
VMEM = pl.BlockSpec(memory_space=pltpu.VMEM)
SMEM = pl.BlockSpec(memory_space=pltpu.SMEM)
ANY = pl.BlockSpec(memory_space=pl.ANY)


def swap(value, bit, n):
    return lax.ppermute(value, "shard", [(s, s ^ bit) for s in range(n)])


def exchange_far(value, n):
    groups = [[z * NEAR + i for z in range(n // NEAR)] for i in range(NEAR)]
    return lax.all_to_all(value, "shard", 0, 0, axis_index_groups=groups, tiled=True)


def exchange_near(value, n, axis=0):
    groups = [[z * NEAR + i for i in range(NEAR)] for z in range(n // NEAR)]
    return lax.all_to_all(value, "shard", axis, axis, axis_index_groups=groups, tiled=True)


def gather_blocks(block, n):
    far = exchange_far(jnp.broadcast_to(block, (n // NEAR,) + block.shape), n)
    across = swap(far, 2, n)
    return [far, swap(far, 1, n), across, swap(across, 1, n)]


def in_hbm(value):
    return pltpu.with_memory_space_constraint(value, pltpu.HBM)


def grads_kernel(me, *refs):
    blocks = refs[:NEAR]
    tokens_hbm, cotangent_hbm, mask_hbm, out, tokens, cotangent, mask, grads, sems = refs[NEAR:]
    far, rank, depth = blocks[0].shape
    pieces = 4
    piece = tokens.shape[0] // pieces
    copies = [
        pltpu.make_async_copy(tokens_hbm.at[pl.ds(i * piece, piece)], tokens.at[pl.ds(i * piece, piece)], sems.at[i])
        for i in range(pieces)
    ]
    copies.append(pltpu.make_async_copy(cotangent_hbm, cotangent, sems.at[pieces]))
    copies.append(pltpu.make_async_copy(mask_hbm, mask, sems.at[pieces + 1]))
    for copy in copies:
        copy.start()
    for copy in copies:
        copy.wait()
    total = jnp.zeros((rank, tokens.shape[0]), jnp.float32)
    for k, block in enumerate(blocks):
        for z in range(far):
            owner = z * NEAR + ((me[0] & (NEAR - 1)) ^ k)
            start = pl.multiple_of(owner * depth, depth)
            total += lax.dot_general(
                block[z], tokens[:, pl.ds(start, depth)], NT, preferred_element_type=jnp.float32
            )
    lowrank = total.astype(jnp.bfloat16) * mask[...].astype(jnp.bfloat16)
    turned = jnp.dot(lowrank, cotangent[...], preferred_element_type=jnp.float32)
    grads[...] = turned.T
    pack = LANES // rank
    share = out.shape[2]
    for z in range(far):
        for i in range(NEAR):
            for q in range(pack):
                start = (z * NEAR + i) * share * pack + q
                rows = grads[pl.ds(start, share, stride=pack), :]
                out[z, i, :, q * rank : (q + 1) * rank] = rows.astype(jnp.bfloat16)


def packed_grads(me, blocks, tokens, cotangent, mask):
    far, rank, _ = blocks[0].shape
    width = cotangent.shape[1]
    rows = width * rank // LANES
    return pl.pallas_call(
        grads_kernel,
        out_shape=jax.ShapeDtypeStruct((far, NEAR, rows // (far * NEAR), LANES), jnp.bfloat16),
        in_specs=[SMEM] + [VMEM] * NEAR + [ANY, ANY, ANY],
        out_specs=VMEM,
        scratch_shapes=[
            pltpu.VMEM(tokens.shape, tokens.dtype),
            pltpu.VMEM(cotangent.shape, cotangent.dtype),
            pltpu.VMEM((1, mask.shape[0]), mask.dtype),
            pltpu.VMEM((width, rank), jnp.float32),
            pltpu.SemaphoreType.DMA((6,)),
        ],
        compiler_params=pltpu.CompilerParams(vmem_limit_bytes=32 * MIB),
        cost_estimate=pl.CostEstimate(flops=300000000, bytes_accessed=5000000, transcendentals=0),
        name="grads",
    )(me, *blocks, in_hbm(tokens), in_hbm(cotangent), in_hbm(mask.reshape(1, -1)))


def features_kernel(me, rows, weights_hbm, send, keep, x, weights, total, sems):
    near, far, share, _ = rows.shape
    n = near * far
    pitch = x.shape[1] // n
    copies = [
        pltpu.make_async_copy(weights_hbm.at[pl.ds(j * LANES, LANES)], weights.at[pl.ds(j * LANES, LANES)], sems.at[j])
        for j in range(share)
    ]
    for copy in copies:
        copy.start()
    for i in range(near):
        for z in range(far):
            for h in range(x.shape[0]):
                part = rows[i, z, :, h * 128 : (h + 1) * 128]
                x[h, pl.ds((z * near + i) * pitch, share), :] = part.astype(jnp.float32)
    for j, copy in enumerate(copies):
        left = jnp.concatenate([x[h, pl.ds(j, n, stride=pitch), :] for h in range(x.shape[0])], axis=1)
        left = left.astype(jnp.bfloat16)
        copy.wait()
        term = jnp.dot(left, weights[pl.ds(j * LANES, LANES), :], preferred_element_type=jnp.float32)
        if j == 0:
            total[...] = term
        else:
            total[...] += term
    part = keep.shape[1]
    for i in range(near):
        send[i] = total[:, i * part : (i + 1) * part].astype(jnp.bfloat16)
    start = pl.multiple_of((me[0] & (near - 1)) * part, part)
    keep[...] = total[:, pl.ds(start, part)]


def partial_features(me, rows, projection):
    near, far, share, _ = rows.shape
    n = near * far
    depth, width = projection.shape
    part = width // near
    return pl.pallas_call(
        features_kernel,
        out_shape=[
            jax.ShapeDtypeStruct((near, n, part), jnp.bfloat16),
            jax.ShapeDtypeStruct((n, part), jnp.float32),
        ],
        in_specs=[SMEM, VMEM, ANY],
        out_specs=[VMEM, VMEM],
        scratch_shapes=[
            pltpu.VMEM((LANES // 128, n * max(share, 8), 128), jnp.float32),
            pltpu.VMEM(projection.shape, projection.dtype),
            pltpu.VMEM((n, width), jnp.float32),
            pltpu.SemaphoreType.DMA((share,)),
        ],
        compiler_params=pltpu.CompilerParams(vmem_limit_bytes=44 * MIB),
        cost_estimate=pl.CostEstimate(flops=600000000, bytes_accessed=34000000, transcendentals=0),
        name="features",
    )(me, rows, projection)


def add_others(kept, came, own):
    total = kept[...]
    for i in range(came.shape[0]):
        term = came[i].astype(jnp.float32)
        total += jnp.where(own == i, jnp.zeros_like(term), term)
    return total


def near_sum_kernel(me, kept, came, keep, send):
    total = add_others(kept, came, me[0] & (NEAR - 1))
    keep[...] = total
    for z in range(send.shape[0]):
        send[z] = total.astype(jnp.bfloat16)


def near_sum(me, kept, came, n):
    return pl.pallas_call(
        near_sum_kernel,
        out_shape=[
            jax.ShapeDtypeStruct(kept.shape, jnp.float32),
            jax.ShapeDtypeStruct((n // NEAR,) + kept.shape, jnp.bfloat16),
        ],
        in_specs=[SMEM, VMEM, VMEM],
        out_specs=[VMEM, VMEM],
        name="near_sum",
    )(me, kept, came)


def scores_kernel(me, kept, came, targets, out):
    features = add_others(kept, came, me[0] // NEAR)
    near, rows, width = targets.shape
    count = features.shape[0]
    high = lax.Precision.HIGHEST
    ones = jnp.ones((rows, width), jnp.float32)
    squares = lax.dot_general(ones, features * features, NT, precision=high, preferred_element_type=jnp.float32)
    flat = targets[...].reshape(near * rows, width)
    dots = lax.dot_general(flat, features, NT, precision=high, preferred_element_type=jnp.float32)
    for i in range(near):
        out[i, :, :count] = dots[i * rows : (i + 1) * rows, :]
        out[i, :, count : 2 * count] = squares
        if 2 * count < out.shape[2]:
            out[i, :, 2 * count :] = jnp.zeros((rows, out.shape[2] - 2 * count), jnp.float32)


def partial_scores(me, kept, came, targets):
    return pl.pallas_call(
        scores_kernel,
        out_shape=jax.ShapeDtypeStruct(targets.shape[:2] + (128,), jnp.float32),
        in_specs=[SMEM] + [VMEM] * 3,
        out_specs=VMEM,
        name="partial_scores",
    )(me, kept, came, targets)


def finish_kernel(parts, targets, out):
    total = parts[0]
    for i in range(1, parts.shape[0]):
        total += parts[i]
    count = out.shape[1]
    scale_t = lax.rsqrt(jnp.sum(targets[...] * targets[...], axis=1, keepdims=True) / PDIM + 1e-06)
    scale_f = lax.rsqrt(total[:, count : 2 * count] / PDIM + 1e-06)
    out[...] = total[:, :count] * scale_f * scale_t / PDIM


def body(tokens, cotangent, response_loss_mask, adapter_down_weight, projection, targets):
    n = lax.axis_size("shard")
    me = lax.axis_index("shard").astype(jnp.int32).reshape(1)
    rows = targets.shape[0]
    target_parts = exchange_near(targets.reshape(rows, NEAR, -1).transpose(1, 0, 2), n)
    blocks = gather_blocks(adapter_down_weight, n)
    packed = packed_grads(me, blocks, tokens, cotangent, response_loss_mask)
    packed = exchange_far(packed, n).transpose(1, 0, 2, 3)
    send, kept = partial_features(me, exchange_near(packed, n), projection)
    kept, send = near_sum(me, kept, exchange_near(send, n), n)
    parts = partial_scores(me, kept, exchange_far(send, n), target_parts)
    scores = pl.pallas_call(
        finish_kernel,
        out_shape=jax.ShapeDtypeStruct((rows, n), jnp.float32),
        in_specs=[VMEM, VMEM],
        out_specs=VMEM,
        name="finish",
    )(exchange_near(parts, n), targets)
    return scores.T


def solution(mesh):
    in_specs = (
        P(("groups", "shard"), None),
        P(("groups", "shard"), None),
        P(("groups", "shard")),
        P(None, "shard"),
        P("shard", None),
        P(("groups", "shard"), None),
    )
    out_specs = P("groups", "shard")
    return jax.shard_map(body, mesh=mesh, in_specs=in_specs, out_specs=out_specs, check_vma=False)
```

```python
import functools

import jax
import jax.numpy as jnp
from jax import lax
from jax.experimental import pallas as pl
from jax.experimental.pallas import tpu as pltpu
from jax.sharding import PartitionSpec as P

PDIM = 4096
LENGTH = 256
LANES = 256
MIB = 1 << 20
NT = (((1,), (1,)), ((), ()))
VMEM = pl.BlockSpec(memory_space=pltpu.VMEM)
SMEM = pl.BlockSpec(memory_space=pltpu.SMEM)
ANY = pl.BlockSpec(memory_space=pl.ANY)


def swap(value, bit, n):
    return lax.ppermute(value, "shard", [(s, s ^ bit) for s in range(n)])


def gather_blocks(block, n):
    held = {0: block}
    bit = n // 2
    while bit >= 1:
        for k in list(held):
            held[k ^ bit] = swap(held[k], bit, n)
        bit //= 2
    return [held[k] for k in range(n)]


def in_hbm(value):
    return pltpu.with_memory_space_constraint(value, pltpu.HBM)


def load_kernel(count, starts, *refs):
    sources, outs, sems = refs[:count], refs[-1 - count : -1], refs[-1]
    copies = [
        pltpu.make_async_copy(source.at[pl.ds(start, out.shape[0])], out, sems.at[i])
        for i, (source, start, out) in enumerate(zip(sources, starts, outs))
    ]
    for copy in copies:
        copy.start()
    for copy in copies:
        copy.wait()


def load(name, parts, after=()):
    size = sum(rows * array.size // array.shape[0] * array.dtype.itemsize for array, _, rows in parts)
    return pl.pallas_call(
        functools.partial(load_kernel, len(parts), [start for _, start, _ in parts]),
        out_shape=[pltpu.VMEM((rows,) + array.shape[1:], array.dtype) for array, _, rows in parts],
        in_specs=[ANY] * (len(parts) + len(after)),
        out_specs=[VMEM] * len(parts),
        scratch_shapes=[pltpu.SemaphoreType.DMA((len(parts),))],
        compiler_params=pltpu.CompilerParams(vmem_limit_bytes=MIB),
        cost_estimate=pl.CostEstimate(flops=0, bytes_accessed=2 * size, transcendentals=0),
        name=name,
    )(*[in_hbm(array) for array, _, _ in parts], *after)


def grads_kernel(n, me, *refs):
    blocks = refs[:n]
    tokens, cotangent, mask, _, out, grads = refs[n:]
    rank, depth = blocks[0].shape
    total = jnp.zeros((rank, tokens.shape[0]), jnp.float32)
    for k, block in enumerate(blocks):
        start = pl.multiple_of((me[0] ^ k) * depth, depth)
        total += lax.dot_general(
            block[...], tokens[:, pl.ds(start, depth)], NT, preferred_element_type=jnp.float32
        )
    lowrank = total.astype(jnp.bfloat16) * mask[...].astype(jnp.bfloat16)
    turned = jnp.dot(lowrank, cotangent[...], preferred_element_type=jnp.float32)
    grads[...] = turned.T
    pack = LANES // rank
    share = out.shape[1]
    for k in range(n):
        for q in range(pack):
            rows = grads[pl.ds(k * share * pack + q, share, stride=pack), :]
            out[k, :, q * rank : (q + 1) * rank] = rows.astype(jnp.bfloat16)


def packed_grads(me, blocks, tokens, cotangent, mask, after):
    n = len(blocks)
    rank, width = blocks[0].shape[0], cotangent.shape[1]
    return pl.pallas_call(
        functools.partial(grads_kernel, n),
        out_shape=jax.ShapeDtypeStruct((n, width * rank // LANES // n, LANES), jnp.bfloat16),
        in_specs=[SMEM] + [VMEM] * (n + 3) + [ANY],
        out_specs=VMEM,
        scratch_shapes=[pltpu.VMEM((width, rank), jnp.float32)],
        compiler_params=pltpu.CompilerParams(vmem_limit_bytes=6 * MIB),
        cost_estimate=pl.CostEstimate(flops=300000000, bytes_accessed=5000000, transcendentals=0),
        name="grads",
    )(me, *blocks, tokens, cotangent, mask, after)


def features_kernel(me, rows, *refs):
    weights = refs[:-4]
    keep, send, x, total = refs[-4:]
    n, share, _ = rows.shape
    pitch = x.shape[1] // n
    for k in range(n):
        for h in range(x.shape[0]):
            x[h, pl.ds(k * pitch, share), :] = rows[k, :, h * 128 : (h + 1) * 128].astype(jnp.float32)
    j = 0
    for part in weights:
        for i in range(part.shape[0] // LANES):
            left = jnp.concatenate([x[h, pl.ds(j, n, stride=pitch), :] for h in range(x.shape[0])], axis=1)
            left = left.astype(jnp.bfloat16)
            term = jnp.dot(left, part[i * LANES : (i + 1) * LANES, :], preferred_element_type=jnp.float32)
            if j == 0:
                total[...] = term
            else:
                total[...] += term
            j += 1
    half = keep.shape[1]
    mine = pl.multiple_of((me[0] & 1) * half, half)
    partner = pl.multiple_of((1 - (me[0] & 1)) * half, half)
    keep[...] = total[:, pl.ds(mine, half)]
    send[...] = total[:, pl.ds(partner, half)].astype(jnp.bfloat16)


def partial_features(me, rows, weights):
    n, share, _ = rows.shape
    width = weights[0].shape[1]
    half = (n, width // 2)
    return pl.pallas_call(
        features_kernel,
        out_shape=[jax.ShapeDtypeStruct(half, jnp.float32), jax.ShapeDtypeStruct(half, jnp.bfloat16)],
        in_specs=[SMEM] + [VMEM] * (1 + len(weights)),
        out_specs=[VMEM, VMEM],
        scratch_shapes=[
            pltpu.VMEM((LANES // 128, n * max(share, 8), 128), jnp.float32),
            pltpu.VMEM((n, width), jnp.float32),
        ],
        compiler_params=pltpu.CompilerParams(vmem_limit_bytes=6 * MIB),
        cost_estimate=pl.CostEstimate(flops=600000000, bytes_accessed=34000000, transcendentals=0),
        name="features",
    )(me, rows, *weights)


def scores_kernel(me, kept, arrived, targets, partner_targets, mine, send):
    features = kept[...] + arrived[...].astype(jnp.float32)
    count, half = features.shape
    start = pl.multiple_of((me[0] & 1) * half, half)
    high = lax.Precision.HIGHEST
    ones = jnp.ones((targets.shape[0], half), jnp.float32)
    squares = lax.dot_general(ones, features * features, NT, precision=high, preferred_element_type=jnp.float32)
    rest = jnp.zeros((targets.shape[0], mine.shape[1] - 2 * count), jnp.float32)
    for source, out in ((targets, mine), (partner_targets, send)):
        scale = lax.rsqrt(jnp.sum(source[...] * source[...], axis=1, keepdims=True) / PDIM + 1e-06)
        dots = lax.dot_general(
            source[:, pl.ds(start, half)], features, NT, precision=high, preferred_element_type=jnp.float32
        )
        parts = [dots * scale, squares] + ([rest] if rest.shape[1] else [])
        out[...] = jnp.concatenate(parts, axis=1)


def partial_scores(me, kept, arrived, targets, partner_targets):
    shape = jax.ShapeDtypeStruct((targets.shape[0], 128), jnp.float32)
    return pl.pallas_call(
        scores_kernel,
        out_shape=[shape, shape],
        in_specs=[SMEM] + [VMEM] * 4,
        out_specs=[VMEM, VMEM],
        compiler_params=pltpu.CompilerParams(vmem_limit_bytes=6 * MIB),
        name="partial_scores",
    )(me, kept, arrived, targets, partner_targets)


def body(tokens, cotangent, response_loss_mask, adapter_down_weight, projection, targets):
    n = lax.axis_size("shard")
    me = lax.axis_index("shard").astype(jnp.int32).reshape(1)
    partner_targets = swap(targets, 1, n)
    blocks = gather_blocks(adapter_down_weight, n)
    chunks = projection.shape[0] // LANES
    first = chunks * 3 // 8 * LANES
    tokens, cotangent, mask, head = load(
        "load_first",
        [(tokens, 0, tokens.shape[0]), (cotangent, 0, cotangent.shape[0])]
        + [(response_loss_mask.reshape(1, -1), 0, 1), (projection, 0, first)],
    )
    packed = packed_grads(me, blocks, tokens, cotangent, mask, partner_targets)
    rows = lax.all_to_all(packed, "shard", 0, 0, tiled=True)
    (tail,) = load("load_rest", [(projection, first, projection.shape[0] - first)], (packed,))
    kept, send = partial_features(me, rows, (head, tail))
    kept = kept + swap(send, 1, n).astype(jnp.float32)
    bit = 2
    while bit < n:
        came = swap(kept.astype(jnp.bfloat16), bit, n)
        bit *= 2
        if bit < n:
            kept = kept + came.astype(jnp.float32)
    mine, send = partial_scores(me, kept, came, targets, partner_targets)
    total = mine + swap(send, 1, n)
    scale = lax.rsqrt(total[:, n : 2 * n] / PDIM + 1e-06)
    return (total[:, :n] * scale / PDIM).T


def solution(mesh):
    in_specs = (
        P(("groups", "shard"), None),
        P(("groups", "shard"), None),
        P(("groups", "shard")),
        P(None, "shard"),
        P("shard", None),
        P(("groups", "shard"), None),
    )
    out_specs = P("groups", "shard")
    return jax.shard_map(body, mesh=mesh, in_specs=in_specs, out_specs=out_specs, check_vma=False)
```

```python
import functools

import jax
import jax.numpy as jnp
from jax import lax
from jax.experimental import pallas as pl
from jax.experimental.pallas import tpu as pltpu
from jax.sharding import PartitionSpec as P

PDIM = 4096
LENGTH = 256
LANES = 256
NEAR = 4
MIB = 1 << 20
NT = (((1,), (1,)), ((), ()))
VMEM = pl.BlockSpec(memory_space=pltpu.VMEM)
SMEM = pl.BlockSpec(memory_space=pltpu.SMEM)
ANY = pl.BlockSpec(memory_space=pl.ANY)


def swap(value, bit, n):
    return lax.ppermute(value, "shard", [(s, s ^ bit) for s in range(n)])


def in_hbm(value):
    return pltpu.with_memory_space_constraint(value, pltpu.HBM)


def load_kernel(count, starts, *refs):
    sources, outs, sems = refs[:count], refs[-1 - count : -1], refs[-1]
    copies = [
        pltpu.make_async_copy(source.at[pl.ds(start, out.shape[0])], out, sems.at[i])
        for i, (source, start, out) in enumerate(zip(sources, starts, outs))
    ]
    for copy in copies:
        copy.start()
    for copy in copies:
        copy.wait()


def load(name, parts, after):
    size = sum(rows * array.size // array.shape[0] * array.dtype.itemsize for array, _, rows in parts)
    return pl.pallas_call(
        functools.partial(load_kernel, len(parts), [start for _, start, _ in parts]),
        out_shape=[pltpu.VMEM((rows,) + array.shape[1:], array.dtype) for array, _, rows in parts],
        in_specs=[ANY] * (len(parts) + len(after)),
        out_specs=[VMEM] * len(parts),
        scratch_shapes=[pltpu.SemaphoreType.DMA((len(parts),))],
        compiler_params=pltpu.CompilerParams(vmem_limit_bytes=MIB),
        cost_estimate=pl.CostEstimate(flops=0, bytes_accessed=2 * size, transcendentals=0),
        name=name,
    )(*[in_hbm(array) for array, _, _ in parts], *after)


def join_kernel(pick, *refs):
    out = refs[-1]
    for target, source in enumerate(pick):
        out[target] = refs[source[0]][source[1]] if len(source) == 2 else refs[source[0]][...]


def join(name, values, pick, shape, after):
    return pl.pallas_call(
        functools.partial(join_kernel, pick),
        out_shape=jax.ShapeDtypeStruct((len(pick),) + shape, values[0].dtype),
        in_specs=[VMEM] * len(values) + [ANY] * len(after),
        out_specs=VMEM,
        compiler_params=pltpu.CompilerParams(vmem_limit_bytes=2 * MIB),
        name=name,
    )(*values, *after)


def grads_kernel(far, me, *refs):
    singles, joined = refs[:NEAR], refs[NEAR : 2 * NEAR]
    tokens, cotangent, mask = refs[2 * NEAR : 2 * NEAR + 3]
    outs, grads = refs[-1 - far : -1], refs[-1]
    rank, depth = singles[0].shape
    total = jnp.zeros((rank, tokens.shape[0]), jnp.float32)
    for k in range(NEAR):
        for d in range(far):
            block = singles[k][...] if d == 0 else joined[k][d - 1]
            start = pl.multiple_of((me[0] ^ (d * NEAR + k)) * depth, depth)
            total += lax.dot_general(
                block, tokens[:, pl.ds(start, depth)], NT, preferred_element_type=jnp.float32
            )
    lowrank = total.astype(jnp.bfloat16) * mask[...].astype(jnp.bfloat16)
    turned = jnp.dot(lowrank, cotangent[...], preferred_element_type=jnp.float32)
    grads[...] = turned.T
    pack = LANES // rank
    share = outs[0].shape[1]
    for d in range(far):
        for i in range(NEAR):
            start = pl.multiple_of((me[0] ^ (d * NEAR + i)) * (share * pack), share * pack)
            for q in range(pack):
                rows = grads[pl.ds(start + q, share, stride=pack), :]
                outs[d][i, :, q * rank : (q + 1) * rank] = rows.astype(jnp.bfloat16)


def packed_grads(me, far, blocks, tokens, cotangent, mask, after):
    rank, width = blocks[0].shape[0], cotangent.shape[1]
    shape = (NEAR, width * rank // LANES // (far * NEAR), LANES)
    return pl.pallas_call(
        functools.partial(grads_kernel, far),
        out_shape=[jax.ShapeDtypeStruct(shape, jnp.bfloat16)] * far,
        in_specs=[SMEM] + [VMEM] * (len(blocks) + 3) + [ANY] * len(after),
        out_specs=[VMEM] * far,
        scratch_shapes=[pltpu.VMEM((width, rank), jnp.float32)],
        compiler_params=pltpu.CompilerParams(vmem_limit_bytes=6 * MIB),
        cost_estimate=pl.CostEstimate(flops=300000000, bytes_accessed=5000000, transcendentals=0),
        name="grads",
    )(me, *blocks, tokens, cotangent, mask, *after)


def features_kernel(far, me, *refs):
    own, across, other = refs[:far], refs[far], refs[far + 1]
    weights = refs[far + 2 : -4]
    keep, send, x, total = refs[-4:]
    n = far * NEAR
    share = other.shape[1]
    pitch = x.shape[1] // n
    for k in range(n):
        d, y, core = k // NEAR, k // 2 % 2, k % 2
        rows = other[2 * d + y] if core else across[2 * d] if y else own[d][0]
        start = pl.multiple_of((me[0] ^ k) * pitch, pitch)
        for h in range(x.shape[0]):
            x[h, pl.ds(start, share), :] = rows[:, h * 128 : (h + 1) * 128].astype(jnp.float32)
    j = 0
    for part in weights:
        for i in range(part.shape[0] // LANES):
            left = jnp.concatenate([x[h, pl.ds(j, n, stride=pitch), :] for h in range(x.shape[0])], axis=1)
            left = left.astype(jnp.bfloat16)
            term = jnp.dot(left, part[i * LANES : (i + 1) * LANES, :], preferred_element_type=jnp.float32)
            if j == 0:
                total[...] = term
            else:
                total[...] += term
            j += 1
    half = keep.shape[1]
    mine = pl.multiple_of((me[0] & 1) * half, half)
    partner = pl.multiple_of((1 - (me[0] & 1)) * half, half)
    keep[...] = total[:, pl.ds(mine, half)]
    send[...] = total[:, pl.ds(partner, half)].astype(jnp.bfloat16)


def partial_features(me, own, across, other, weights):
    far = len(own)
    n = far * NEAR
    share = other.shape[1]
    width = weights[0].shape[1]
    half = (n, width // 2)
    return pl.pallas_call(
        functools.partial(features_kernel, far),
        out_shape=[jax.ShapeDtypeStruct(half, jnp.float32), jax.ShapeDtypeStruct(half, jnp.bfloat16)],
        in_specs=[SMEM] + [VMEM] * (far + 2 + len(weights)),
        out_specs=[VMEM, VMEM],
        scratch_shapes=[
            pltpu.VMEM((LANES // 128, n * max(share, 8), 128), jnp.float32),
            pltpu.VMEM((n, width), jnp.float32),
        ],
        compiler_params=pltpu.CompilerParams(vmem_limit_bytes=6 * MIB),
        cost_estimate=pl.CostEstimate(flops=600000000, bytes_accessed=34000000, transcendentals=0),
        name="features",
    )(me, *own, across, other, *weights)


def scores_kernel(me, targets, partner_targets, kept, *refs):
    mine, send = refs[-2:]
    features = kept[...]
    for arrived in refs[:-2]:
        features += arrived[...].astype(jnp.float32)
    count, half = features.shape
    start = pl.multiple_of((me[0] & 1) * half, half)
    high = lax.Precision.HIGHEST
    ones = jnp.ones((targets.shape[0], half), jnp.float32)
    squares = lax.dot_general(ones, features * features, NT, precision=high, preferred_element_type=jnp.float32)
    rest = jnp.zeros((targets.shape[0], mine.shape[1] - 2 * count), jnp.float32)
    for source, out in ((targets, mine), (partner_targets, send)):
        scale = lax.rsqrt(jnp.sum(source[...] * source[...], axis=1, keepdims=True) / PDIM + 1e-06)
        dots = lax.dot_general(
            source[:, pl.ds(start, half)], features, NT, precision=high, preferred_element_type=jnp.float32
        )
        parts = [dots * scale, squares] + ([rest] if rest.shape[1] else [])
        out[...] = jnp.concatenate(parts, axis=1)


def partial_scores(me, targets, partner_targets, kept, arrived):
    shape = jax.ShapeDtypeStruct((targets.shape[0], 128), jnp.float32)
    return pl.pallas_call(
        scores_kernel,
        out_shape=[shape, shape],
        in_specs=[SMEM] + [VMEM] * (3 + len(arrived)),
        out_specs=[VMEM, VMEM],
        compiler_params=pltpu.CompilerParams(vmem_limit_bytes=6 * MIB),
        name="partial_scores",
    )(me, targets, partner_targets, kept, *arrived)


def body(tokens, cotangent, response_loss_mask, adapter_down_weight, projection, targets):
    n = lax.axis_size("shard")
    far = n // NEAR
    me = lax.axis_index("shard").astype(jnp.int32).reshape(1)
    chunks = projection.shape[0] // LANES
    cuts = [chunks * i // 8 * LANES for i in (0, 1, 4, 6, 8)]
    strips = [[(projection, lo, hi - lo)] if hi > lo else [] for lo, hi in zip(cuts, cuts[1:])]
    block = adapter_down_weight
    partner_targets = swap(targets, 1, n)

    whole = [(tokens, 0, tokens.shape[0]), (cotangent, 0, cotangent.shape[0])]
    whole += [(response_loss_mask.reshape(1, -1), 0, 1)]
    tokens, cotangent, mask, *weights = load("load_1", whole + strips[0], (me,))
    singles = [block, swap(block, 1, n), swap(block, 2, n)]
    column = [swap(block, NEAR * d, n) for d in range(1, far)]
    after = (mask, singles[1], singles[2], partner_targets)
    column = join("join_blocks", column, [(d,) for d in range(far - 1)], block.shape, after)
    weights += load("load_2", strips[1], (column,))
    joined = [column, swap(column, 1, n), swap(column, 2, n)]
    singles += [swap(singles[2], 1, n)]
    joined += [swap(joined[2], 1, n)]
    rows = packed_grads(me, far, singles + joined, tokens, cotangent, mask, (weights[-1],))

    weights += load("load_3", strips[2], (rows[0],))
    rows = [rows[0]] + [swap(rows[d], NEAR * d, n) for d in range(1, far)]
    pick = [(d, 2 + i) for d in range(far) for i in range(2)]
    across = join("join_y", rows, pick, rows[0].shape[1:], (weights[-1],))
    weights += load("load_4", strips[3], (across,))
    across = swap(across, 2, n)
    pick = [p for d in range(far) for p in ((d, 1), (far, 2 * d + 1))]
    other = swap(join("join_core", rows + [across], pick, rows[0].shape[1:], (weights[-1],)), 1, n)

    kept, send = partial_features(me, rows, across, other, weights)
    kept = kept + swap(send, 1, n).astype(jnp.float32)
    kept = kept + swap(kept.astype(jnp.bfloat16), 2, n).astype(jnp.float32)
    half = kept.astype(jnp.bfloat16)
    arrived = [swap(half, NEAR * d, n) for d in range(1, far)]
    mine, send = partial_scores(me, targets, partner_targets, kept, arrived)
    total = mine + swap(send, 1, n)
    scale = lax.rsqrt(total[:, n : 2 * n] / PDIM + 1e-06)
    return (total[:, :n] * scale / PDIM).T


def solution(mesh):
    in_specs = (
        P(("groups", "shard"), None),
        P(("groups", "shard"), None),
        P(("groups", "shard")),
        P(None, "shard"),
        P("shard", None),
        P(("groups", "shard"), None),
    )
    out_specs = P("groups", "shard")
    return jax.shard_map(body, mesh=mesh, in_specs=in_specs, out_specs=out_specs, check_vma=False)
```

```python
import functools

import jax
import jax.numpy as jnp
from jax import lax
from jax.experimental import pallas as pl
from jax.experimental.pallas import tpu as pltpu
from jax.sharding import PartitionSpec as P

PDIM = 4096
LENGTH = 256
LANES = 256
NEAR = 4
MIB = 1 << 20
NT = (((1,), (1,)), ((), ()))
VMEM = pl.BlockSpec(memory_space=pltpu.VMEM)
SMEM = pl.BlockSpec(memory_space=pltpu.SMEM)
ANY = pl.BlockSpec(memory_space=pl.ANY)


def swap(value, bit, n):
    return lax.ppermute(value, "shard", [(s, s ^ bit) for s in range(n)])


def in_hbm(value):
    return pltpu.with_memory_space_constraint(value, pltpu.HBM)


def load_kernel(count, starts, *refs):
    sources, outs, sems = refs[:count], refs[-1 - count : -1], refs[-1]
    copies = []
    for source, start, out in zip(sources, starts, outs):
        rows = out.shape[0]
        step = min(rows, LANES // 2)
        for i in range(0, rows, step):
            part = source.at[pl.ds(start + i, step)]
            copies.append(pltpu.make_async_copy(part, out.at[pl.ds(i, step)], sems.at[len(copies)]))
    for copy in copies:
        copy.start()
    for copy in copies:
        copy.wait()


def load(name, parts, after):
    size = sum(rows * array.size // array.shape[0] * array.dtype.itemsize for array, _, rows in parts)
    pieces = sum(max(rows // (LANES // 2), 1) for _, _, rows in parts)
    return pl.pallas_call(
        functools.partial(load_kernel, len(parts), [start for _, start, _ in parts]),
        out_shape=[pltpu.VMEM((rows,) + array.shape[1:], array.dtype) for array, _, rows in parts],
        in_specs=[ANY] * (len(parts) + len(after)),
        out_specs=[VMEM] * len(parts),
        scratch_shapes=[pltpu.SemaphoreType.DMA((pieces,))],
        compiler_params=pltpu.CompilerParams(vmem_limit_bytes=MIB),
        cost_estimate=pl.CostEstimate(flops=0, bytes_accessed=2 * size, transcendentals=0),
        name=name,
    )(*[in_hbm(array) for array, _, _ in parts], *after)


def hold(name, value, after):
    return pl.pallas_call(
        lambda *refs: None,
        out_shape=jax.ShapeDtypeStruct(value.shape, value.dtype),
        in_specs=[ANY] * (1 + len(after)),
        out_specs=ANY,
        input_output_aliases={0: 0},
        compiler_params=pltpu.CompilerParams(vmem_limit_bytes=MIB),
        name=name,
    )(value, *after)


def join_kernel(pick, *refs):
    out = refs[-1]
    for target, source in enumerate(pick):
        out[target] = refs[source[0]][source[1]] if len(source) == 2 else refs[source[0]][...]


def join(name, values, pick, shape, after):
    return pl.pallas_call(
        functools.partial(join_kernel, pick),
        out_shape=jax.ShapeDtypeStruct((len(pick),) + shape, values[0].dtype),
        in_specs=[VMEM] * len(values) + [ANY] * len(after),
        out_specs=VMEM,
        compiler_params=pltpu.CompilerParams(vmem_limit_bytes=2 * MIB),
        name=name,
    )(*values, *after)


def grads_kernel(far, me, *refs):
    singles, joined = refs[:NEAR], refs[NEAR : 2 * NEAR]
    tokens, cotangent, mask = refs[2 * NEAR : 2 * NEAR + 3]
    outs, grads = refs[-1 - far : -1], refs[-1]
    rank, depth = singles[0].shape
    total = jnp.zeros((rank, tokens.shape[0]), jnp.float32)
    for k in range(NEAR):
        for d in range(far):
            block = singles[k][...] if d == 0 else joined[k][d - 1]
            start = pl.multiple_of((me[0] ^ (d * NEAR + k)) * depth, depth)
            total += lax.dot_general(
                block, tokens[:, pl.ds(start, depth)], NT, preferred_element_type=jnp.float32
            )
    lowrank = total.astype(jnp.bfloat16) * mask[...].astype(jnp.bfloat16)
    turned = jnp.dot(lowrank, cotangent[...], preferred_element_type=jnp.float32)
    grads[...] = turned.T
    pack = LANES // rank
    share = outs[0].shape[1]
    for d in range(far):
        for i in range(NEAR):
            start = pl.multiple_of((me[0] ^ (d * NEAR + i)) * (share * pack), share * pack)
            for q in range(pack):
                rows = grads[pl.ds(start + q, share, stride=pack), :]
                outs[d][i, :, q * rank : (q + 1) * rank] = rows.astype(jnp.bfloat16)


def packed_grads(me, far, blocks, tokens, cotangent, mask, after):
    rank, width = blocks[0].shape[0], cotangent.shape[1]
    shape = (NEAR, width * rank // LANES // (far * NEAR), LANES)
    return pl.pallas_call(
        functools.partial(grads_kernel, far),
        out_shape=[jax.ShapeDtypeStruct(shape, jnp.bfloat16)] * far,
        in_specs=[SMEM] + [VMEM] * (len(blocks) + 3) + [ANY] * len(after),
        out_specs=[VMEM] * far,
        scratch_shapes=[pltpu.VMEM((width, rank), jnp.float32)],
        compiler_params=pltpu.CompilerParams(vmem_limit_bytes=6 * MIB),
        cost_estimate=pl.CostEstimate(flops=300000000, bytes_accessed=5000000, transcendentals=0),
        name="grads",
    )(me, *blocks, tokens, cotangent, mask, *after)


def features_kernel(far, start, me, *refs):
    own, across, other = refs[:far], refs[far], refs[far + 1]
    weights = refs[far + 2 : -9]
    weights_hbm, keep, rest, send, x, left, streamed, total, sems = refs[-9:]
    n = far * NEAR
    share = other.shape[1]
    pitch = x.shape[1] // n
    copies = [
        pltpu.make_async_copy(
            weights_hbm.at[pl.ds(start + i, LANES)], streamed.at[pl.ds(i, LANES)], sems.at[i // LANES]
        )
        for i in range(0, streamed.shape[0], LANES)
    ]
    for copy in copies:
        copy.start()
    for k in range(n):
        d, y, core = k // NEAR, k // 2 % 2, k % 2
        rows = other[2 * d + y] if core else across[2 * d] if y else own[d][0]
        place = pl.multiple_of((me[0] ^ k) * pitch, pitch)
        for h in range(x.shape[0]):
            x[h, pl.ds(place, share), :] = rows[:, h * 128 : (h + 1) * 128].astype(jnp.float32)
    for j in range(share):
        for h in range(x.shape[0]):
            at = j * LANES + h * 128
            left[:, at : at + 128] = x[h, pl.ds(j, n, stride=pitch), :].astype(jnp.bfloat16)
    row = 0
    for part in weights:
        term = jnp.dot(left[:, row : row + part.shape[0]], part[...], preferred_element_type=jnp.float32)
        total[...] = term if row == 0 else total[...] + term
        row += part.shape[0]
    for i, copy in enumerate(copies):
        copy.wait()
        part = streamed[i * LANES : (i + 1) * LANES, :]
        total[...] += jnp.dot(left[:, row : row + LANES], part, preferred_element_type=jnp.float32)
        row += LANES
    part = keep.shape[1]
    core, y = me[0] & 1, (me[0] >> 1) & 1
    for out, c, h, at in ((keep, core, y, None), (rest, core, 1 - y, None), (send, 1 - core, y, 0), (send, 1 - core, 1 - y, 1)):
        columns = total[:, pl.ds(pl.multiple_of((2 * c + h) * part, part), part)]
        if at is None:
            out[...] = columns
        else:
            out[at] = columns.astype(jnp.bfloat16)


def partial_features(me, own, across, other, weights, projection):
    far = len(own)
    n = far * NEAR
    share = other.shape[1]
    depth, width = projection.shape
    start = sum(part.shape[0] for part in weights)
    quarter = (n, width // NEAR)
    return pl.pallas_call(
        functools.partial(features_kernel, far, start),
        out_shape=[
            jax.ShapeDtypeStruct(quarter, jnp.float32),
            jax.ShapeDtypeStruct(quarter, jnp.float32),
            jax.ShapeDtypeStruct((2,) + quarter, jnp.bfloat16),
        ],
        in_specs=[SMEM] + [VMEM] * (far + 2 + len(weights)) + [ANY],
        out_specs=[VMEM, VMEM, VMEM],
        scratch_shapes=[
            pltpu.VMEM((LANES // 128, n * max(share, 8), 128), jnp.float32),
            pltpu.VMEM((n, depth), jnp.bfloat16),
            pltpu.VMEM((depth - start, width), projection.dtype),
            pltpu.VMEM((n, width), jnp.float32),
            pltpu.SemaphoreType.DMA(((depth - start) // LANES,)),
        ],
        compiler_params=pltpu.CompilerParams(vmem_limit_bytes=20 * MIB),
        cost_estimate=pl.CostEstimate(flops=600000000, bytes_accessed=34000000, transcendentals=0),
        name="features",
    )(me, *own, across, other, *weights, in_hbm(projection))


def scores_kernel(me, targets, *refs):
    quarters, out = refs[:-1], refs[-1]
    width = quarters[0].shape[1]
    high = lax.Precision.HIGHEST
    ones = jnp.ones((targets.shape[0], width), jnp.float32)
    dots = squares = 0.0
    for k, quarter in enumerate(quarters):
        features = quarter[...].astype(jnp.float32)
        near = me[0] ^ k
        place = pl.multiple_of((2 * (near & 1) + ((near >> 1) & 1)) * width, width)
        side = targets[:, pl.ds(place, width)]
        dots += lax.dot_general(side, features, NT, precision=high, preferred_element_type=jnp.float32)
        squares += lax.dot_general(
            ones, features * features, NT, precision=high, preferred_element_type=jnp.float32
        )
    scale_t = lax.rsqrt(jnp.sum(targets[...] * targets[...], axis=1, keepdims=True) / PDIM + 1e-06)
    out[...] = dots * lax.rsqrt(squares / PDIM + 1e-06) * scale_t / PDIM


def own_scores(me, targets, quarters):
    return pl.pallas_call(
        scores_kernel,
        out_shape=jax.ShapeDtypeStruct((targets.shape[0], quarters[0].shape[0]), jnp.float32),
        in_specs=[SMEM] + [VMEM] * (1 + len(quarters)),
        out_specs=VMEM,
        compiler_params=pltpu.CompilerParams(vmem_limit_bytes=6 * MIB),
        name="scores",
    )(me, targets, *quarters)


def body(tokens, cotangent, response_loss_mask, adapter_down_weight, projection, targets):
    n = lax.axis_size("shard")
    far = n // NEAR
    me = lax.axis_index("shard").astype(jnp.int32).reshape(1)
    chunks = projection.shape[0] // LANES
    cuts = [chunks * i // 16 * LANES for i in (0, 3, 10)]
    strips = [[(projection, lo, hi - lo)] if hi > lo else [] for lo, hi in zip(cuts, cuts[1:])]
    block = adapter_down_weight

    whole = [(tokens, 0, tokens.shape[0]), (cotangent, 0, cotangent.shape[0])]
    whole += [(response_loss_mask.reshape(1, -1), 0, 1)]
    tokens, cotangent, mask, *weights = load("load_1", whole + strips[0], (me,))
    column = [swap(block, NEAR * d, n) for d in range(1, far)]
    singles = [block, swap(block, 1, n), swap(block, 2, n)]
    after = (mask, singles[1], singles[2])
    column = join("join_blocks", column, [(d,) for d in range(far - 1)], block.shape, after)
    weights += load("load_2", strips[1], (column,))
    joined = [column, swap(column, 1, n), hold("hold", swap(column, 2, n), (weights[-1],))]
    singles += [swap(singles[2], 1, n)]
    joined += [swap(joined[2], 1, n)]
    rows = packed_grads(me, far, singles + joined, tokens, cotangent, mask, ())

    rows = [rows[0]] + [swap(rows[d], NEAR * d, n) for d in range(1, far)]
    pick = [(d, 2 + i) for d in range(far) for i in range(2)]
    across = swap(join("join_y", rows, pick, rows[0].shape[1:], ()), 2, n)
    pick = [p for d in range(far) for p in ((d, 1), (far, 2 * d + 1))]
    other = swap(join("join_core", rows + [across], pick, rows[0].shape[1:], ()), 1, n)

    keep, rest, send = partial_features(me, rows, across, other, weights, projection)
    came = swap(send, 1, n).astype(jnp.float32)
    keep = keep + came[0] + swap((rest + came[1]).astype(jnp.bfloat16), 2, n).astype(jnp.float32)
    half = keep.astype(jnp.bfloat16)
    for d in range(1, far):
        keep = keep + swap(half, NEAR * d, n).astype(jnp.float32)
    half = keep.astype(jnp.bfloat16)
    return own_scores(me, targets, [keep] + [swap(half, k, n) for k in range(1, NEAR)]).T


def solution(mesh):
    in_specs = (
        P(("groups", "shard"), None),
        P(("groups", "shard"), None),
        P(("groups", "shard")),
        P(None, "shard"),
        P("shard", None),
        P(("groups", "shard"), None),
    )
    out_specs = P("groups", "shard")
    return jax.shard_map(body, mesh=mesh, in_specs=in_specs, out_specs=out_specs, check_vma=False)
```

```python
import functools

import jax
import jax.numpy as jnp
from jax import lax
from jax.experimental import pallas as pl
from jax.experimental.pallas import tpu as pltpu
from jax.sharding import PartitionSpec as P

PDIM = 4096
LENGTH = 256
LANES = 256
NEAR = 4
MIB = 1 << 20
NT = (((1,), (1,)), ((), ()))
VMEM = pl.BlockSpec(memory_space=pltpu.VMEM)
SMEM = pl.BlockSpec(memory_space=pltpu.SMEM)
ANY = pl.BlockSpec(memory_space=pl.ANY)


def swap(value, bit, n):
    return lax.ppermute(value, "shard", [(s, s ^ bit) for s in range(n)])


def in_hbm(value):
    return pltpu.with_memory_space_constraint(value, pltpu.HBM)


def load_kernel(count, starts, *refs):
    sources, outs, sems = refs[:count], refs[-1 - count : -1], refs[-1]
    copies = []
    for source, start, out in zip(sources, starts, outs):
        rows = out.shape[0]
        step = min(rows, LANES // 2)
        for i in range(0, rows, step):
            part = source.at[pl.ds(start + i, step)]
            copies.append(pltpu.make_async_copy(part, out.at[pl.ds(i, step)], sems.at[len(copies)]))
    for copy in copies:
        copy.start()
    for copy in copies:
        copy.wait()


def load(name, parts, after):
    size = sum(rows * array.size // array.shape[0] * array.dtype.itemsize for array, _, rows in parts)
    pieces = sum(max(rows // (LANES // 2), 1) for _, _, rows in parts)
    return pl.pallas_call(
        functools.partial(load_kernel, len(parts), [start for _, start, _ in parts]),
        out_shape=[pltpu.VMEM((rows,) + array.shape[1:], array.dtype) for array, _, rows in parts],
        in_specs=[ANY] * (len(parts) + len(after)),
        out_specs=[VMEM] * len(parts),
        scratch_shapes=[pltpu.SemaphoreType.DMA((pieces,))],
        compiler_params=pltpu.CompilerParams(vmem_limit_bytes=MIB),
        cost_estimate=pl.CostEstimate(flops=0, bytes_accessed=2 * size, transcendentals=0),
        name=name,
    )(*[in_hbm(array) for array, _, _ in parts], *after)


def hold(name, value, after):
    return pl.pallas_call(
        lambda *refs: None,
        out_shape=jax.ShapeDtypeStruct(value.shape, value.dtype),
        in_specs=[ANY] * (1 + len(after)),
        out_specs=ANY,
        input_output_aliases={0: 0},
        compiler_params=pltpu.CompilerParams(vmem_limit_bytes=MIB),
        name=name,
    )(value, *after)


def join_kernel(pick, *refs):
    out = refs[-1]
    for target, source in enumerate(pick):
        out[target] = refs[source[0]][source[1]] if len(source) == 2 else refs[source[0]][...]


def join(name, values, pick, shape, after):
    return pl.pallas_call(
        functools.partial(join_kernel, pick),
        out_shape=jax.ShapeDtypeStruct((len(pick),) + shape, values[0].dtype),
        in_specs=[VMEM] * len(values) + [ANY] * len(after),
        out_specs=VMEM,
        compiler_params=pltpu.CompilerParams(vmem_limit_bytes=2 * MIB),
        name=name,
    )(*values, *after)


def grads_kernel(far, me, *refs):
    singles, joined = refs[:NEAR], refs[NEAR : 2 * NEAR]
    tokens, cotangent, mask = refs[2 * NEAR : 2 * NEAR + 3]
    outs, grads = refs[-1 - far : -1], refs[-1]
    rank, depth = singles[0].shape
    total = jnp.zeros((rank, tokens.shape[0]), jnp.float32)
    for k in range(NEAR):
        for d in range(far):
            block = singles[k][...] if d == 0 else joined[k][d - 1]
            start = pl.multiple_of((me[0] ^ (d * NEAR + k)) * depth, depth)
            total += lax.dot_general(
                block, tokens[:, pl.ds(start, depth)], NT, preferred_element_type=jnp.float32
            )
    lowrank = total.astype(jnp.bfloat16) * mask[...].astype(jnp.bfloat16)
    turned = jnp.dot(lowrank, cotangent[...], preferred_element_type=jnp.float32)
    grads[...] = turned.T
    pack = LANES // rank
    share = outs[0].shape[1]
    for d in range(far):
        for i in range(NEAR):
            start = pl.multiple_of((me[0] ^ (d * NEAR + i)) * (share * pack), share * pack)
            for q in range(pack):
                rows = grads[pl.ds(start + q, share, stride=pack), :]
                outs[d][i, :, q * rank : (q + 1) * rank] = rows.astype(jnp.bfloat16)


def packed_grads(me, far, blocks, tokens, cotangent, mask, after):
    rank, width = blocks[0].shape[0], cotangent.shape[1]
    shape = (NEAR, width * rank // LANES // (far * NEAR), LANES)
    return pl.pallas_call(
        functools.partial(grads_kernel, far),
        out_shape=[jax.ShapeDtypeStruct(shape, jnp.bfloat16)] * far,
        in_specs=[SMEM] + [VMEM] * (len(blocks) + 3) + [ANY] * len(after),
        out_specs=[VMEM] * far,
        scratch_shapes=[pltpu.VMEM((width, rank), jnp.float32)],
        compiler_params=pltpu.CompilerParams(vmem_limit_bytes=6 * MIB),
        cost_estimate=pl.CostEstimate(flops=300000000, bytes_accessed=5000000, transcendentals=0),
        name="grads",
    )(me, *blocks, tokens, cotangent, mask, *after)


def features_kernel(far, start, me, *refs):
    own, across, other = refs[:far], refs[far], refs[far + 1]
    weights = refs[far + 2 : -8]
    weights_hbm, keep, send, x, left, streamed, total, sems = refs[-8:]
    n = far * NEAR
    share = other.shape[1]
    pitch = x.shape[1] // n
    copies = [
        pltpu.make_async_copy(
            weights_hbm.at[pl.ds(start + i, LANES)], streamed.at[pl.ds(i, LANES)], sems.at[i // LANES]
        )
        for i in range(0, streamed.shape[0], LANES)
    ]
    for copy in copies:
        copy.start()
    for k in range(n):
        d, y, core = k // NEAR, k // 2 % 2, k % 2
        rows = other[2 * d + y] if core else across[2 * d] if y else own[d][0]
        place = pl.multiple_of((me[0] ^ k) * pitch, pitch)
        for h in range(x.shape[0]):
            x[h, pl.ds(place, share), :] = rows[:, h * 128 : (h + 1) * 128].astype(jnp.float32)
    for j in range(share):
        for h in range(x.shape[0]):
            at = j * LANES + h * 128
            left[:, at : at + 128] = x[h, pl.ds(j, n, stride=pitch), :].astype(jnp.bfloat16)
    row = 0
    for part in weights:
        term = jnp.dot(left[:, row : row + part.shape[0]], part[...], preferred_element_type=jnp.float32)
        total[...] = term if row == 0 else total[...] + term
        row += part.shape[0]
    for i, copy in enumerate(copies):
        copy.wait()
        part = streamed[i * LANES : (i + 1) * LANES, :]
        total[...] += jnp.dot(left[:, row : row + LANES], part, preferred_element_type=jnp.float32)
        row += LANES
    part = keep.shape[1]
    mine = pl.multiple_of((me[0] & 1) * part, part)
    partner = pl.multiple_of((1 - (me[0] & 1)) * part, part)
    keep[...] = total[:, pl.ds(mine, part)]
    send[...] = total[:, pl.ds(partner, part)].astype(jnp.bfloat16)


def partial_features(me, own, across, other, weights, projection):
    far = len(own)
    n = far * NEAR
    share = other.shape[1]
    depth, width = projection.shape
    start = sum(part.shape[0] for part in weights)
    half = (n, width // 2)
    return pl.pallas_call(
        functools.partial(features_kernel, far, start),
        out_shape=[jax.ShapeDtypeStruct(half, jnp.float32), jax.ShapeDtypeStruct(half, jnp.bfloat16)],
        in_specs=[SMEM] + [VMEM] * (far + 2 + len(weights)) + [ANY],
        out_specs=[VMEM, VMEM],
        scratch_shapes=[
            pltpu.VMEM((LANES // 128, n * max(share, 8), 128), jnp.float32),
            pltpu.VMEM((n, depth), jnp.bfloat16),
            pltpu.VMEM((depth - start, width), projection.dtype),
            pltpu.VMEM((n, width), jnp.float32),
            pltpu.SemaphoreType.DMA(((depth - start) // LANES,)),
        ],
        compiler_params=pltpu.CompilerParams(vmem_limit_bytes=20 * MIB),
        cost_estimate=pl.CostEstimate(flops=600000000, bytes_accessed=34000000, transcendentals=0),
        name="features",
    )(me, *own, across, other, *weights, in_hbm(projection))


def scores_kernel(me, targets, partner_targets, kept, *refs):
    mine, send = refs[-2:]
    features = kept[...]
    for arrived in refs[:-2]:
        features += arrived[...].astype(jnp.float32)
    count, half = features.shape
    start = pl.multiple_of((me[0] & 1) * half, half)
    high = lax.Precision.HIGHEST
    ones = jnp.ones((targets.shape[0], half), jnp.float32)
    squares = lax.dot_general(ones, features * features, NT, precision=high, preferred_element_type=jnp.float32)
    rest = jnp.zeros((targets.shape[0], mine.shape[1] - 2 * count), jnp.float32)
    for source, out in ((targets, mine), (partner_targets, send)):
        scale = lax.rsqrt(jnp.sum(source[...] * source[...], axis=1, keepdims=True) / PDIM + 1e-06)
        dots = lax.dot_general(
            source[:, pl.ds(start, half)], features, NT, precision=high, preferred_element_type=jnp.float32
        )
        parts = [dots * scale, squares] + ([rest] if rest.shape[1] else [])
        out[...] = jnp.concatenate(parts, axis=1)


def partial_scores(me, targets, partner_targets, kept, arrived):
    shape = jax.ShapeDtypeStruct((targets.shape[0], 128), jnp.float32)
    return pl.pallas_call(
        scores_kernel,
        out_shape=[shape, shape],
        in_specs=[SMEM] + [VMEM] * (3 + len(arrived)),
        out_specs=[VMEM, VMEM],
        compiler_params=pltpu.CompilerParams(vmem_limit_bytes=6 * MIB),
        name="partial_scores",
    )(me, targets, partner_targets, kept, *arrived)


def body(tokens, cotangent, response_loss_mask, adapter_down_weight, projection, targets):
    n = lax.axis_size("shard")
    far = n // NEAR
    me = lax.axis_index("shard").astype(jnp.int32).reshape(1)
    chunks = projection.shape[0] // LANES
    cuts = [chunks * i // 16 * LANES for i in (0, 4, 8, 11)]
    strips = [[(projection, lo, hi - lo)] if hi > lo else [] for lo, hi in zip(cuts, cuts[1:])]
    block = adapter_down_weight

    whole = [(tokens, 0, tokens.shape[0]), (cotangent, 0, cotangent.shape[0])]
    whole += [(response_loss_mask.reshape(1, -1), 0, 1)]
    tokens, cotangent, mask = load("load_1", whole, (me,))
    column = [swap(block, NEAR * d, n) for d in range(1, far)]
    singles = [block, swap(block, 1, n), swap(block, 2, n)]
    after = (mask, singles[1], singles[2])
    column = join("join_blocks", column, [(d,) for d in range(far - 1)], block.shape, after)
    weights = list(load("load_2", strips[0], (column,)))
    joined = [column, swap(column, 1, n), hold("hold", swap(column, 2, n), (weights[-1],))]
    singles += [swap(singles[2], 1, n)]
    joined += [swap(joined[2], 1, n)]
    rows = packed_grads(me, far, singles + joined, tokens, cotangent, mask, ())

    targets, *part = load("load_3", [(targets, 0, targets.shape[0])] + strips[1], (rows[0],))
    weights += part
    rows = [rows[0]] + [swap(rows[d], NEAR * d, n) for d in range(1, far)]
    pick = [(d, 2 + i) for d in range(far) for i in range(2)]
    across = join("join_y", rows, pick, rows[0].shape[1:], (targets,))
    partner_targets = swap(targets, 1, n)
    weights += load("load_4", strips[2], (across,)) if strips[2] else []
    across = swap(across, 2, n)
    pick = [p for d in range(far) for p in ((d, 1), (far, 2 * d + 1))]
    other = swap(join("join_core", rows + [across], pick, rows[0].shape[1:], (weights[-1],)), 1, n)

    kept, send = partial_features(me, rows, across, other, weights, projection)
    kept = kept + swap(send, 1, n).astype(jnp.float32)
    kept = kept + swap(kept.astype(jnp.bfloat16), 2, n).astype(jnp.float32)
    half = kept.astype(jnp.bfloat16)
    arrived = [swap(half, NEAR * d, n) for d in range(1, far)]
    mine, send = partial_scores(me, targets, partner_targets, kept, arrived)
    total = mine + swap(send, 1, n)
    scale = lax.rsqrt(total[:, n : 2 * n] / PDIM + 1e-06)
    return (total[:, :n] * scale / PDIM).T


def solution(mesh):
    in_specs = (
        P(("groups", "shard"), None),
        P(("groups", "shard"), None),
        P(("groups", "shard")),
        P(None, "shard"),
        P("shard", None),
        P(("groups", "shard"), None),
    )
    out_specs = P("groups", "shard")
    return jax.shard_map(body, mesh=mesh, in_specs=in_specs, out_specs=out_specs, check_vma=False)
```

```python
import functools

import jax
import jax.numpy as jnp
from jax import lax
from jax.experimental import pallas as pl
from jax.experimental.pallas import tpu as pltpu
from jax.sharding import PartitionSpec as P

PDIM = 4096
LENGTH = 256
LANES = 256
NEAR = 4
MIB = 1 << 20
NT = (((1,), (1,)), ((), ()))
VMEM = pl.BlockSpec(memory_space=pltpu.VMEM)
SMEM = pl.BlockSpec(memory_space=pltpu.SMEM)
ANY = pl.BlockSpec(memory_space=pl.ANY)


def swap(value, bit, n):
    return lax.ppermute(value, "shard", [(s, s ^ bit) for s in range(n)])


def in_hbm(value):
    return pltpu.with_memory_space_constraint(value, pltpu.HBM)


def load_kernel(count, starts, *refs):
    sources, outs, sems = refs[:count], refs[-1 - count : -1], refs[-1]
    copies = []
    for source, start, out in zip(sources, starts, outs):
        rows = out.shape[0]
        step = min(rows, LANES // 2)
        for i in range(0, rows, step):
            part = source.at[pl.ds(start + i, step)]
            copies.append(pltpu.make_async_copy(part, out.at[pl.ds(i, step)], sems.at[len(copies)]))
    for copy in copies:
        copy.start()
    for copy in copies:
        copy.wait()


def load(name, parts, after):
    size = sum(rows * array.size // array.shape[0] * array.dtype.itemsize for array, _, rows in parts)
    pieces = sum(max(rows // (LANES // 2), 1) for _, _, rows in parts)
    return pl.pallas_call(
        functools.partial(load_kernel, len(parts), [start for _, start, _ in parts]),
        out_shape=[pltpu.VMEM((rows,) + array.shape[1:], array.dtype) for array, _, rows in parts],
        in_specs=[ANY] * (len(parts) + len(after)),
        out_specs=[VMEM] * len(parts),
        scratch_shapes=[pltpu.SemaphoreType.DMA((pieces,))],
        compiler_params=pltpu.CompilerParams(vmem_limit_bytes=MIB),
        cost_estimate=pl.CostEstimate(flops=0, bytes_accessed=2 * size, transcendentals=0),
        name=name,
    )(*[in_hbm(array) for array, _, _ in parts], *after)


def hold(name, value, after):
    return pl.pallas_call(
        lambda *refs: None,
        out_shape=jax.ShapeDtypeStruct(value.shape, value.dtype),
        in_specs=[ANY] * (1 + len(after)),
        out_specs=ANY,
        input_output_aliases={0: 0},
        compiler_params=pltpu.CompilerParams(vmem_limit_bytes=MIB),
        name=name,
    )(value, *after)


def join_kernel(picks, *refs):
    for pick, out in zip(picks, refs[-len(picks) :]):
        for target, (source, *entry) in enumerate(pick):
            out[target] = refs[source][entry[0]] if entry else refs[source][...]


def join(name, values, picks, shape, after=()):
    return pl.pallas_call(
        functools.partial(join_kernel, picks),
        out_shape=[jax.ShapeDtypeStruct((len(pick),) + shape, values[0].dtype) for pick in picks],
        in_specs=[VMEM] * len(values) + [ANY] * len(after),
        out_specs=[VMEM] * len(picks),
        compiler_params=pltpu.CompilerParams(vmem_limit_bytes=2 * MIB),
        name=name,
    )(*values, *after)


def grads_kernel(far, me, *refs):
    blocks = refs[:NEAR]
    tokens, cotangent, mask = refs[NEAR : NEAR + 3]
    outs, grads = refs[-1 - far : -1], refs[-1]
    _, rank, depth = blocks[0].shape
    total = jnp.zeros((rank, tokens.shape[0]), jnp.float32)
    for k in range(NEAR):
        for d in range(far):
            start = pl.multiple_of((me[0] ^ (d * NEAR + k)) * depth, depth)
            total += lax.dot_general(
                blocks[k][d], tokens[:, pl.ds(start, depth)], NT, preferred_element_type=jnp.float32
            )
    lowrank = total.astype(jnp.bfloat16) * mask[...].astype(jnp.bfloat16)
    turned = jnp.dot(lowrank, cotangent[...], preferred_element_type=jnp.float32)
    grads[...] = turned.T
    pack = LANES // rank
    share = outs[0].shape[1]
    for d in range(far):
        for i in range(NEAR):
            start = pl.multiple_of((me[0] ^ (d * NEAR + i)) * (share * pack), share * pack)
            for q in range(pack):
                rows = grads[pl.ds(start + q, share, stride=pack), :]
                outs[d][i, :, q * rank : (q + 1) * rank] = rows.astype(jnp.bfloat16)


def packed_grads(me, blocks, tokens, cotangent, mask):
    (far, rank, _), width = blocks[0].shape, cotangent.shape[1]
    shape = (NEAR, width * rank // LANES // (far * NEAR), LANES)
    return pl.pallas_call(
        functools.partial(grads_kernel, far),
        out_shape=[jax.ShapeDtypeStruct(shape, jnp.bfloat16)] * far,
        in_specs=[SMEM] + [VMEM] * (len(blocks) + 3),
        out_specs=[VMEM] * far,
        scratch_shapes=[pltpu.VMEM((width, rank), jnp.float32)],
        compiler_params=pltpu.CompilerParams(vmem_limit_bytes=6 * MIB),
        cost_estimate=pl.CostEstimate(flops=300000000, bytes_accessed=5000000, transcendentals=0),
        name="grads",
    )(me, *blocks, tokens, cotangent, mask)


def features_kernel(far, start, me, *refs):
    own, came = refs[:far], refs[far : far + NEAR - 1]
    weights = refs[far + NEAR - 1 : -8]
    weights_hbm, keep, send, x, left, streamed, total, sems = refs[-8:]
    n = far * NEAR
    share = own[0].shape[1]
    pitch = x.shape[1] // n
    copies = [
        pltpu.make_async_copy(
            weights_hbm.at[pl.ds(start + i, LANES)], streamed.at[pl.ds(i, LANES)], sems.at[i // LANES]
        )
        for i in range(0, streamed.shape[0], LANES)
    ]
    for copy in copies:
        copy.start()
    for k in range(n):
        d, near = k // NEAR, k % NEAR
        rows = came[near - 1][d] if near else own[d][0]
        place = pl.multiple_of((me[0] ^ k) * pitch, pitch)
        for h in range(x.shape[0]):
            x[h, pl.ds(place, share), :] = rows[:, h * 128 : (h + 1) * 128].astype(jnp.float32)
    for j in range(share):
        for h in range(x.shape[0]):
            at = j * LANES + h * 128
            left[:, at : at + 128] = x[h, pl.ds(j, n, stride=pitch), :].astype(jnp.bfloat16)
    row = 0
    for part in weights:
        term = jnp.dot(left[:, row : row + part.shape[0]], part[...], preferred_element_type=jnp.float32)
        total[...] = term if row == 0 else total[...] + term
        row += part.shape[0]
    for i, copy in enumerate(copies):
        copy.wait()
        part = streamed[i * LANES : (i + 1) * LANES, :]
        total[...] += jnp.dot(left[:, row : row + LANES], part, preferred_element_type=jnp.float32)
        row += LANES
    part = keep.shape[1]
    mine = pl.multiple_of((me[0] & 1) * part, part)
    partner = pl.multiple_of((1 - (me[0] & 1)) * part, part)
    keep[...] = total[:, pl.ds(mine, part)]
    send[...] = total[:, pl.ds(partner, part)].astype(jnp.bfloat16)


def partial_features(me, own, came, weights, projection):
    far = len(own)
    n = far * NEAR
    share = own[0].shape[1]
    depth, width = projection.shape
    start = sum(part.shape[0] for part in weights)
    half = (n, width // 2)
    return pl.pallas_call(
        functools.partial(features_kernel, far, start),
        out_shape=[jax.ShapeDtypeStruct(half, jnp.float32), jax.ShapeDtypeStruct(half, jnp.bfloat16)],
        in_specs=[SMEM] + [VMEM] * (far + len(came) + len(weights)) + [ANY],
        out_specs=[VMEM, VMEM],
        scratch_shapes=[
            pltpu.VMEM((LANES // 128, n * max(share, 8), 128), jnp.float32),
            pltpu.VMEM((n, depth), jnp.bfloat16),
            pltpu.VMEM((depth - start, width), projection.dtype),
            pltpu.VMEM((n, width), jnp.float32),
            pltpu.SemaphoreType.DMA(((depth - start) // LANES,)),
        ],
        compiler_params=pltpu.CompilerParams(vmem_limit_bytes=20 * MIB),
        cost_estimate=pl.CostEstimate(flops=600000000, bytes_accessed=34000000, transcendentals=0),
        name="features",
    )(me, *own, *came, *weights, in_hbm(projection))


def scores_kernel(me, targets, partner_targets, kept, *refs):
    mine, send = refs[-2:]
    features = kept[...]
    for arrived in refs[:-2]:
        features += arrived[...].astype(jnp.float32)
    count, half = features.shape
    start = pl.multiple_of((me[0] & 1) * half, half)
    high = lax.Precision.HIGHEST
    ones = jnp.ones((targets.shape[0], half), jnp.float32)
    squares = lax.dot_general(ones, features * features, NT, precision=high, preferred_element_type=jnp.float32)
    rest = jnp.zeros((targets.shape[0], mine.shape[1] - 2 * count), jnp.float32)
    for source, out in ((targets, mine), (partner_targets, send)):
        scale = lax.rsqrt(jnp.sum(source[...] * source[...], axis=1, keepdims=True) / PDIM + 1e-06)
        dots = lax.dot_general(
            source[:, pl.ds(start, half)], features, NT, precision=high, preferred_element_type=jnp.float32
        )
        parts = [dots * scale, squares] + ([rest] if rest.shape[1] else [])
        out[...] = jnp.concatenate(parts, axis=1)


def partial_scores(me, targets, partner_targets, kept, arrived):
    shape = jax.ShapeDtypeStruct((targets.shape[0], 128), jnp.float32)
    return pl.pallas_call(
        scores_kernel,
        out_shape=[shape, shape],
        in_specs=[SMEM] + [VMEM] * (3 + len(arrived)),
        out_specs=[VMEM, VMEM],
        compiler_params=pltpu.CompilerParams(vmem_limit_bytes=6 * MIB),
        name="partial_scores",
    )(me, targets, partner_targets, kept, *arrived)


def body(tokens, cotangent, response_loss_mask, adapter_down_weight, projection, targets):
    n = lax.axis_size("shard")
    far = n // NEAR
    me = lax.axis_index("shard").astype(jnp.int32).reshape(1)
    chunks = projection.shape[0] // LANES
    cuts = [chunks * i // 16 * LANES for i in (0, 3, 10, 13)]
    strips = [[(projection, lo, hi - lo)] if hi > lo else [] for lo, hi in zip(cuts, cuts[1:])]
    block = adapter_down_weight

    whole = [(tokens, 0, tokens.shape[0]), (cotangent, 0, cotangent.shape[0])]
    whole += [(response_loss_mask.reshape(1, -1), 0, 1)]
    tokens, cotangent, mask, *weights = load("load_1", whole + strips[0], (me,))
    column = [block] + [swap(block, NEAR * d, n) for d in range(1, far)]
    (column,) = join("join_blocks", column, [[(d,) for d in range(far)]], block.shape, (mask,))
    weights += load("load_2", strips[1], (column,))
    across = hold("hold", swap(column, 2, n), (weights[-1],))
    blocks = [column, swap(column, 1, n), across, swap(across, 1, n)]
    rows = packed_grads(me, blocks, tokens, cotangent, mask)

    targets, *part = load("load_3", [(targets, 0, targets.shape[0])] + strips[2], (rows[0],))
    weights += part
    rows = [rows[0]] + [swap(rows[d], NEAR * d, n) for d in range(1, far)]
    picks = [[(d, k) for d in range(far)] for k in range(1, NEAR)]
    came = join("join_rows", rows, picks, rows[0].shape[1:], (targets,))
    came = [swap(came[k - 1], k, n) for k in range(1, NEAR)]
    partner_targets = swap(targets, 1, n)

    kept, send = partial_features(me, rows, came, weights, projection)
    kept = kept + swap(send, 1, n).astype(jnp.float32)
    kept = kept + swap(kept.astype(jnp.bfloat16), 2, n).astype(jnp.float32)
    half = kept.astype(jnp.bfloat16)
    arrived = [swap(half, NEAR * d, n) for d in range(1, far)]
    mine, send = partial_scores(me, targets, partner_targets, kept, arrived)
    total = mine + swap(send, 1, n)
    scale = lax.rsqrt(total[:, n : 2 * n] / PDIM + 1e-06)
    return (total[:, :n] * scale / PDIM).T


def solution(mesh):
    in_specs = (
        P(("groups", "shard"), None),
        P(("groups", "shard"), None),
        P(("groups", "shard")),
        P(None, "shard"),
        P("shard", None),
        P(("groups", "shard"), None),
    )
    out_specs = P("groups", "shard")
    return jax.shard_map(body, mesh=mesh, in_specs=in_specs, out_specs=out_specs, check_vma=False)
```

```python
import functools

import jax
import jax.numpy as jnp
from jax import lax
from jax.experimental import pallas as pl
from jax.experimental.pallas import tpu as pltpu
from jax.sharding import PartitionSpec as P

PDIM = 4096
LENGTH = 256
LANES = 256
NEAR = 4
MIB = 1 << 20
NT = (((1,), (1,)), ((), ()))
VMEM = pl.BlockSpec(memory_space=pltpu.VMEM)
SMEM = pl.BlockSpec(memory_space=pltpu.SMEM)
ANY = pl.BlockSpec(memory_space=pl.ANY)


def swap(value, bit, n):
    return lax.ppermute(value, "shard", [(s, s ^ bit) for s in range(n)])


def in_hbm(value):
    return pltpu.with_memory_space_constraint(value, pltpu.HBM)


def load_kernel(count, starts, *refs):
    sources, outs, sems = refs[:count], refs[-1 - count : -1], refs[-1]
    copies = []
    for source, start, out in zip(sources, starts, outs):
        rows = out.shape[0]
        step = min(rows, LANES // 2)
        for i in range(0, rows, step):
            part = source.at[pl.ds(start + i, step)]
            copies.append(pltpu.make_async_copy(part, out.at[pl.ds(i, step)], sems.at[len(copies)]))
    for copy in copies:
        copy.start()
    for copy in copies:
        copy.wait()


def load(name, parts, after):
    size = sum(rows * array.size // array.shape[0] * array.dtype.itemsize for array, _, rows in parts)
    pieces = sum(max(rows // (LANES // 2), 1) for _, _, rows in parts)
    return pl.pallas_call(
        functools.partial(load_kernel, len(parts), [start for _, start, _ in parts]),
        out_shape=[pltpu.VMEM((rows,) + array.shape[1:], array.dtype) for array, _, rows in parts],
        in_specs=[ANY] * (len(parts) + len(after)),
        out_specs=[VMEM] * len(parts),
        scratch_shapes=[pltpu.SemaphoreType.DMA((pieces,))],
        compiler_params=pltpu.CompilerParams(vmem_limit_bytes=MIB),
        cost_estimate=pl.CostEstimate(flops=0, bytes_accessed=2 * size, transcendentals=0),
        name=name,
    )(*[in_hbm(array) for array, _, _ in parts], *after)


def hold(name, value, after):
    return pl.pallas_call(
        lambda *refs: None,
        out_shape=jax.ShapeDtypeStruct(value.shape, value.dtype),
        in_specs=[ANY] * (1 + len(after)),
        out_specs=ANY,
        input_output_aliases={0: 0},
        compiler_params=pltpu.CompilerParams(vmem_limit_bytes=MIB),
        name=name,
    )(value, *after)


def join_kernel(picks, *refs):
    for pick, out in zip(picks, refs[-len(picks) :]):
        for target, (source, *entry) in enumerate(pick):
            out[target] = refs[source][entry[0]] if entry else refs[source][...]


def join(name, values, picks, shape, after=()):
    return pl.pallas_call(
        functools.partial(join_kernel, picks),
        out_shape=[jax.ShapeDtypeStruct((len(pick),) + shape, values[0].dtype) for pick in picks],
        in_specs=[VMEM] * len(values) + [ANY] * len(after),
        out_specs=[VMEM] * len(picks),
        compiler_params=pltpu.CompilerParams(vmem_limit_bytes=2 * MIB),
        name=name,
    )(*values, *after)


def add_lowrank(total, me, blocks, places, tokens):
    for block, owners in zip(blocks, places):
        depth = block.shape[-1]
        for i, k in enumerate(owners):
            start = pl.multiple_of((me[0] ^ k) * depth, depth)
            part = block[i] if len(block.shape) == 3 else block[...]
            total += lax.dot_general(part, tokens[:, pl.ds(start, depth)], NT, preferred_element_type=jnp.float32)
    return total


def lowrank_kernel(places, me, tokens, *refs):
    blocks, out = refs[: len(places)], refs[-1]
    before = refs[len(places)][...] if len(refs) > len(places) + 1 else jnp.zeros(out.shape, jnp.float32)
    out[...] = add_lowrank(before, me, blocks, places, tokens)


def partial_lowrank(name, me, tokens, blocks, places, before=()):
    return pl.pallas_call(
        functools.partial(lowrank_kernel, places),
        out_shape=jax.ShapeDtypeStruct((blocks[0].shape[-2], tokens.shape[0]), jnp.float32),
        in_specs=[SMEM] + [VMEM] * (1 + len(blocks) + len(before)),
        out_specs=VMEM,
        compiler_params=pltpu.CompilerParams(vmem_limit_bytes=2 * MIB),
        cost_estimate=pl.CostEstimate(flops=200000000, bytes_accessed=2000000, transcendentals=0),
        name=name,
    )(me, tokens, *blocks, *before)


def grads_kernel(far, places, me, tokens, *refs):
    blocks = refs[: len(places)]
    before, cotangent, mask = refs[len(places) : len(places) + 3]
    outs, grads = refs[-1 - far : -1], refs[-1]
    total = add_lowrank(before[...], me, blocks, places, tokens)
    rank = total.shape[0]
    lowrank = total.astype(jnp.bfloat16) * mask[...].astype(jnp.bfloat16)
    turned = jnp.dot(lowrank, cotangent[...], preferred_element_type=jnp.float32)
    grads[...] = turned.T
    pack = LANES // rank
    share = outs[0].shape[1]
    for d in range(far):
        for i in range(NEAR):
            start = pl.multiple_of((me[0] ^ (d * NEAR + i)) * (share * pack), share * pack)
            for q in range(pack):
                rows = grads[pl.ds(start + q, share, stride=pack), :]
                outs[d][i, :, q * rank : (q + 1) * rank] = rows.astype(jnp.bfloat16)


def packed_grads(me, far, tokens, blocks, places, before, cotangent, mask):
    rank, width = blocks[0].shape[-2], cotangent.shape[1]
    shape = (NEAR, width * rank // LANES // (far * NEAR), LANES)
    return pl.pallas_call(
        functools.partial(grads_kernel, far, places),
        out_shape=[jax.ShapeDtypeStruct(shape, jnp.bfloat16)] * far,
        in_specs=[SMEM] + [VMEM] * (len(blocks) + 4),
        out_specs=[VMEM] * far,
        scratch_shapes=[pltpu.VMEM((width, rank), jnp.float32)],
        compiler_params=pltpu.CompilerParams(vmem_limit_bytes=6 * MIB),
        cost_estimate=pl.CostEstimate(flops=300000000, bytes_accessed=5000000, transcendentals=0),
        name="grads",
    )(me, tokens, *blocks, before, cotangent, mask)


def times_weights(left, first, weights, weights_hbm, start, streamed, sems, total):
    width = total.shape[1]
    copies = [
        pltpu.make_async_copy(
            weights_hbm.at[pl.ds(start + i, LANES), pl.ds(first, width)],
            streamed.at[pl.ds(i, LANES)],
            sems.at[i // LANES],
        )
        for i in range(0, streamed.shape[0], LANES)
    ]
    for copy in copies:
        copy.start()
    left = left()
    row = 0
    for part in weights:
        rows = part.shape[0]
        term = jnp.dot(left[:, row : row + rows], part[:, pl.ds(first, width)], preferred_element_type=jnp.float32)
        total[...] = term if row == 0 else total[...] + term
        row += rows
    for i, copy in enumerate(copies):
        copy.wait()
        part = streamed[i * LANES : (i + 1) * LANES, :]
        total[...] += jnp.dot(left[:, row : row + LANES], part, preferred_element_type=jnp.float32)
        row += LANES


def send_kernel(far, start, me, *refs):
    own, came = refs[:far], refs[far : far + NEAR - 1]
    weights = refs[far + NEAR - 1 : -7]
    weights_hbm, send, left, x, streamed, total, sems = refs[-7:]
    n = far * NEAR
    share = own[0].shape[1]
    pitch = x.shape[1] // n

    def arrange():
        for k in range(n):
            d, near = k // NEAR, k % NEAR
            rows = came[near - 1][d] if near else own[d][0]
            place = pl.multiple_of((me[0] ^ k) * pitch, pitch)
            for h in range(x.shape[0]):
                x[h, pl.ds(place, share), :] = rows[:, h * 128 : (h + 1) * 128].astype(jnp.float32)
        for j in range(share):
            for h in range(x.shape[0]):
                at = j * LANES + h * 128
                left[:, at : at + 128] = x[h, pl.ds(j, n, stride=pitch), :].astype(jnp.bfloat16)
        return left

    half = total.shape[1]
    first = pl.multiple_of((1 - (me[0] & 1)) * half, half)
    times_weights(arrange, first, weights, weights_hbm, start, streamed, sems, total)
    send[...] = total[...].astype(jnp.bfloat16)


def keep_kernel(start, me, left, *refs):
    weights = refs[:-4]
    weights_hbm, total, streamed, sems = refs[-4:]
    half = total.shape[1]
    first = pl.multiple_of((me[0] & 1) * half, half)
    times_weights(lambda: left, first, weights, weights_hbm, start, streamed, sems, total)


def send_features(me, own, came, weights, projection):
    far = len(own)
    n = far * NEAR
    share = own[0].shape[1]
    depth, width = projection.shape
    start = sum(part.shape[0] for part in weights)
    half = (n, width // 2)
    return pl.pallas_call(
        functools.partial(send_kernel, far, start),
        out_shape=[jax.ShapeDtypeStruct(half, jnp.bfloat16), jax.ShapeDtypeStruct((n, depth), jnp.bfloat16)],
        in_specs=[SMEM] + [VMEM] * (far + len(came) + len(weights)) + [ANY],
        out_specs=[VMEM, VMEM],
        scratch_shapes=[
            pltpu.VMEM((LANES // 128, n * max(share, 8), 128), jnp.float32),
            pltpu.VMEM((depth - start, width // 2), projection.dtype),
            pltpu.VMEM(half, jnp.float32),
            pltpu.SemaphoreType.DMA(((depth - start) // LANES,)),
        ],
        compiler_params=pltpu.CompilerParams(vmem_limit_bytes=12 * MIB),
        cost_estimate=pl.CostEstimate(flops=300000000, bytes_accessed=17000000, transcendentals=0),
        name="features_send",
    )(me, *own, *came, *weights, in_hbm(projection))


def keep_features(me, left, weights, projection):
    n = left.shape[0]
    depth, width = projection.shape
    start = sum(part.shape[0] for part in weights)
    return pl.pallas_call(
        functools.partial(keep_kernel, start),
        out_shape=jax.ShapeDtypeStruct((n, width // 2), jnp.float32),
        in_specs=[SMEM, VMEM] + [VMEM] * len(weights) + [ANY],
        out_specs=VMEM,
        scratch_shapes=[
            pltpu.VMEM((depth - start, width // 2), projection.dtype),
            pltpu.SemaphoreType.DMA(((depth - start) // LANES,)),
        ],
        compiler_params=pltpu.CompilerParams(vmem_limit_bytes=12 * MIB),
        cost_estimate=pl.CostEstimate(flops=300000000, bytes_accessed=17000000, transcendentals=0),
        name="features_keep",
    )(me, left, *weights, in_hbm(projection))


def scores_kernel(me, targets, partner_targets, kept, *refs):
    mine, send = refs[-2:]
    features = kept[...]
    for arrived in refs[:-2]:
        features += arrived[...].astype(jnp.float32)
    count, half = features.shape
    start = pl.multiple_of((me[0] & 1) * half, half)
    high = lax.Precision.HIGHEST
    ones = jnp.ones((targets.shape[0], half), jnp.float32)
    squares = lax.dot_general(ones, features * features, NT, precision=high, preferred_element_type=jnp.float32)
    rest = jnp.zeros((targets.shape[0], mine.shape[1] - 2 * count), jnp.float32)
    for source, out in ((targets, mine), (partner_targets, send)):
        scale = lax.rsqrt(jnp.sum(source[...] * source[...], axis=1, keepdims=True) / PDIM + 1e-06)
        dots = lax.dot_general(
            source[:, pl.ds(start, half)], features, NT, precision=high, preferred_element_type=jnp.float32
        )
        parts = [dots * scale, squares] + ([rest] if rest.shape[1] else [])
        out[...] = jnp.concatenate(parts, axis=1)


def partial_scores(me, targets, partner_targets, kept, arrived):
    shape = jax.ShapeDtypeStruct((targets.shape[0], 128), jnp.float32)
    return pl.pallas_call(
        scores_kernel,
        out_shape=[shape, shape],
        in_specs=[SMEM] + [VMEM] * (3 + len(arrived)),
        out_specs=[VMEM, VMEM],
        compiler_params=pltpu.CompilerParams(vmem_limit_bytes=6 * MIB),
        name="partial_scores",
    )(me, targets, partner_targets, kept, *arrived)


def body(tokens, cotangent, response_loss_mask, adapter_down_weight, projection, targets):
    n = lax.axis_size("shard")
    far = n // NEAR
    me = lax.axis_index("shard").astype(jnp.int32).reshape(1)
    chunks = projection.shape[0] // LANES
    cuts = [chunks * i // 16 * LANES for i in (0, 2, 7, 11)]
    strips = [[(projection, lo, hi - lo)] if hi > lo else [] for lo, hi in zip(cuts, cuts[1:])]
    block = adapter_down_weight

    whole = [(tokens, 0, tokens.shape[0]), (cotangent, 0, cotangent.shape[0])]
    whole += [(response_loss_mask.reshape(1, -1), 0, 1), (block, 0, block.shape[0])]
    tokens, cotangent, mask, own = load("load_1", whole, (me,))
    column = [swap(block, NEAR * d, n) for d in range(1, far)]
    across = swap(own, 2, n)
    weights = list(load("load_head", strips[0], (own,))) if strips[0] else []
    picks = [[(d,) for d in range(far)], [(d,) for d in range(1, far)]]
    column, sent = join("join_blocks", [own] + column, picks, block.shape, (across, *weights))
    near = [NEAR * d for d in range(far)]
    weights += load("load_2", strips[1], (sent,))
    other = swap(column, 1, n)
    blocks, places = [column, across, swap(across, 1, n), other], [near, [2], [3], [k + 1 for k in near]]
    total = partial_lowrank("lowrank_1", me, tokens, blocks, places)
    sent = hold("hold", swap(sent, 2, n), (weights[-1], total))
    total = partial_lowrank("lowrank_2", me, tokens, [sent], [[k + 2 for k in near[1:]]], (total,))
    places = [[k + 3 for k in near[1:]]]
    rows = packed_grads(me, far, tokens, [swap(sent, 1, n)], places, total, cotangent, mask)

    targets, *part = load("load_3", [(targets, 0, targets.shape[0])] + strips[2], (rows[0],))
    weights += part
    rows = [rows[0]] + [swap(rows[d], NEAR * d, n) for d in range(1, far)]
    picks = [[(d, k) for d in range(far)] for k in range(1, NEAR)]
    came = join("join_rows", rows, picks, rows[0].shape[1:], (targets,))
    came = [swap(came[k - 1], k, n) for k in range(1, NEAR)]
    partner_targets = swap(targets, 1, n)

    send, left = send_features(me, rows, came, weights, projection)
    kept = keep_features(me, left, weights, projection) + swap(send, 1, n).astype(jnp.float32)
    kept = kept + swap(kept.astype(jnp.bfloat16), 2, n).astype(jnp.float32)
    half = kept.astype(jnp.bfloat16)
    arrived = [swap(half, NEAR * d, n) for d in range(1, far)]
    mine, send = partial_scores(me, targets, partner_targets, kept, arrived)
    total = mine + swap(send, 1, n)
    scale = lax.rsqrt(total[:, n : 2 * n] / PDIM + 1e-06)
    return (total[:, :n] * scale / PDIM).T


def solution(mesh):
    in_specs = (
        P(("groups", "shard"), None),
        P(("groups", "shard"), None),
        P(("groups", "shard")),
        P(None, "shard"),
        P("shard", None),
        P(("groups", "shard"), None),
    )
    out_specs = P("groups", "shard")
    return jax.shard_map(body, mesh=mesh, in_specs=in_specs, out_specs=out_specs, check_vma=False)
```

```python
import functools

import jax
import jax.numpy as jnp
from jax import lax
from jax.experimental import pallas as pl
from jax.experimental.pallas import tpu as pltpu
from jax.sharding import PartitionSpec as P

PDIM = 4096
LENGTH = 256
LANES = 256
NEAR = 4
MIB = 1 << 20
NT = (((1,), (1,)), ((), ()))
VMEM = pl.BlockSpec(memory_space=pltpu.VMEM)
SMEM = pl.BlockSpec(memory_space=pltpu.SMEM)
ANY = pl.BlockSpec(memory_space=pl.ANY)


def swap(value, bit, n):
    return lax.ppermute(value, "shard", [(s, s ^ bit) for s in range(n)])


def span(bits):
    sums = [0]
    for bit in bits:
        sums += [k + bit for k in sums]
    return sums


def in_hbm(value):
    return pltpu.with_memory_space_constraint(value, pltpu.HBM)


def load_kernel(count, starts, *refs):
    sources, outs, sems = refs[:count], refs[-1 - count : -1], refs[-1]
    copies = []
    for source, start, out in zip(sources, starts, outs):
        rows = out.shape[0]
        step = min(rows, LANES // 2)
        for i in range(0, rows, step):
            part = source.at[pl.ds(start + i, step)]
            copies.append(pltpu.make_async_copy(part, out.at[pl.ds(i, step)], sems.at[len(copies)]))
    for copy in copies:
        copy.start()
    for copy in copies:
        copy.wait()


def load(name, parts, after):
    size = sum(rows * array.size // array.shape[0] * array.dtype.itemsize for array, _, rows in parts)
    pieces = sum(max(rows // (LANES // 2), 1) for _, _, rows in parts)
    return pl.pallas_call(
        functools.partial(load_kernel, len(parts), [start for _, start, _ in parts]),
        out_shape=[pltpu.VMEM((rows,) + array.shape[1:], array.dtype) for array, _, rows in parts],
        in_specs=[ANY] * (len(parts) + len(after)),
        out_specs=[VMEM] * len(parts),
        scratch_shapes=[pltpu.SemaphoreType.DMA((pieces,))],
        compiler_params=pltpu.CompilerParams(vmem_limit_bytes=MIB),
        cost_estimate=pl.CostEstimate(flops=0, bytes_accessed=2 * size, transcendentals=0),
        name=name,
    )(*[in_hbm(array) for array, _, _ in parts], *after)


def hold(name, value, after):
    return pl.pallas_call(
        lambda *refs: None,
        out_shape=jax.ShapeDtypeStruct(value.shape, value.dtype),
        in_specs=[ANY] * (1 + len(after)),
        out_specs=ANY,
        input_output_aliases={0: 0},
        compiler_params=pltpu.CompilerParams(vmem_limit_bytes=MIB),
        name=name,
    )(value, *after)


def join_kernel(picks, *refs):
    for pick, out in zip(picks, refs[-len(picks) :]):
        for target, (source, *entry) in enumerate(pick):
            out[target] = refs[source][entry[0]] if entry else refs[source][...]


def join(name, values, picks, shape, after=()):
    return pl.pallas_call(
        functools.partial(join_kernel, picks),
        out_shape=[jax.ShapeDtypeStruct((len(pick),) + shape, values[0].dtype) for pick in picks],
        in_specs=[VMEM] * len(values) + [ANY] * len(after),
        out_specs=[VMEM] * len(picks),
        compiler_params=pltpu.CompilerParams(vmem_limit_bytes=2 * MIB),
        name=name,
    )(*values, *after)


def add_lowrank(total, me, blocks, places, tokens):
    for block, owners in zip(blocks, places):
        depth = block.shape[-1]
        for i, k in enumerate(owners):
            start = pl.multiple_of((me[0] ^ k) * depth, depth)
            part = block[i] if len(block.shape) == 3 else block[...]
            total += lax.dot_general(part, tokens[:, pl.ds(start, depth)], NT, preferred_element_type=jnp.float32)
    return total


def lowrank_kernel(places, me, tokens, *refs):
    blocks, out = refs[: len(places)], refs[-1]
    before = refs[len(places)][...] if len(refs) > len(places) + 1 else jnp.zeros(out.shape, jnp.float32)
    out[...] = add_lowrank(before, me, blocks, places, tokens)


def partial_lowrank(name, me, tokens, blocks, places, before=()):
    return pl.pallas_call(
        functools.partial(lowrank_kernel, places),
        out_shape=jax.ShapeDtypeStruct((blocks[0].shape[-2], tokens.shape[0]), jnp.float32),
        in_specs=[SMEM] + [VMEM] * (1 + len(blocks) + len(before)),
        out_specs=VMEM,
        compiler_params=pltpu.CompilerParams(vmem_limit_bytes=2 * MIB),
        cost_estimate=pl.CostEstimate(flops=200000000, bytes_accessed=2000000, transcendentals=0),
        name=name,
    )(me, tokens, *blocks, *before)


def grads_kernel(owners, places, me, tokens, *refs):
    blocks = refs[: len(places)]
    before, cotangent, mask = refs[len(places) : len(places) + 3]
    outs, grads = refs[-1 - len(owners) : -1], refs[-1]
    total = add_lowrank(before[...], me, blocks, places, tokens)
    rank = total.shape[0]
    lowrank = total.astype(jnp.bfloat16) * mask[...].astype(jnp.bfloat16)
    turned = jnp.dot(lowrank, cotangent[...], preferred_element_type=jnp.float32)
    grads[...] = turned.T
    pack = LANES // rank
    share = outs[0].shape[1]
    for out, ks in zip(outs, owners):
        for i, k in enumerate(ks):
            start = pl.multiple_of((me[0] ^ k) * (share * pack), share * pack)
            for q in range(pack):
                rows = grads[pl.ds(start + q, share, stride=pack), :]
                out[i, :, q * rank : (q + 1) * rank] = rows.astype(jnp.bfloat16)


def packed_grads(me, owners, tokens, blocks, places, before, cotangent, mask):
    rank, width = blocks[0].shape[-2], cotangent.shape[1]
    share = width * rank // LANES // sum(len(ks) for ks in owners)
    return pl.pallas_call(
        functools.partial(grads_kernel, owners, places),
        out_shape=[jax.ShapeDtypeStruct((len(ks), share, LANES), jnp.bfloat16) for ks in owners],
        in_specs=[SMEM] + [VMEM] * (len(blocks) + 4),
        out_specs=[VMEM] * len(owners),
        scratch_shapes=[pltpu.VMEM((width, rank), jnp.float32)],
        compiler_params=pltpu.CompilerParams(vmem_limit_bytes=6 * MIB),
        cost_estimate=pl.CostEstimate(flops=300000000, bytes_accessed=5000000, transcendentals=0),
        name="grads",
    )(me, tokens, *blocks, before, cotangent, mask)


def features_kernel(places, count, start, me, *refs):
    arrays, weights = refs[:count], refs[count:-8]
    weights_hbm, keep, send, x, left, streamed, total, sems = refs[-8:]
    n = len(places)
    share = arrays[0].shape[1]
    pitch = x.shape[1] // n
    copies = [
        pltpu.make_async_copy(
            weights_hbm.at[pl.ds(start + i, LANES)], streamed.at[pl.ds(i, LANES)], sems.at[i // LANES]
        )
        for i in range(0, streamed.shape[0], LANES)
    ]
    for copy in copies:
        copy.start()
    for k, (source, entry) in enumerate(places):
        rows = arrays[source][entry]
        place = pl.multiple_of((me[0] ^ k) * pitch, pitch)
        for h in range(x.shape[0]):
            x[h, pl.ds(place, share), :] = rows[:, h * 128 : (h + 1) * 128].astype(jnp.float32)
    for j in range(share):
        for h in range(x.shape[0]):
            at = j * LANES + h * 128
            left[:, at : at + 128] = x[h, pl.ds(j, n, stride=pitch), :].astype(jnp.bfloat16)
    row = 0
    for part in weights:
        term = jnp.dot(left[:, row : row + part.shape[0]], part[...], preferred_element_type=jnp.float32)
        total[...] = term if row == 0 else total[...] + term
        row += part.shape[0]
    for i, copy in enumerate(copies):
        copy.wait()
        part = streamed[i * LANES : (i + 1) * LANES, :]
        total[...] += jnp.dot(left[:, row : row + LANES], part, preferred_element_type=jnp.float32)
        row += LANES
    part = keep.shape[1]
    mine = pl.multiple_of((me[0] & 1) * part, part)
    partner = pl.multiple_of((1 - (me[0] & 1)) * part, part)
    keep[...] = total[:, pl.ds(mine, part)]
    send[...] = total[:, pl.ds(partner, part)].astype(jnp.bfloat16)


def partial_features(me, arrays, places, weights, projection):
    n = len(places)
    share = arrays[0].shape[1]
    depth, width = projection.shape
    start = sum(part.shape[0] for part in weights)
    half = (n, width // 2)
    return pl.pallas_call(
        functools.partial(features_kernel, places, len(arrays), start),
        out_shape=[jax.ShapeDtypeStruct(half, jnp.float32), jax.ShapeDtypeStruct(half, jnp.bfloat16)],
        in_specs=[SMEM] + [VMEM] * (len(arrays) + len(weights)) + [ANY],
        out_specs=[VMEM, VMEM],
        scratch_shapes=[
            pltpu.VMEM((LANES // 128, n * max(share, 8), 128), jnp.float32),
            pltpu.VMEM((n, depth), jnp.bfloat16),
            pltpu.VMEM((depth - start, width), projection.dtype),
            pltpu.VMEM((n, width), jnp.float32),
            pltpu.SemaphoreType.DMA(((depth - start) // LANES,)),
        ],
        compiler_params=pltpu.CompilerParams(vmem_limit_bytes=20 * MIB),
        cost_estimate=pl.CostEstimate(flops=600000000, bytes_accessed=34000000, transcendentals=0),
        name="features",
    )(me, *arrays, *weights, in_hbm(projection))


def scores_kernel(me, targets, partner_targets, kept, *refs):
    mine, send = refs[-2:]
    features = kept[...]
    for arrived in refs[:-2]:
        features += arrived[...].astype(jnp.float32)
    count, half = features.shape
    start = pl.multiple_of((me[0] & 1) * half, half)
    high = lax.Precision.HIGHEST
    ones = jnp.ones((targets.shape[0], half), jnp.float32)
    squares = lax.dot_general(ones, features * features, NT, precision=high, preferred_element_type=jnp.float32)
    rest = jnp.zeros((targets.shape[0], mine.shape[1] - 2 * count), jnp.float32)
    for source, out in ((targets, mine), (partner_targets, send)):
        scale = lax.rsqrt(jnp.sum(source[...] * source[...], axis=1, keepdims=True) / PDIM + 1e-06)
        dots = lax.dot_general(
            source[:, pl.ds(start, half)], features, NT, precision=high, preferred_element_type=jnp.float32
        )
        parts = [dots * scale, squares] + ([rest] if rest.shape[1] else [])
        out[...] = jnp.concatenate(parts, axis=1)


def partial_scores(me, targets, partner_targets, kept, arrived):
    shape = jax.ShapeDtypeStruct((targets.shape[0], 128), jnp.float32)
    return pl.pallas_call(
        scores_kernel,
        out_shape=[shape, shape],
        in_specs=[SMEM] + [VMEM] * (3 + len(arrived)),
        out_specs=[VMEM, VMEM],
        compiler_params=pltpu.CompilerParams(vmem_limit_bytes=6 * MIB),
        name="partial_scores",
    )(me, targets, partner_targets, kept, *arrived)


def body(tokens, cotangent, response_loss_mask, adapter_down_weight, projection, targets):
    n = lax.axis_size("shard")
    far = n // NEAR
    me = lax.axis_index("shard").astype(jnp.int32).reshape(1)
    chunks = projection.shape[0] // LANES
    cuts = [chunks * i // 16 * LANES for i in (0, 3, 8, 11)]
    strips = [[(projection, lo, hi - lo)] if hi > lo else [] for lo, hi in zip(cuts, cuts[1:])]
    block = adapter_down_weight
    bits = [1 << i for i in range(n.bit_length() - 1)]

    whole = [(tokens, 0, tokens.shape[0]), (cotangent, 0, cotangent.shape[0])]
    whole += [(response_loss_mask.reshape(1, -1), 0, 1)]
    tokens, cotangent, mask, *weights = load("load_1", whole + strips[0], (me,))
    column = [block] + [swap(block, NEAR * d, n) for d in range(1, far)]
    (column,) = join("join_blocks", column, [[(d,) for d in range(far)]], block.shape, (mask,))
    weights += load("load_2", strips[1], (column,))
    places = [[NEAR * d + k for d in range(far)] for k in range(NEAR)]
    total = partial_lowrank("lowrank_1", me, tokens, [column, swap(column, 1, n)], places[:2])
    across = hold("hold", swap(column, 2, n), (weights[-1], total))
    total = partial_lowrank("lowrank_2", me, tokens, [across], places[2:3], (total,))

    stages = [[1, bits[-1]]] + [bits[i : i + 2] for i in range(1, len(bits) - 1, 2)]
    left = span([b for stage in stages[1:] for b in stage])
    moves = span(stages[0])
    owners = [[m ^ r for r in left] for m in moves]
    rows = packed_grads(me, owners, tokens, [swap(across, 1, n)], places[3:], total, cotangent, mask)
    targets, *part = load("load_3", [(targets, 0, targets.shape[0])] + strips[2], (rows[0],))
    weights += part
    arrays = [rows[0]] + [swap(array, m, n) for array, m in zip(rows[1:], moves[1:])]
    held = {(m, r): (a, i) for a, m in enumerate(moves) for i, r in enumerate(left)}
    for number, stage in enumerate(stages[1:]):
        moves, left = span(stage), span([b for later in stages[number + 2 :] for b in later])
        pairs = [[(src, r ^ m) for src in sorted({s for s, _ in held}) for r in left] for m in moves]
        picks = [[held[pair] for pair in group] for group in pairs[1:]]
        after = (targets,) if number == 0 else ()
        sent = join(f"join_rows_{number}", arrays, picks, rows[0].shape[1:], after)
        kept = {pair: held[pair] for pair in pairs[0]}
        for m, group, array in zip(moves[1:], pairs[1:], sent):
            kept.update({(src ^ m, r ^ m): (len(arrays), i) for i, (src, r) in enumerate(group)})
            arrays.append(swap(array, m, n))
        held = kept
    partner_targets = swap(targets, 1, n)

    places = [held[k, 0] for k in range(n)]
    kept, send = partial_features(me, arrays, places, weights, projection)
    kept = kept + swap(send, 1, n).astype(jnp.float32)
    for stage in [bits[1:3]] + [[bit] for bit in bits[3:]]:
        half = kept.astype(jnp.bfloat16)
        arrived = [swap(half, m, n) for m in span(stage)[1:]]
        if bits[-1] not in stage:
            kept = kept + sum(value.astype(jnp.float32) for value in arrived)
    mine, send = partial_scores(me, targets, partner_targets, kept, arrived)
    total = mine + swap(send, 1, n)
    scale = lax.rsqrt(total[:, n : 2 * n] / PDIM + 1e-06)
    return (total[:, :n] * scale / PDIM).T


def solution(mesh):
    in_specs = (
        P(("groups", "shard"), None),
        P(("groups", "shard"), None),
        P(("groups", "shard")),
        P(None, "shard"),
        P("shard", None),
        P(("groups", "shard"), None),
    )
    out_specs = P("groups", "shard")
    return jax.shard_map(body, mesh=mesh, in_specs=in_specs, out_specs=out_specs, check_vma=False)
```

```python
import functools

import jax
import jax.numpy as jnp
from jax import lax
from jax.experimental import pallas as pl
from jax.experimental.pallas import tpu as pltpu
from jax.sharding import PartitionSpec as P

PDIM = 4096
LENGTH = 256
LANES = 256
NEAR = 4
MIB = 1 << 20
NT = (((1,), (1,)), ((), ()))
VMEM = pl.BlockSpec(memory_space=pltpu.VMEM)
SMEM = pl.BlockSpec(memory_space=pltpu.SMEM)
ANY = pl.BlockSpec(memory_space=pl.ANY)


def swap(value, bit, n):
    return lax.ppermute(value, "shard", [(s, s ^ bit) for s in range(n)])


def span(bits):
    sums = [0]
    for bit in bits:
        sums += [k + bit for k in sums]
    return sums


def in_hbm(value):
    return pltpu.with_memory_space_constraint(value, pltpu.HBM)


def load_kernel(count, starts, *refs):
    sources, outs, sems = refs[:count], refs[-1 - count : -1], refs[-1]
    copies = []
    for source, start, out in zip(sources, starts, outs):
        rows = out.shape[0]
        step = min(rows, LANES // 2)
        for i in range(0, rows, step):
            part = source.at[pl.ds(start + i, step)]
            copies.append(pltpu.make_async_copy(part, out.at[pl.ds(i, step)], sems.at[len(copies)]))
    for copy in copies:
        copy.start()
    for copy in copies:
        copy.wait()


def load(name, parts, after):
    size = sum(rows * array.size // array.shape[0] * array.dtype.itemsize for array, _, rows in parts)
    pieces = sum(max(rows // (LANES // 2), 1) for _, _, rows in parts)
    return pl.pallas_call(
        functools.partial(load_kernel, len(parts), [start for _, start, _ in parts]),
        out_shape=[pltpu.VMEM((rows,) + array.shape[1:], array.dtype) for array, _, rows in parts],
        in_specs=[ANY] * (len(parts) + len(after)),
        out_specs=[VMEM] * len(parts),
        scratch_shapes=[pltpu.SemaphoreType.DMA((pieces,))],
        compiler_params=pltpu.CompilerParams(vmem_limit_bytes=MIB),
        cost_estimate=pl.CostEstimate(flops=0, bytes_accessed=2 * size, transcendentals=0),
        name=name,
    )(*[in_hbm(array) for array, _, _ in parts], *after)


def hold(name, value, after):
    return pl.pallas_call(
        lambda *refs: None,
        out_shape=jax.ShapeDtypeStruct(value.shape, value.dtype),
        in_specs=[ANY] * (1 + len(after)),
        out_specs=ANY,
        input_output_aliases={0: 0},
        compiler_params=pltpu.CompilerParams(vmem_limit_bytes=MIB),
        name=name,
    )(value, *after)


def join_kernel(picks, *refs):
    for pick, out in zip(picks, refs[-len(picks) :]):
        for target, (source, *entry) in enumerate(pick):
            out[target] = refs[source][entry[0]] if entry else refs[source][...]


def join(name, values, picks, shape, after=()):
    return pl.pallas_call(
        functools.partial(join_kernel, picks),
        out_shape=[jax.ShapeDtypeStruct((len(pick),) + shape, values[0].dtype) for pick in picks],
        in_specs=[VMEM] * len(values) + [ANY] * len(after),
        out_specs=[VMEM] * len(picks),
        compiler_params=pltpu.CompilerParams(vmem_limit_bytes=2 * MIB),
        name=name,
    )(*values, *after)


def add_lowrank(total, me, blocks, places, tokens):
    for block, owners in zip(blocks, places):
        depth = block.shape[-1]
        for i, k in enumerate(owners):
            start = pl.multiple_of((me[0] ^ k) * depth, depth)
            part = block[i] if len(block.shape) == 3 else block[...]
            total += lax.dot_general(part, tokens[:, pl.ds(start, depth)], NT, preferred_element_type=jnp.float32)
    return total


def lowrank_kernel(places, me, tokens, *refs):
    blocks, out = refs[: len(places)], refs[-1]
    before = refs[len(places)][...] if len(refs) > len(places) + 1 else jnp.zeros(out.shape, jnp.float32)
    out[...] = add_lowrank(before, me, blocks, places, tokens)


def partial_lowrank(name, me, tokens, blocks, places, before=()):
    return pl.pallas_call(
        functools.partial(lowrank_kernel, places),
        out_shape=jax.ShapeDtypeStruct((blocks[0].shape[-2], tokens.shape[0]), jnp.float32),
        in_specs=[SMEM] + [VMEM] * (1 + len(blocks) + len(before)),
        out_specs=VMEM,
        compiler_params=pltpu.CompilerParams(vmem_limit_bytes=2 * MIB),
        cost_estimate=pl.CostEstimate(flops=200000000, bytes_accessed=2000000, transcendentals=0),
        name=name,
    )(me, tokens, *blocks, *before)


def grads_kernel(owners, places, me, tokens, *refs):
    blocks = refs[: len(places)]
    before, cotangent, mask = refs[len(places) : len(places) + 3]
    outs, grads = refs[-1 - len(owners) : -1], refs[-1]
    total = add_lowrank(before[...], me, blocks, places, tokens)
    rank = total.shape[0]
    lowrank = total.astype(jnp.bfloat16) * mask[...].astype(jnp.bfloat16)
    turned = jnp.dot(lowrank, cotangent[...], preferred_element_type=jnp.float32)
    grads[...] = turned.T
    pack = LANES // rank
    share = outs[0].shape[1]
    for out, ks in zip(outs, owners):
        for i, k in enumerate(ks):
            start = pl.multiple_of((me[0] ^ k) * (share * pack), share * pack)
            for q in range(pack):
                rows = grads[pl.ds(start + q, share, stride=pack), :]
                out[i, :, q * rank : (q + 1) * rank] = rows.astype(jnp.bfloat16)


def packed_grads(me, owners, tokens, blocks, places, before, cotangent, mask):
    rank, width = blocks[0].shape[-2], cotangent.shape[1]
    share = width * rank // LANES // sum(len(ks) for ks in owners)
    return pl.pallas_call(
        functools.partial(grads_kernel, owners, places),
        out_shape=[jax.ShapeDtypeStruct((len(ks), share, LANES), jnp.bfloat16) for ks in owners],
        in_specs=[SMEM] + [VMEM] * (len(blocks) + 4),
        out_specs=[VMEM] * len(owners),
        scratch_shapes=[pltpu.VMEM((width, rank), jnp.float32)],
        compiler_params=pltpu.CompilerParams(vmem_limit_bytes=6 * MIB),
        cost_estimate=pl.CostEstimate(flops=300000000, bytes_accessed=5000000, transcendentals=0),
        name="grads",
    )(me, tokens, *blocks, before, cotangent, mask)


def features_kernel(places, count, start, me, *refs):
    arrays, weights = refs[:count], refs[count:-8]
    weights_hbm, keep, send, x, left, streamed, total, sems = refs[-8:]
    n = len(places)
    share = arrays[0].shape[1]
    pitch = x.shape[1] // n
    copies = [
        pltpu.make_async_copy(
            weights_hbm.at[pl.ds(start + i, LANES)], streamed.at[pl.ds(i, LANES)], sems.at[i // LANES]
        )
        for i in range(0, streamed.shape[0], LANES)
    ]
    for copy in copies:
        copy.start()
    for k, (source, entry) in enumerate(places):
        rows = arrays[source][entry]
        place = pl.multiple_of((me[0] ^ k) * pitch, pitch)
        for h in range(x.shape[0]):
            x[h, pl.ds(place, share), :] = rows[:, h * 128 : (h + 1) * 128].astype(jnp.float32)
    for j in range(share):
        for h in range(x.shape[0]):
            at = j * LANES + h * 128
            left[:, at : at + 128] = x[h, pl.ds(j, n, stride=pitch), :].astype(jnp.bfloat16)
    row = 0
    for part in weights:
        term = jnp.dot(left[:, row : row + part.shape[0]], part[...], preferred_element_type=jnp.float32)
        total[...] = term if row == 0 else total[...] + term
        row += part.shape[0]
    for i, copy in enumerate(copies):
        copy.wait()
        part = streamed[i * LANES : (i + 1) * LANES, :]
        total[...] += jnp.dot(left[:, row : row + LANES], part, preferred_element_type=jnp.float32)
        row += LANES
    part = keep.shape[1]
    mine = pl.multiple_of((me[0] & 1) * part, part)
    partner = pl.multiple_of((1 - (me[0] & 1)) * part, part)
    keep[...] = total[:, pl.ds(mine, part)]
    send[...] = total[:, pl.ds(partner, part)].astype(jnp.bfloat16)


def partial_features(me, arrays, places, weights, projection):
    n = len(places)
    share = arrays[0].shape[1]
    depth, width = projection.shape
    start = sum(part.shape[0] for part in weights)
    half = (n, width // 2)
    return pl.pallas_call(
        functools.partial(features_kernel, places, len(arrays), start),
        out_shape=[jax.ShapeDtypeStruct(half, jnp.float32), jax.ShapeDtypeStruct(half, jnp.bfloat16)],
        in_specs=[SMEM] + [VMEM] * (len(arrays) + len(weights)) + [ANY],
        out_specs=[VMEM, VMEM],
        scratch_shapes=[
            pltpu.VMEM((LANES // 128, n * max(share, 8), 128), jnp.float32),
            pltpu.VMEM((n, depth), jnp.bfloat16),
            pltpu.VMEM((depth - start, width), projection.dtype),
            pltpu.VMEM((n, width), jnp.float32),
            pltpu.SemaphoreType.DMA(((depth - start) // LANES,)),
        ],
        compiler_params=pltpu.CompilerParams(vmem_limit_bytes=20 * MIB),
        cost_estimate=pl.CostEstimate(flops=600000000, bytes_accessed=34000000, transcendentals=0),
        name="features",
    )(me, *arrays, *weights, in_hbm(projection))


def scores_kernel(me, targets, partner_targets, kept, *refs):
    mine, send = refs[-2:]
    features = kept[...]
    for arrived in refs[:-2]:
        features += arrived[...].astype(jnp.float32)
    count, half = features.shape
    start = pl.multiple_of((me[0] & 1) * half, half)
    high = lax.Precision.HIGHEST
    ones = jnp.ones((targets.shape[0], half), jnp.float32)
    squares = lax.dot_general(ones, features * features, NT, precision=high, preferred_element_type=jnp.float32)
    rest = jnp.zeros((targets.shape[0], mine.shape[1] - 2 * count), jnp.float32)
    for source, out in ((targets, mine), (partner_targets, send)):
        scale = lax.rsqrt(jnp.sum(source[...] * source[...], axis=1, keepdims=True) / PDIM + 1e-06)
        dots = lax.dot_general(
            source[:, pl.ds(start, half)], features, NT, precision=high, preferred_element_type=jnp.float32
        )
        parts = [dots * scale, squares] + ([rest] if rest.shape[1] else [])
        out[...] = jnp.concatenate(parts, axis=1)


def partial_scores(me, targets, partner_targets, kept, arrived):
    shape = jax.ShapeDtypeStruct((targets.shape[0], 128), jnp.float32)
    return pl.pallas_call(
        scores_kernel,
        out_shape=[shape, shape],
        in_specs=[SMEM] + [VMEM] * (3 + len(arrived)),
        out_specs=[VMEM, VMEM],
        compiler_params=pltpu.CompilerParams(vmem_limit_bytes=6 * MIB),
        name="partial_scores",
    )(me, targets, partner_targets, kept, *arrived)


def body(tokens, cotangent, response_loss_mask, adapter_down_weight, projection, targets):
    n = lax.axis_size("shard")
    far = n // NEAR
    me = lax.axis_index("shard").astype(jnp.int32).reshape(1)
    chunks = projection.shape[0] // LANES
    cuts = [chunks * i // 16 * LANES for i in (0, 3, 10, 13)]
    strips = [[(projection, lo, hi - lo)] if hi > lo else [] for lo, hi in zip(cuts, cuts[1:])]
    block = adapter_down_weight
    bits = [1 << i for i in range(n.bit_length() - 1)]

    whole = [(tokens, 0, tokens.shape[0]), (cotangent, 0, cotangent.shape[0])]
    whole += [(response_loss_mask.reshape(1, -1), 0, 1)]
    tokens, cotangent, mask, *weights = load("load_1", whole + strips[0], (me,))
    column = [block] + [swap(block, NEAR * d, n) for d in range(1, far)]
    (column,) = join("join_blocks", column, [[(d,) for d in range(far)]], block.shape, (mask,))
    weights += load("load_2", strips[1], (column,))
    places = [[NEAR * d + k for d in range(far)] for k in range(NEAR)]
    total = partial_lowrank("lowrank_1", me, tokens, [column], places[:1])
    across = hold("hold", swap(column, 2, n), (weights[-1], total))
    total = partial_lowrank("lowrank_2", me, tokens, [swap(column, 1, n), across], places[1:3], (total,))

    stages = [bits[i : i + 2] for i in range(2, len(bits), 2)] + [bits[:2]]
    left = span([b for stage in stages[1:] for b in stage])
    moves = span(stages[0])
    owners = [[m ^ r for r in left] for m in moves]
    rows = packed_grads(me, owners, tokens, [swap(across, 1, n)], places[3:], total, cotangent, mask)
    targets, *part = load("load_3", [(targets, 0, targets.shape[0])] + strips[2], (rows[0],))
    weights += part
    arrays = [rows[0]] + [swap(array, m, n) for array, m in zip(rows[1:], moves[1:])]
    held = {(m, r): (a, i) for a, m in enumerate(moves) for i, r in enumerate(left)}
    for number, stage in enumerate(stages[1:]):
        moves, left = span(stage), span([b for later in stages[number + 2 :] for b in later])
        pairs = [[(src, r ^ m) for src in sorted({s for s, _ in held}) for r in left] for m in moves]
        picks = [[held[pair] for pair in group] for group in pairs[1:]]
        after = (targets,) if number == 0 else ()
        sent = join(f"join_rows_{number}", arrays, picks, rows[0].shape[1:], after)
        kept = {pair: held[pair] for pair in pairs[0]}
        for m, group, array in zip(moves[1:], pairs[1:], sent):
            kept.update({(src ^ m, r ^ m): (len(arrays), i) for i, (src, r) in enumerate(group)})
            arrays.append(swap(array, m, n))
        held = kept
    partner_targets = swap(targets, 1, n)

    places = [held[k, 0] for k in range(n)]
    kept, send = partial_features(me, arrays, places, weights, projection)
    kept = kept + swap(send, 1, n).astype(jnp.float32)
    for stage in [bits[1:3]] + [[bit] for bit in bits[3:]]:
        half = kept.astype(jnp.bfloat16)
        arrived = [swap(half, m, n) for m in span(stage)[1:]]
        if bits[-1] not in stage:
            kept = kept + sum(value.astype(jnp.float32) for value in arrived)
    mine, send = partial_scores(me, targets, partner_targets, kept, arrived)
    total = mine + swap(send, 1, n)
    scale = lax.rsqrt(total[:, n : 2 * n] / PDIM + 1e-06)
    return (total[:, :n] * scale / PDIM).T


def solution(mesh):
    in_specs = (
        P(("groups", "shard"), None),
        P(("groups", "shard"), None),
        P(("groups", "shard")),
        P(None, "shard"),
        P("shard", None),
        P(("groups", "shard"), None),
    )
    out_specs = P("groups", "shard")
    return jax.shard_map(body, mesh=mesh, in_specs=in_specs, out_specs=out_specs, check_vma=False)
```

```python
import functools

import jax
import jax.numpy as jnp
from jax import lax
from jax.experimental import pallas as pl
from jax.experimental.pallas import tpu as pltpu
from jax.sharding import PartitionSpec as P

PDIM = 4096
LENGTH = 256
LANES = 256
NEAR = 4
MIB = 1 << 20
HIDE = 30 * 10**9
NT = (((1,), (1,)), ((), ()))
VMEM = pl.BlockSpec(memory_space=pltpu.VMEM)
SMEM = pl.BlockSpec(memory_space=pltpu.SMEM)
ANY = pl.BlockSpec(memory_space=pl.ANY)


def swap(value, bit, n):
    return lax.ppermute(value, "shard", [(s, s ^ bit) for s in range(n)])


def span(bits):
    sums = [0]
    for bit in bits:
        sums += [k + bit for k in sums]
    return sums


def in_hbm(value):
    return pltpu.with_memory_space_constraint(value, pltpu.HBM)


def in_vmem(value):
    return pltpu.with_memory_space_constraint(value, pltpu.VMEM)


def load_kernel(count, starts, *refs):
    sources, outs, sems = refs[:count], refs[-1 - count : -1], refs[-1]
    copies = []
    for source, start, out in zip(sources, starts, outs):
        rows = out.shape[0]
        step = min(rows, LANES // 2)
        for i in range(0, rows, step):
            part = source.at[pl.ds(start + i, step)]
            copies.append(pltpu.make_async_copy(part, out.at[pl.ds(i, step)], sems.at[len(copies)]))
    for copy in copies:
        copy.start()
    for copy in copies:
        copy.wait()


def load(name, parts, after):
    size = sum(rows * array.size // array.shape[0] * array.dtype.itemsize for array, _, rows in parts)
    pieces = sum(max(rows // (LANES // 2), 1) for _, _, rows in parts)
    return pl.pallas_call(
        functools.partial(load_kernel, len(parts), [start for _, start, _ in parts]),
        out_shape=[pltpu.VMEM((rows,) + array.shape[1:], array.dtype) for array, _, rows in parts],
        in_specs=[ANY] * (len(parts) + len(after)),
        out_specs=[VMEM] * len(parts),
        scratch_shapes=[pltpu.SemaphoreType.DMA((pieces,))],
        compiler_params=pltpu.CompilerParams(vmem_limit_bytes=MIB),
        cost_estimate=pl.CostEstimate(flops=0, bytes_accessed=2 * size, transcendentals=0),
        name=name,
    )(*[in_hbm(array) for array, _, _ in parts], *after)


def hold(name, value, after, flops=0):
    return pl.pallas_call(
        lambda *refs: None,
        out_shape=jax.ShapeDtypeStruct(value.shape, value.dtype),
        in_specs=[ANY] * (1 + len(after)),
        out_specs=ANY,
        input_output_aliases={0: 0},
        compiler_params=pltpu.CompilerParams(vmem_limit_bytes=MIB),
        cost_estimate=pl.CostEstimate(flops=flops, bytes_accessed=2000000, transcendentals=0),
        name=name,
    )(value, *after)


def join_kernel(picks, *refs):
    for pick, out in zip(picks, refs[-len(picks) :]):
        for target, (source, *entry) in enumerate(pick):
            out[target] = refs[source][entry[0]] if entry else refs[source][...]


def join(name, values, picks, shape, after=(), flops=0):
    return pl.pallas_call(
        functools.partial(join_kernel, picks),
        out_shape=[jax.ShapeDtypeStruct((len(pick),) + shape, values[0].dtype) for pick in picks],
        in_specs=[VMEM] * len(values) + [ANY] * len(after),
        out_specs=[VMEM] * len(picks),
        compiler_params=pltpu.CompilerParams(vmem_limit_bytes=2 * MIB),
        cost_estimate=pl.CostEstimate(flops=flops, bytes_accessed=2000000, transcendentals=0),
        name=name,
    )(*values, *after)


def add_lowrank(total, me, blocks, places, tokens):
    for block, owners in zip(blocks, places):
        depth = block.shape[-1]
        for i, k in enumerate(owners):
            start = pl.multiple_of((me[0] ^ k) * depth, depth)
            part = block[i] if len(block.shape) == 3 else block[...]
            total += lax.dot_general(part, tokens[:, pl.ds(start, depth)], NT, preferred_element_type=jnp.float32)
    return total


def lowrank_kernel(places, me, tokens, *refs):
    blocks, out = refs[: len(places)], refs[-1]
    before = refs[len(places)][...] if len(refs) > len(places) + 1 else jnp.zeros(out.shape, jnp.float32)
    out[...] = add_lowrank(before, me, blocks, places, tokens)


def partial_lowrank(name, me, tokens, blocks, places, before=()):
    return pl.pallas_call(
        functools.partial(lowrank_kernel, places),
        out_shape=jax.ShapeDtypeStruct((blocks[0].shape[-2], tokens.shape[0]), jnp.float32),
        in_specs=[SMEM] + [VMEM] * (1 + len(blocks) + len(before)),
        out_specs=VMEM,
        compiler_params=pltpu.CompilerParams(vmem_limit_bytes=2 * MIB),
        cost_estimate=pl.CostEstimate(flops=100000000, bytes_accessed=2000000, transcendentals=0),
        name=name,
    )(me, tokens, *blocks, *before)


def grads_kernel(owners, places, me, tokens, *refs):
    blocks = refs[: len(places)]
    before, cotangent, mask = refs[len(places) : len(places) + 3]
    outs, grads = refs[-1 - len(owners) : -1], refs[-1]
    total = add_lowrank(before[...], me, blocks, places, tokens)
    rank = total.shape[0]
    lowrank = total.astype(jnp.bfloat16) * mask[...].astype(jnp.bfloat16)
    turned = jnp.dot(lowrank, cotangent[...], preferred_element_type=jnp.float32)
    grads[...] = turned.T
    pack = LANES // rank
    share = outs[0].shape[1]
    for out, ks in zip(outs, owners):
        for i, k in enumerate(ks):
            start = pl.multiple_of((me[0] ^ k) * (share * pack), share * pack)
            for q in range(pack):
                rows = grads[pl.ds(start + q, share, stride=pack), :]
                out[i, :, q * rank : (q + 1) * rank] = rows.astype(jnp.bfloat16)


def packed_grads(me, owners, tokens, blocks, places, before, cotangent, mask):
    rank, width = blocks[0].shape[-2], cotangent.shape[1]
    share = width * rank // LANES // sum(len(ks) for ks in owners)
    return pl.pallas_call(
        functools.partial(grads_kernel, owners, places),
        out_shape=[jax.ShapeDtypeStruct((len(ks), share, LANES), jnp.bfloat16) for ks in owners],
        in_specs=[SMEM] + [VMEM] * (len(blocks) + 4),
        out_specs=[VMEM] * len(owners),
        scratch_shapes=[pltpu.VMEM((width, rank), jnp.float32)],
        compiler_params=pltpu.CompilerParams(vmem_limit_bytes=6 * MIB),
        cost_estimate=pl.CostEstimate(flops=100000000, bytes_accessed=2000000, transcendentals=0),
        name="grads",
    )(me, tokens, *blocks, before, cotangent, mask)


def features_kernel(places, count, me, *refs):
    arrays, weights = refs[:count], refs[count]
    keep, send, x, left, total = refs[-5:]
    n = len(places)
    share = arrays[0].shape[1]
    pitch = x.shape[1] // n
    for k, (source, entry) in enumerate(places):
        rows = arrays[source][entry]
        place = pl.multiple_of((me[0] ^ k) * pitch, pitch)
        for h in range(x.shape[0]):
            x[h, pl.ds(place, share), :] = rows[:, h * 128 : (h + 1) * 128].astype(jnp.float32)
    for j in range(share):
        for h in range(x.shape[0]):
            at = j * LANES + h * 128
            left[:, at : at + 128] = x[h, pl.ds(j, n, stride=pitch), :].astype(jnp.bfloat16)
    total[...] = jnp.dot(left[...], weights[...], preferred_element_type=jnp.float32)
    part = keep.shape[1]
    mine = pl.multiple_of((me[0] & 1) * part, part)
    partner = pl.multiple_of((1 - (me[0] & 1)) * part, part)
    keep[...] = total[:, pl.ds(mine, part)]
    send[...] = total[:, pl.ds(partner, part)].astype(jnp.bfloat16)


def partial_features(me, arrays, places, projection):
    n = len(places)
    share = arrays[0].shape[1]
    depth, width = projection.shape
    half = (n, width // 2)
    return pl.pallas_call(
        functools.partial(features_kernel, places, len(arrays)),
        out_shape=[jax.ShapeDtypeStruct(half, jnp.float32), jax.ShapeDtypeStruct(half, jnp.bfloat16)],
        in_specs=[SMEM] + [VMEM] * (len(arrays) + 1),
        out_specs=[VMEM, VMEM],
        scratch_shapes=[
            pltpu.VMEM((LANES // 128, n * max(share, 8), 128), jnp.float32),
            pltpu.VMEM((n, depth), jnp.bfloat16),
            pltpu.VMEM((n, width), jnp.float32),
        ],
        compiler_params=pltpu.CompilerParams(vmem_limit_bytes=4 * MIB),
        cost_estimate=pl.CostEstimate(flops=600000000, bytes_accessed=34000000, transcendentals=0),
        name="features",
    )(me, *arrays, in_vmem(projection))


def scores_kernel(me, targets, partner_targets, kept, *refs):
    mine, send = refs[-2:]
    features = kept[...]
    for arrived in refs[:-2]:
        features += arrived[...].astype(jnp.float32)
    count, half = features.shape
    start = pl.multiple_of((me[0] & 1) * half, half)
    high = lax.Precision.HIGHEST
    ones = jnp.ones((targets.shape[0], half), jnp.float32)
    squares = lax.dot_general(ones, features * features, NT, precision=high, preferred_element_type=jnp.float32)
    rest = jnp.zeros((targets.shape[0], mine.shape[1] - 2 * count), jnp.float32)
    for source, out in ((targets, mine), (partner_targets, send)):
        scale = lax.rsqrt(jnp.sum(source[...] * source[...], axis=1, keepdims=True) / PDIM + 1e-06)
        dots = lax.dot_general(
            source[:, pl.ds(start, half)], features, NT, precision=high, preferred_element_type=jnp.float32
        )
        parts = [dots * scale, squares] + ([rest] if rest.shape[1] else [])
        out[...] = jnp.concatenate(parts, axis=1)


def partial_scores(me, targets, partner_targets, kept, arrived):
    shape = jax.ShapeDtypeStruct((targets.shape[0], 128), jnp.float32)
    return pl.pallas_call(
        scores_kernel,
        out_shape=[shape, shape],
        in_specs=[SMEM] + [VMEM] * (3 + len(arrived)),
        out_specs=[VMEM, VMEM],
        compiler_params=pltpu.CompilerParams(vmem_limit_bytes=6 * MIB),
        name="partial_scores",
    )(me, targets, partner_targets, kept, *arrived)


def body(tokens, cotangent, response_loss_mask, adapter_down_weight, projection, targets):
    n = lax.axis_size("shard")
    far = n // NEAR
    me = lax.axis_index("shard").astype(jnp.int32).reshape(1)
    block = adapter_down_weight
    bits = [1 << i for i in range(n.bit_length() - 1)]

    whole = [(tokens, 0, tokens.shape[0]), (cotangent, 0, cotangent.shape[0])]
    whole += [(response_loss_mask.reshape(1, -1), 0, 1), (targets, 0, targets.shape[0])]
    tokens, cotangent, mask, targets = load("load_1", whole, (me,))
    column = [block] + [swap(block, NEAR * d, n) for d in range(1, far)]
    (column,) = join("join_blocks", column, [[(d,) for d in range(far)]], block.shape, (mask,))
    places = [[NEAR * d + k for d in range(far)] for k in range(NEAR)]
    total = partial_lowrank("lowrank_1", me, tokens, [column], places[:1])
    across = hold("hold", swap(column, 2, n), (total,))
    total = partial_lowrank("lowrank_2", me, tokens, [swap(column, 1, n), across], places[1:3], (total,))

    stages = [bits[i : i + 2] for i in range(2, len(bits), 2)] + [bits[:2]]
    left = span([b for stage in stages[1:] for b in stage])
    moves = span(stages[0])
    owners = [[m ^ r for r in left] for m in moves]
    rows = packed_grads(me, owners, tokens, [swap(across, 1, n)], places[3:], total, cotangent, mask)
    rows = list(rows)
    rows[1] = hold("hold_rows", rows[1], (), HIDE)
    arrays = [rows[0]] + [swap(array, m, n) for array, m in zip(rows[1:], moves[1:])]
    held = {(m, r): (a, i) for a, m in enumerate(moves) for i, r in enumerate(left)}
    for number, stage in enumerate(stages[1:]):
        moves, left = span(stage), span([b for later in stages[number + 2 :] for b in later])
        pairs = [[(src, r ^ m) for src in sorted({s for s, _ in held}) for r in left] for m in moves]
        picks = [[held[pair] for pair in group] for group in pairs[1:]]
        sent = join(f"join_rows_{number}", arrays, picks, rows[0].shape[1:])
        kept = {pair: held[pair] for pair in pairs[0]}
        for m, group, array in zip(moves[1:], pairs[1:], sent):
            kept.update({(src ^ m, r ^ m): (len(arrays), i) for i, (src, r) in enumerate(group)})
            arrays.append(swap(array, m, n))
        held = kept
    partner_targets = swap(targets, 1, n)

    places = [held[k, 0] for k in range(n)]
    kept, send = partial_features(me, arrays, places, projection)
    kept = kept + swap(send, 1, n).astype(jnp.float32)
    for stage in [bits[1:3]] + [[bit] for bit in bits[3:]]:
        half = kept.astype(jnp.bfloat16)
        arrived = [swap(half, m, n) for m in span(stage)[1:]]
        if bits[-1] not in stage:
            kept = kept + sum(value.astype(jnp.float32) for value in arrived)
    mine, send = partial_scores(me, targets, partner_targets, kept, arrived)
    total = mine + swap(send, 1, n)
    scale = lax.rsqrt(total[:, n : 2 * n] / PDIM + 1e-06)
    return (total[:, :n] * scale / PDIM).T


def solution(mesh):
    in_specs = (
        P(("groups", "shard"), None),
        P(("groups", "shard"), None),
        P(("groups", "shard")),
        P(None, "shard"),
        P("shard", None),
        P(("groups", "shard"), None),
    )
    out_specs = P("groups", "shard")
    return jax.shard_map(body, mesh=mesh, in_specs=in_specs, out_specs=out_specs, check_vma=False)
```

```python
import functools

import jax
import jax.numpy as jnp
from jax import lax
from jax.experimental import pallas as pl
from jax.experimental.pallas import tpu as pltpu
from jax.sharding import PartitionSpec as P

PDIM = 4096
LENGTH = 256
LANES = 256
NEAR = 4
MIB = 1 << 20
HIDE = 30 * 10**9
NT = (((1,), (1,)), ((), ()))
VMEM = pl.BlockSpec(memory_space=pltpu.VMEM)
SMEM = pl.BlockSpec(memory_space=pltpu.SMEM)
ANY = pl.BlockSpec(memory_space=pl.ANY)


def swap(value, bit, n):
    return lax.ppermute(value, "shard", [(s, s ^ bit) for s in range(n)])


def span(bits):
    sums = [0]
    for bit in bits:
        sums += [k + bit for k in sums]
    return sums


def in_hbm(value):
    return pltpu.with_memory_space_constraint(value, pltpu.HBM)


def in_vmem(value):
    return pltpu.with_memory_space_constraint(value, pltpu.VMEM)


def load_kernel(count, starts, *refs):
    sources, outs, sems = refs[:count], refs[-1 - count : -1], refs[-1]
    copies = []
    for source, start, out in zip(sources, starts, outs):
        rows = out.shape[0]
        step = min(rows, LANES // 2)
        for i in range(0, rows, step):
            part = source.at[pl.ds(start + i, step)]
            copies.append(pltpu.make_async_copy(part, out.at[pl.ds(i, step)], sems.at[len(copies)]))
    for copy in copies:
        copy.start()
    for copy in copies:
        copy.wait()


def load(name, parts, after):
    size = sum(rows * array.size // array.shape[0] * array.dtype.itemsize for array, _, rows in parts)
    pieces = sum(max(rows // (LANES // 2), 1) for _, _, rows in parts)
    return pl.pallas_call(
        functools.partial(load_kernel, len(parts), [start for _, start, _ in parts]),
        out_shape=[pltpu.VMEM((rows,) + array.shape[1:], array.dtype) for array, _, rows in parts],
        in_specs=[ANY] * (len(parts) + len(after)),
        out_specs=[VMEM] * len(parts),
        scratch_shapes=[pltpu.SemaphoreType.DMA((pieces,))],
        compiler_params=pltpu.CompilerParams(vmem_limit_bytes=MIB),
        cost_estimate=pl.CostEstimate(flops=0, bytes_accessed=2 * size, transcendentals=0),
        name=name,
    )(*[in_hbm(array) for array, _, _ in parts], *after)


def hold(name, value, after, flops=0):
    return pl.pallas_call(
        lambda *refs: None,
        out_shape=jax.ShapeDtypeStruct(value.shape, value.dtype),
        in_specs=[ANY] * (1 + len(after)),
        out_specs=ANY,
        input_output_aliases={0: 0},
        compiler_params=pltpu.CompilerParams(vmem_limit_bytes=MIB),
        cost_estimate=pl.CostEstimate(flops=flops, bytes_accessed=2000000, transcendentals=0),
        name=name,
    )(value, *after)


def join_kernel(picks, *refs):
    for pick, out in zip(picks, refs[-len(picks) :]):
        for target, (source, *entry) in enumerate(pick):
            out[target] = refs[source][entry[0]] if entry else refs[source][...]


def join(name, values, picks, shape, after=(), flops=0):
    return pl.pallas_call(
        functools.partial(join_kernel, picks),
        out_shape=[jax.ShapeDtypeStruct((len(pick),) + shape, values[0].dtype) for pick in picks],
        in_specs=[VMEM] * len(values) + [ANY] * len(after),
        out_specs=[VMEM] * len(picks),
        compiler_params=pltpu.CompilerParams(vmem_limit_bytes=2 * MIB),
        cost_estimate=pl.CostEstimate(flops=flops, bytes_accessed=2000000, transcendentals=0),
        name=name,
    )(*values, *after)


def add_lowrank(total, me, blocks, places, tokens):
    for block, owners in zip(blocks, places):
        depth = block.shape[-1]
        for i, k in enumerate(owners):
            start = pl.multiple_of((me[0] ^ k) * depth, depth)
            part = block[i] if len(block.shape) == 3 else block[...]
            total += lax.dot_general(part, tokens[:, pl.ds(start, depth)], NT, preferred_element_type=jnp.float32)
    return total


def lowrank_kernel(places, me, tokens, *refs):
    blocks, out = refs[: len(places)], refs[-1]
    before = refs[len(places)][...] if len(refs) > len(places) + 1 else jnp.zeros(out.shape, jnp.float32)
    out[...] = add_lowrank(before, me, blocks, places, tokens)


def partial_lowrank(name, me, tokens, blocks, places, before=()):
    return pl.pallas_call(
        functools.partial(lowrank_kernel, places),
        out_shape=jax.ShapeDtypeStruct((blocks[0].shape[-2], tokens.shape[0]), jnp.float32),
        in_specs=[SMEM] + [VMEM] * (1 + len(blocks) + len(before)),
        out_specs=VMEM,
        compiler_params=pltpu.CompilerParams(vmem_limit_bytes=2 * MIB),
        cost_estimate=pl.CostEstimate(flops=100000000, bytes_accessed=2000000, transcendentals=0),
        name=name,
    )(me, tokens, *blocks, *before)


def grads_kernel(owners, places, me, tokens, *refs):
    blocks = refs[: len(places)]
    before, cotangent, mask = refs[len(places) : len(places) + 3]
    outs, grads = refs[-1 - len(owners) : -1], refs[-1]
    total = add_lowrank(before[...], me, blocks, places, tokens)
    rank = total.shape[0]
    lowrank = total.astype(jnp.bfloat16) * mask[...].astype(jnp.bfloat16)
    turned = jnp.dot(lowrank, cotangent[...], preferred_element_type=jnp.float32)
    grads[...] = turned.T
    pack = LANES // rank
    share = outs[0].shape[1]
    for out, ks in zip(outs, owners):
        for i, k in enumerate(ks):
            start = pl.multiple_of((me[0] ^ k) * (share * pack), share * pack)
            for q in range(pack):
                rows = grads[pl.ds(start + q, share, stride=pack), :]
                out[i, :, q * rank : (q + 1) * rank] = rows.astype(jnp.bfloat16)


def packed_grads(me, owners, tokens, blocks, places, before, cotangent, mask):
    rank, width = blocks[0].shape[-2], cotangent.shape[1]
    share = width * rank // LANES // sum(len(ks) for ks in owners)
    return pl.pallas_call(
        functools.partial(grads_kernel, owners, places),
        out_shape=[jax.ShapeDtypeStruct((len(ks), share, LANES), jnp.bfloat16) for ks in owners],
        in_specs=[SMEM] + [VMEM] * (len(blocks) + 4),
        out_specs=[VMEM] * len(owners),
        scratch_shapes=[pltpu.VMEM((width, rank), jnp.float32)],
        compiler_params=pltpu.CompilerParams(vmem_limit_bytes=6 * MIB),
        cost_estimate=pl.CostEstimate(flops=100000000, bytes_accessed=2000000, transcendentals=0),
        name="grads",
    )(me, tokens, *blocks, before, cotangent, mask)


def features_kernel(places, count, me, *refs):
    arrays, weights = refs[:count], refs[count]
    keep, send, x, left, total = refs[-5:]
    n = len(places)
    share = arrays[0].shape[1]
    pitch = x.shape[1] // n
    for k, (source, entry) in enumerate(places):
        rows = arrays[source][entry]
        place = pl.multiple_of((me[0] ^ k) * pitch, pitch)
        for h in range(x.shape[0]):
            x[h, pl.ds(place, share), :] = rows[:, h * 128 : (h + 1) * 128].astype(jnp.float32)
    for j in range(share):
        for h in range(x.shape[0]):
            at = j * LANES + h * 128
            left[:, at : at + 128] = x[h, pl.ds(j, n, stride=pitch), :].astype(jnp.bfloat16)
    total[...] = jnp.dot(left[...], weights[...], preferred_element_type=jnp.float32)
    part = keep.shape[1]
    mine = pl.multiple_of((me[0] & 1) * part, part)
    partner = pl.multiple_of((1 - (me[0] & 1)) * part, part)
    keep[...] = total[:, pl.ds(mine, part)]
    send[...] = total[:, pl.ds(partner, part)].astype(jnp.bfloat16)


def partial_features(me, arrays, places, projection):
    n = len(places)
    share = arrays[0].shape[1]
    depth, width = projection.shape
    half = (n, width // 2)
    return pl.pallas_call(
        functools.partial(features_kernel, places, len(arrays)),
        out_shape=[jax.ShapeDtypeStruct(half, jnp.float32), jax.ShapeDtypeStruct(half, jnp.bfloat16)],
        in_specs=[SMEM] + [VMEM] * (len(arrays) + 1),
        out_specs=[VMEM, VMEM],
        scratch_shapes=[
            pltpu.VMEM((LANES // 128, n * max(share, 8), 128), jnp.float32),
            pltpu.VMEM((n, depth), jnp.bfloat16),
            pltpu.VMEM((n, width), jnp.float32),
        ],
        compiler_params=pltpu.CompilerParams(vmem_limit_bytes=4 * MIB),
        cost_estimate=pl.CostEstimate(flops=600000000, bytes_accessed=34000000, transcendentals=0),
        name="features",
    )(me, *arrays, in_vmem(projection))


def scores_kernel(me, targets, partner_targets, kept, *refs):
    mine, send = refs[-2:]
    features = kept[...]
    for arrived in refs[:-2]:
        features += arrived[...].astype(jnp.float32)
    count, half = features.shape
    start = pl.multiple_of((me[0] & 1) * half, half)
    high = lax.Precision.HIGHEST
    ones = jnp.ones((targets.shape[0], half), jnp.float32)
    squares = lax.dot_general(ones, features * features, NT, precision=high, preferred_element_type=jnp.float32)
    rest = jnp.zeros((targets.shape[0], mine.shape[1] - 2 * count), jnp.float32)
    for source, out in ((targets, mine), (partner_targets, send)):
        scale = lax.rsqrt(jnp.sum(source[...] * source[...], axis=1, keepdims=True) / PDIM + 1e-06)
        dots = lax.dot_general(
            source[:, pl.ds(start, half)], features, NT, precision=high, preferred_element_type=jnp.float32
        )
        parts = [dots * scale, squares] + ([rest] if rest.shape[1] else [])
        out[...] = jnp.concatenate(parts, axis=1)


def partial_scores(me, targets, partner_targets, kept, arrived):
    shape = jax.ShapeDtypeStruct((targets.shape[0], 128), jnp.float32)
    return pl.pallas_call(
        scores_kernel,
        out_shape=[shape, shape],
        in_specs=[SMEM] + [VMEM] * (3 + len(arrived)),
        out_specs=[VMEM, VMEM],
        compiler_params=pltpu.CompilerParams(vmem_limit_bytes=6 * MIB),
        name="partial_scores",
    )(me, targets, partner_targets, kept, *arrived)


def body(tokens, cotangent, response_loss_mask, adapter_down_weight, projection, targets):
    n = lax.axis_size("shard")
    far = n // NEAR
    me = lax.axis_index("shard").astype(jnp.int32).reshape(1)
    block = adapter_down_weight
    bits = [1 << i for i in range(n.bit_length() - 1)]

    whole = [(tokens, 0, tokens.shape[0]), (cotangent, 0, cotangent.shape[0])]
    whole += [(response_loss_mask.reshape(1, -1), 0, 1), (targets, 0, targets.shape[0])]
    tokens, cotangent, mask, targets = load("load_1", whole, (me,))
    column = list(load("load_own", [(block, 0, block.shape[0])], (me,)))
    column += [swap(block, NEAR * d, n) for d in range(1, far)]
    cut = far // 2
    picks = [[(i,) for i in range(cut)]]
    (head,) = join("join_head", column[:cut], picks, block.shape)
    (tail,) = join("join_tail", column[cut:], picks, block.shape, (mask, head))
    places = [[[NEAR * d + k for d in half] for half in (range(cut), range(cut, far))] for k in range(NEAR)]
    across = [swap(head, 2, n), swap(tail, 2, n)]
    blocks, owners = [head, tail, swap(head, 1, n), across[0]], places[0] + places[1][:1] + places[2][:1]
    total = partial_lowrank("lowrank_1", me, tokens, blocks, owners)
    picks = [[(a, i) for a in range(3) for i in range(cut)]]
    (gathered,) = join("join_core", [tail] + across, picks, block.shape, (total,))
    other = swap(gathered, 1, n)
    total = partial_lowrank("lowrank_2", me, tokens, across[1:], places[2][1:], (total,))
    owners = [places[1][1] + places[3][0] + places[3][1]]

    stages = [bits[i : i + 2] for i in range(2, len(bits), 2)] + [bits[:2]]
    left = span([b for stage in stages[1:] for b in stage])
    moves = span(stages[0])
    targets_of = [[m ^ r for r in left] for m in moves]
    rows = packed_grads(me, targets_of, tokens, [other], owners, total, cotangent, mask)
    rows = list(rows)
    rows[1] = hold("hold_rows", rows[1], (), HIDE)
    arrays = [rows[0]] + [swap(array, m, n) for array, m in zip(rows[1:], moves[1:])]
    held = {(m, r): (a, i) for a, m in enumerate(moves) for i, r in enumerate(left)}
    for number, stage in enumerate(stages[1:]):
        moves, left = span(stage), span([b for later in stages[number + 2 :] for b in later])
        pairs = [[(src, r ^ m) for src in sorted({s for s, _ in held}) for r in left] for m in moves]
        picks = [[held[pair] for pair in group] for group in pairs[1:]]
        sent = join(f"join_rows_{number}", arrays, picks, rows[0].shape[1:])
        kept = {pair: held[pair] for pair in pairs[0]}
        for m, group, array in zip(moves[1:], pairs[1:], sent):
            kept.update({(src ^ m, r ^ m): (len(arrays), i) for i, (src, r) in enumerate(group)})
            arrays.append(swap(array, m, n))
        held = kept
    partner_targets = swap(targets, 1, n)

    places = [held[k, 0] for k in range(n)]
    kept, send = partial_features(me, arrays, places, projection)
    kept = kept + swap(send, 1, n).astype(jnp.float32)
    for stage in [bits[1:3]] + [[bit] for bit in bits[3:]]:
        half = kept.astype(jnp.bfloat16)
        arrived = [swap(half, m, n) for m in span(stage)[1:]]
        if bits[-1] not in stage:
            kept = kept + sum(value.astype(jnp.float32) for value in arrived)
    mine, send = partial_scores(me, targets, partner_targets, kept, arrived)
    total = mine + swap(send, 1, n)
    scale = lax.rsqrt(total[:, n : 2 * n] / PDIM + 1e-06)
    return (total[:, :n] * scale / PDIM).T


def solution(mesh):
    in_specs = (
        P(("groups", "shard"), None),
        P(("groups", "shard"), None),
        P(("groups", "shard")),
        P(None, "shard"),
        P("shard", None),
        P(("groups", "shard"), None),
    )
    out_specs = P("groups", "shard")
    return jax.shard_map(body, mesh=mesh, in_specs=in_specs, out_specs=out_specs, check_vma=False)
```

```python
import functools

import jax
import jax.numpy as jnp
from jax import lax
from jax.experimental import pallas as pl
from jax.experimental.pallas import tpu as pltpu
from jax.sharding import PartitionSpec as P

PDIM = 4096
LENGTH = 256
LANES = 256
NEAR = 4
MIB = 1 << 20
HIDE = 30 * 10**9
NT = (((1,), (1,)), ((), ()))
VMEM = pl.BlockSpec(memory_space=pltpu.VMEM)
SMEM = pl.BlockSpec(memory_space=pltpu.SMEM)
ANY = pl.BlockSpec(memory_space=pl.ANY)


def swap(value, bit, n):
    return lax.ppermute(value, "shard", [(s, s ^ bit) for s in range(n)])


def span(bits):
    sums = [0]
    for bit in bits:
        sums += [k + bit for k in sums]
    return sums


def in_hbm(value):
    return pltpu.with_memory_space_constraint(value, pltpu.HBM)


def in_vmem(value):
    return pltpu.with_memory_space_constraint(value, pltpu.VMEM)


def load_kernel(count, starts, *refs):
    sources, outs, sems = refs[:count], refs[-1 - count : -1], refs[-1]
    copies = []
    for source, start, out in zip(sources, starts, outs):
        rows = out.shape[0]
        step = min(rows, LANES // 2)
        for i in range(0, rows, step):
            part = source.at[pl.ds(start + i, step)]
            copies.append(pltpu.make_async_copy(part, out.at[pl.ds(i, step)], sems.at[len(copies)]))
    for copy in copies:
        copy.start()
    for copy in copies:
        copy.wait()


def load(name, parts, after):
    size = sum(rows * array.size // array.shape[0] * array.dtype.itemsize for array, _, rows in parts)
    pieces = sum(max(rows // (LANES // 2), 1) for _, _, rows in parts)
    return pl.pallas_call(
        functools.partial(load_kernel, len(parts), [start for _, start, _ in parts]),
        out_shape=[pltpu.VMEM((rows,) + array.shape[1:], array.dtype) for array, _, rows in parts],
        in_specs=[ANY] * (len(parts) + len(after)),
        out_specs=[VMEM] * len(parts),
        scratch_shapes=[pltpu.SemaphoreType.DMA((pieces,))],
        compiler_params=pltpu.CompilerParams(vmem_limit_bytes=MIB),
        cost_estimate=pl.CostEstimate(flops=0, bytes_accessed=2 * size, transcendentals=0),
        name=name,
    )(*[in_hbm(array) for array, _, _ in parts], *after)


def hold(name, value, after, flops=0):
    return pl.pallas_call(
        lambda *refs: None,
        out_shape=jax.ShapeDtypeStruct(value.shape, value.dtype),
        in_specs=[ANY] * (1 + len(after)),
        out_specs=ANY,
        input_output_aliases={0: 0},
        compiler_params=pltpu.CompilerParams(vmem_limit_bytes=MIB),
        cost_estimate=pl.CostEstimate(flops=flops, bytes_accessed=2000000, transcendentals=0),
        name=name,
    )(value, *after)


def join_kernel(picks, *refs):
    for pick, out in zip(picks, refs[-len(picks) :]):
        for target, (source, *entry) in enumerate(pick):
            out[target] = refs[source][entry[0]] if entry else refs[source][...]


def join(name, values, picks, shape, after=(), flops=0):
    return pl.pallas_call(
        functools.partial(join_kernel, picks),
        out_shape=[jax.ShapeDtypeStruct((len(pick),) + shape, values[0].dtype) for pick in picks],
        in_specs=[VMEM] * len(values) + [ANY] * len(after),
        out_specs=[VMEM] * len(picks),
        compiler_params=pltpu.CompilerParams(vmem_limit_bytes=2 * MIB),
        cost_estimate=pl.CostEstimate(flops=flops, bytes_accessed=2000000, transcendentals=0),
        name=name,
    )(*values, *after)


def add_lowrank(total, me, blocks, places, tokens):
    for block, owners in zip(blocks, places):
        depth = block.shape[-1]
        for i, k in enumerate(owners):
            start = pl.multiple_of((me[0] ^ k) * depth, depth)
            part = block[i] if len(block.shape) == 3 else block[...]
            total += lax.dot_general(part, tokens[:, pl.ds(start, depth)], NT, preferred_element_type=jnp.float32)
    return total


def lowrank_kernel(places, me, tokens, *refs):
    blocks, out = refs[: len(places)], refs[-1]
    before = refs[len(places)][...] if len(refs) > len(places) + 1 else jnp.zeros(out.shape, jnp.float32)
    out[...] = add_lowrank(before, me, blocks, places, tokens)


def partial_lowrank(name, me, tokens, blocks, places, before=()):
    return pl.pallas_call(
        functools.partial(lowrank_kernel, places),
        out_shape=jax.ShapeDtypeStruct((blocks[0].shape[-2], tokens.shape[0]), jnp.float32),
        in_specs=[SMEM] + [VMEM] * (1 + len(blocks) + len(before)),
        out_specs=VMEM,
        compiler_params=pltpu.CompilerParams(vmem_limit_bytes=2 * MIB),
        cost_estimate=pl.CostEstimate(flops=100000000, bytes_accessed=2000000, transcendentals=0),
        name=name,
    )(me, tokens, *blocks, *before)


def grads_kernel(owners, places, me, tokens, *refs):
    blocks = refs[: len(places)]
    before, cotangent, mask = refs[len(places) : len(places) + 3]
    outs, grads = refs[-1 - len(owners) : -1], refs[-1]
    total = add_lowrank(before[...], me, blocks, places, tokens)
    rank = total.shape[0]
    lowrank = total.astype(jnp.bfloat16) * mask[...].astype(jnp.bfloat16)
    turned = jnp.dot(lowrank, cotangent[...], preferred_element_type=jnp.float32)
    grads[...] = turned.T
    pack = LANES // rank
    share = outs[0].shape[1]
    for out, ks in zip(outs, owners):
        for i, k in enumerate(ks):
            start = pl.multiple_of((me[0] ^ k) * (share * pack), share * pack)
            for q in range(pack):
                rows = grads[pl.ds(start + q, share, stride=pack), :]
                out[i, :, q * rank : (q + 1) * rank] = rows.astype(jnp.bfloat16)


def packed_grads(me, owners, tokens, blocks, places, before, cotangent, mask):
    rank, width = blocks[0].shape[-2], cotangent.shape[1]
    share = width * rank // LANES // sum(len(ks) for ks in owners)
    return pl.pallas_call(
        functools.partial(grads_kernel, owners, places),
        out_shape=[jax.ShapeDtypeStruct((len(ks), share, LANES), jnp.bfloat16) for ks in owners],
        in_specs=[SMEM] + [VMEM] * (len(blocks) + 4),
        out_specs=[VMEM] * len(owners),
        scratch_shapes=[pltpu.VMEM((width, rank), jnp.float32)],
        compiler_params=pltpu.CompilerParams(vmem_limit_bytes=6 * MIB),
        cost_estimate=pl.CostEstimate(flops=100000000, bytes_accessed=2000000, transcendentals=0),
        name="grads",
    )(me, tokens, *blocks, before, cotangent, mask)


def features_kernel(places, count, me, *refs):
    arrays, weights = refs[:count], refs[count]
    keep, send, x, left, total = refs[-5:]
    n = len(places)
    share = arrays[0].shape[1]
    pitch = x.shape[1] // n
    for k, (source, entry) in enumerate(places):
        rows = arrays[source][entry]
        place = pl.multiple_of((me[0] ^ k) * pitch, pitch)
        for h in range(x.shape[0]):
            x[h, pl.ds(place, share), :] = rows[:, h * 128 : (h + 1) * 128].astype(jnp.float32)
    for j in range(share):
        for h in range(x.shape[0]):
            at = j * LANES + h * 128
            left[:, at : at + 128] = x[h, pl.ds(j, n, stride=pitch), :].astype(jnp.bfloat16)
    total[...] = jnp.dot(left[...], weights[...], preferred_element_type=jnp.float32)
    part = keep.shape[1]
    mine = pl.multiple_of((me[0] & 1) * part, part)
    partner = pl.multiple_of((1 - (me[0] & 1)) * part, part)
    keep[...] = total[:, pl.ds(mine, part)]
    send[...] = total[:, pl.ds(partner, part)].astype(jnp.bfloat16)


def partial_features(me, arrays, places, projection):
    n = len(places)
    share = arrays[0].shape[1]
    depth, width = projection.shape
    half = (n, width // 2)
    return pl.pallas_call(
        functools.partial(features_kernel, places, len(arrays)),
        out_shape=[jax.ShapeDtypeStruct(half, jnp.float32), jax.ShapeDtypeStruct(half, jnp.bfloat16)],
        in_specs=[SMEM] + [VMEM] * (len(arrays) + 1),
        out_specs=[VMEM, VMEM],
        scratch_shapes=[
            pltpu.VMEM((LANES // 128, n * max(share, 8), 128), jnp.float32),
            pltpu.VMEM((n, depth), jnp.bfloat16),
            pltpu.VMEM((n, width), jnp.float32),
        ],
        compiler_params=pltpu.CompilerParams(vmem_limit_bytes=4 * MIB),
        cost_estimate=pl.CostEstimate(flops=600000000, bytes_accessed=34000000, transcendentals=0),
        name="features",
    )(me, *arrays, in_vmem(projection))


def scores_kernel(me, targets, partner_targets, kept, *refs):
    mine, send = refs[-2:]
    features = kept[...]
    for arrived in refs[:-2]:
        features += arrived[...].astype(jnp.float32)
    count, half = features.shape
    start = pl.multiple_of((me[0] & 1) * half, half)
    high = lax.Precision.HIGHEST
    ones = jnp.ones((targets.shape[0], half), jnp.float32)
    squares = lax.dot_general(ones, features * features, NT, precision=high, preferred_element_type=jnp.float32)
    rest = jnp.zeros((targets.shape[0], mine.shape[1] - 2 * count), jnp.float32)
    for source, out in ((targets, mine), (partner_targets, send)):
        scale = lax.rsqrt(jnp.sum(source[...] * source[...], axis=1, keepdims=True) / PDIM + 1e-06)
        dots = lax.dot_general(
            source[:, pl.ds(start, half)], features, NT, precision=high, preferred_element_type=jnp.float32
        )
        parts = [dots * scale, squares] + ([rest] if rest.shape[1] else [])
        out[...] = jnp.concatenate(parts, axis=1)


def partial_scores(me, targets, partner_targets, kept, arrived):
    shape = jax.ShapeDtypeStruct((targets.shape[0], 128), jnp.float32)
    return pl.pallas_call(
        scores_kernel,
        out_shape=[shape, shape],
        in_specs=[SMEM] + [VMEM] * (3 + len(arrived)),
        out_specs=[VMEM, VMEM],
        compiler_params=pltpu.CompilerParams(vmem_limit_bytes=6 * MIB),
        name="partial_scores",
    )(me, targets, partner_targets, kept, *arrived)


def body(tokens, cotangent, response_loss_mask, adapter_down_weight, projection, targets):
    n = lax.axis_size("shard")
    far = n // NEAR
    me = lax.axis_index("shard").astype(jnp.int32).reshape(1)
    block = adapter_down_weight
    bits = [1 << i for i in range(n.bit_length() - 1)]

    whole = [(tokens, 0, tokens.shape[0]), (cotangent, 0, cotangent.shape[0])]
    whole += [(response_loss_mask.reshape(1, -1), 0, 1), (targets, 0, targets.shape[0])]
    whole += [(block, 0, block.shape[0])]
    tokens, cotangent, mask, targets, own = load("load_1", whole, (me,))
    cut = far // 2
    column = [own] + [swap(block, NEAR * d, n) for d in range(1, cut + 1)]
    head, farthest = join("join_head", column, [[(i,) for i in range(cut + 1)], [(cut,)]], block.shape)
    far_blocks = [swap(farthest, NEAR * r, n) for r in range(1, cut)]
    picks = [[(i, 0) for i in range(cut - 1)], [(cut - 1, i) for i in range(cut + 1)]]
    tail, again = join("join_tail", far_blocks + [head], picks, block.shape)
    across = [swap(head, 2, n), swap(tail, 2, n)]
    halves = [range(cut + 1), range(cut + 1, far)]
    places = [[[NEAR * d + k for d in half] for half in halves] for k in range(NEAR)]
    blocks, owners = [head, tail, swap(again, 1, n), across[0]], places[0] + places[1][:1] + places[2][:1]
    total = partial_lowrank("lowrank_1", me, tokens, blocks, owners)
    pick = [(a, i) for a, half in ((0, halves[1]), (1, halves[0]), (2, halves[1])) for i in range(len(half))]
    (gathered,) = join("join_core", [tail] + across, [pick], block.shape, (total,))
    other = swap(gathered, 1, n)
    total = partial_lowrank("lowrank_2", me, tokens, across[1:], places[2][1:], (total,))
    owners = [places[1][1] + places[3][0] + places[3][1]]

    stages = [bits[i : i + 2] for i in range(2, len(bits), 2)] + [bits[:2]]
    left = span([b for stage in stages[1:] for b in stage])
    moves = span(stages[0])
    targets_of = [[m ^ r for r in left] for m in moves]
    rows = packed_grads(me, targets_of, tokens, [other], owners, total, cotangent, mask)
    rows = list(rows)
    rows[1] = hold("hold_rows", rows[1], (), HIDE)
    arrays = [rows[0]] + [swap(array, m, n) for array, m in zip(rows[1:], moves[1:])]
    held = {(m, r): (a, i) for a, m in enumerate(moves) for i, r in enumerate(left)}
    for number, stage in enumerate(stages[1:]):
        moves, left = span(stage), span([b for later in stages[number + 2 :] for b in later])
        pairs = [[(src, r ^ m) for src in sorted({s for s, _ in held}) for r in left] for m in moves]
        picks = [[held[pair] for pair in group] for group in pairs[1:]]
        sent = join(f"join_rows_{number}", arrays, picks, rows[0].shape[1:])
        kept = {pair: held[pair] for pair in pairs[0]}
        for m, group, array in zip(moves[1:], pairs[1:], sent):
            kept.update({(src ^ m, r ^ m): (len(arrays), i) for i, (src, r) in enumerate(group)})
            arrays.append(swap(array, m, n))
        held = kept
    partner_targets = swap(targets, 1, n)

    places = [held[k, 0] for k in range(n)]
    kept, send = partial_features(me, arrays, places, projection)
    kept = kept + swap(send, 1, n).astype(jnp.float32)
    for stage in [bits[1:3]] + [[bit] for bit in bits[3:]]:
        half = kept.astype(jnp.bfloat16)
        arrived = [swap(half, m, n) for m in span(stage)[1:]]
        if bits[-1] not in stage:
            kept = kept + sum(value.astype(jnp.float32) for value in arrived)
    mine, send = partial_scores(me, targets, partner_targets, kept, arrived)
    total = mine + swap(send, 1, n)
    scale = lax.rsqrt(total[:, n : 2 * n] / PDIM + 1e-06)
    return (total[:, :n] * scale / PDIM).T


def solution(mesh):
    in_specs = (
        P(("groups", "shard"), None),
        P(("groups", "shard"), None),
        P(("groups", "shard")),
        P(None, "shard"),
        P("shard", None),
        P(("groups", "shard"), None),
    )
    out_specs = P("groups", "shard")
    return jax.shard_map(body, mesh=mesh, in_specs=in_specs, out_specs=out_specs, check_vma=False)
```

```python
import functools

import jax
import jax.numpy as jnp
from jax import lax
from jax.experimental import pallas as pl
from jax.experimental.pallas import tpu as pltpu
from jax.sharding import PartitionSpec as P

PDIM = 4096
LENGTH = 256
LANES = 256
NEAR = 4
MIB = 1 << 20
HIDE = 30 * 10**9
NT = (((1,), (1,)), ((), ()))
VMEM = pl.BlockSpec(memory_space=pltpu.VMEM)
SMEM = pl.BlockSpec(memory_space=pltpu.SMEM)
ANY = pl.BlockSpec(memory_space=pl.ANY)


def swap(value, bit, n):
    return lax.ppermute(value, "shard", [(s, s ^ bit) for s in range(n)])


def span(bits):
    sums = [0]
    for bit in bits:
        sums += [k + bit for k in sums]
    return sums


def in_hbm(value):
    return pltpu.with_memory_space_constraint(value, pltpu.HBM)


def in_vmem(value):
    return pltpu.with_memory_space_constraint(value, pltpu.VMEM)


def load_kernel(count, starts, *refs):
    sources, outs, sems = refs[:count], refs[-1 - count : -1], refs[-1]
    copies = []
    for source, start, out in zip(sources, starts, outs):
        rows = out.shape[0]
        step = min(rows, LANES // 2)
        for i in range(0, rows, step):
            part = source.at[pl.ds(start + i, step)]
            copies.append(pltpu.make_async_copy(part, out.at[pl.ds(i, step)], sems.at[len(copies)]))
    for copy in copies:
        copy.start()
    for copy in copies:
        copy.wait()


def load(name, parts, after):
    size = sum(rows * array.size // array.shape[0] * array.dtype.itemsize for array, _, rows in parts)
    pieces = sum(max(rows // (LANES // 2), 1) for _, _, rows in parts)
    return pl.pallas_call(
        functools.partial(load_kernel, len(parts), [start for _, start, _ in parts]),
        out_shape=[pltpu.VMEM((rows,) + array.shape[1:], array.dtype) for array, _, rows in parts],
        in_specs=[ANY] * (len(parts) + len(after)),
        out_specs=[VMEM] * len(parts),
        scratch_shapes=[pltpu.SemaphoreType.DMA((pieces,))],
        compiler_params=pltpu.CompilerParams(vmem_limit_bytes=MIB),
        cost_estimate=pl.CostEstimate(flops=0, bytes_accessed=2 * size, transcendentals=0),
        name=name,
    )(*[in_hbm(array) for array, _, _ in parts], *after)


def hold(name, value, after, flops=0):
    return pl.pallas_call(
        lambda *refs: None,
        out_shape=jax.ShapeDtypeStruct(value.shape, value.dtype),
        in_specs=[ANY] * (1 + len(after)),
        out_specs=ANY,
        input_output_aliases={0: 0},
        compiler_params=pltpu.CompilerParams(vmem_limit_bytes=MIB),
        cost_estimate=pl.CostEstimate(flops=flops, bytes_accessed=2000000, transcendentals=0),
        name=name,
    )(value, *after)


def join_kernel(picks, *refs):
    for pick, out in zip(picks, refs[-len(picks) :]):
        for target, (source, *entry) in enumerate(pick):
            out[target] = refs[source][entry[0]] if entry else refs[source][...]


def join(name, values, picks, shape, after=(), flops=0):
    return pl.pallas_call(
        functools.partial(join_kernel, picks),
        out_shape=[jax.ShapeDtypeStruct((len(pick),) + shape, values[0].dtype) for pick in picks],
        in_specs=[VMEM] * len(values) + [ANY] * len(after),
        out_specs=[VMEM] * len(picks),
        compiler_params=pltpu.CompilerParams(vmem_limit_bytes=2 * MIB),
        cost_estimate=pl.CostEstimate(flops=flops, bytes_accessed=2000000, transcendentals=0),
        name=name,
    )(*values, *after)


def add_lowrank(total, me, blocks, places, tokens):
    for block, owners in zip(blocks, places):
        depth = block.shape[-1]
        for i, k in enumerate(owners):
            start = pl.multiple_of((me[0] ^ k) * depth, depth)
            part = block[i] if len(block.shape) == 3 else block[...]
            total += lax.dot_general(part, tokens[:, pl.ds(start, depth)], NT, preferred_element_type=jnp.float32)
    return total


def lowrank_kernel(places, me, tokens, *refs):
    blocks, out = refs[: len(places)], refs[-1]
    before = refs[len(places)][...] if len(refs) > len(places) + 1 else jnp.zeros(out.shape, jnp.float32)
    out[...] = add_lowrank(before, me, blocks, places, tokens)


def partial_lowrank(name, me, tokens, blocks, places, before=()):
    return pl.pallas_call(
        functools.partial(lowrank_kernel, places),
        out_shape=jax.ShapeDtypeStruct((blocks[0].shape[-2], tokens.shape[0]), jnp.float32),
        in_specs=[SMEM] + [VMEM] * (1 + len(blocks) + len(before)),
        out_specs=VMEM,
        compiler_params=pltpu.CompilerParams(vmem_limit_bytes=2 * MIB),
        cost_estimate=pl.CostEstimate(flops=100000000, bytes_accessed=2000000, transcendentals=0),
        name=name,
    )(me, tokens, *blocks, *before)


def grads_kernel(owners, places, me, tokens, *refs):
    blocks = refs[: len(places)]
    before, cotangent, mask = refs[len(places) : len(places) + 3]
    outs, grads = refs[-1 - len(owners) : -1], refs[-1]
    total = add_lowrank(before[...], me, blocks, places, tokens)
    rank = total.shape[0]
    lowrank = total.astype(jnp.bfloat16) * mask[...].astype(jnp.bfloat16)
    turned = jnp.dot(lowrank, cotangent[...], preferred_element_type=jnp.float32)
    grads[...] = turned.T
    pack = LANES // rank
    share = outs[0].shape[1]
    for out, ks in zip(outs, owners):
        for i, k in enumerate(ks):
            start = pl.multiple_of((me[0] ^ k) * (share * pack), share * pack)
            for q in range(pack):
                rows = grads[pl.ds(start + q, share, stride=pack), :]
                out[i, :, q * rank : (q + 1) * rank] = rows.astype(jnp.bfloat16)


def packed_grads(me, owners, tokens, blocks, places, before, cotangent, mask):
    rank, width = blocks[0].shape[-2], cotangent.shape[1]
    share = width * rank // LANES // sum(len(ks) for ks in owners)
    return pl.pallas_call(
        functools.partial(grads_kernel, owners, places),
        out_shape=[jax.ShapeDtypeStruct((len(ks), share, LANES), jnp.bfloat16) for ks in owners],
        in_specs=[SMEM] + [VMEM] * (len(blocks) + 4),
        out_specs=[VMEM] * len(owners),
        scratch_shapes=[pltpu.VMEM((width, rank), jnp.float32)],
        compiler_params=pltpu.CompilerParams(vmem_limit_bytes=6 * MIB),
        cost_estimate=pl.CostEstimate(flops=100000000, bytes_accessed=2000000, transcendentals=0),
        name="grads",
    )(me, tokens, *blocks, before, cotangent, mask)


def features_kernel(places, count, me, *refs):
    arrays, weights = refs[:count], refs[count]
    keep, send, x, left, total = refs[-5:]
    n = len(places)
    share = arrays[0].shape[1]
    pitch = x.shape[1] // n
    for k, (source, entry) in enumerate(places):
        rows = arrays[source][entry]
        place = pl.multiple_of((me[0] ^ k) * pitch, pitch)
        for h in range(x.shape[0]):
            x[h, pl.ds(place, share), :] = rows[:, h * 128 : (h + 1) * 128].astype(jnp.float32)
    for j in range(share):
        for h in range(x.shape[0]):
            at = j * LANES + h * 128
            left[:, at : at + 128] = x[h, pl.ds(j, n, stride=pitch), :].astype(jnp.bfloat16)
    total[...] = jnp.dot(left[...], weights[...], preferred_element_type=jnp.float32)
    part = keep.shape[1]
    mine = pl.multiple_of((me[0] & 1) * part, part)
    partner = pl.multiple_of((1 - (me[0] & 1)) * part, part)
    keep[...] = total[:, pl.ds(mine, part)]
    send[...] = total[:, pl.ds(partner, part)].astype(jnp.bfloat16)


def partial_features(me, arrays, places, projection, after):
    n = len(places)
    share = arrays[0].shape[1]
    depth, width = projection.shape
    half = (n, width // 2)
    return pl.pallas_call(
        functools.partial(features_kernel, places, len(arrays)),
        out_shape=[jax.ShapeDtypeStruct(half, jnp.float32), jax.ShapeDtypeStruct(half, jnp.bfloat16)],
        in_specs=[SMEM] + [VMEM] * (len(arrays) + 1) + [ANY],
        out_specs=[VMEM, VMEM],
        scratch_shapes=[
            pltpu.VMEM((LANES // 128, n * max(share, 8), 128), jnp.float32),
            pltpu.VMEM((n, depth), jnp.bfloat16),
            pltpu.VMEM((n, width), jnp.float32),
        ],
        compiler_params=pltpu.CompilerParams(vmem_limit_bytes=4 * MIB),
        cost_estimate=pl.CostEstimate(flops=600000000, bytes_accessed=34000000, transcendentals=0),
        name="features",
    )(me, *arrays, in_vmem(projection), after)


def scores_kernel(me, targets, partner_targets, kept, *refs):
    mine, send = refs[-2:]
    features = kept[...]
    for arrived in refs[:-2]:
        features += arrived[...].astype(jnp.float32)
    count, half = features.shape
    start = pl.multiple_of((me[0] & 1) * half, half)
    high = lax.Precision.HIGHEST
    ones = jnp.ones((targets.shape[0], half), jnp.float32)
    squares = lax.dot_general(ones, features * features, NT, precision=high, preferred_element_type=jnp.float32)
    rest = jnp.zeros((targets.shape[0], mine.shape[1] - 2 * count), jnp.float32)
    for source, out in ((targets, mine), (partner_targets, send)):
        scale = lax.rsqrt(jnp.sum(source[...] * source[...], axis=1, keepdims=True) / PDIM + 1e-06)
        dots = lax.dot_general(
            source[:, pl.ds(start, half)], features, NT, precision=high, preferred_element_type=jnp.float32
        )
        parts = [dots * scale, squares] + ([rest] if rest.shape[1] else [])
        out[...] = jnp.concatenate(parts, axis=1)


def partial_scores(me, targets, partner_targets, kept, arrived):
    shape = jax.ShapeDtypeStruct((targets.shape[0], 128), jnp.float32)
    return pl.pallas_call(
        scores_kernel,
        out_shape=[shape, shape],
        in_specs=[SMEM] + [VMEM] * (3 + len(arrived)),
        out_specs=[VMEM, VMEM],
        compiler_params=pltpu.CompilerParams(vmem_limit_bytes=6 * MIB),
        name="partial_scores",
    )(me, targets, partner_targets, kept, *arrived)


def body(tokens, cotangent, response_loss_mask, adapter_down_weight, projection, targets):
    n = lax.axis_size("shard")
    far = n // NEAR
    me = lax.axis_index("shard").astype(jnp.int32).reshape(1)
    block = adapter_down_weight
    bits = [1 << i for i in range(n.bit_length() - 1)]

    whole = [(tokens, 0, tokens.shape[0]), (cotangent, 0, cotangent.shape[0])]
    whole += [(response_loss_mask.reshape(1, -1), 0, 1), (targets, 0, targets.shape[0])]
    tokens, cotangent, mask, targets = load("load_1", whole, (me,))
    cut = far // 2
    column = [block] + [swap(block, NEAR * d, n) for d in range(1, far)]
    across = [swap(value, 2, n) for value in column]
    places = [[[NEAR * d + k] for d in range(far)] for k in range(NEAR)]
    blocks, owners = column + across[:cut], places[0] + places[2][:cut]
    total = partial_lowrank("lowrank_1", me, tokens, blocks, owners)
    picks = [[(i,) for i in range(2 * far)]]
    (gathered,) = join("join_core", column + across, picks, block.shape, (total,))
    other = swap(gathered, 1, n)
    total = partial_lowrank("lowrank_2", me, tokens, across[cut:], places[2][cut:], (total,))
    owners = [[k + 1 for part in places[0] + places[2] for k in part]]

    stages = [bits[i : i + 2] for i in range(2, len(bits), 2)] + [bits[:2]]
    left = span([b for stage in stages[1:] for b in stage])
    moves = span(stages[0])
    targets_of = [[m ^ r for r in left] for m in moves]
    rows = packed_grads(me, targets_of, tokens, [other], owners, total, cotangent, mask)
    rows = list(rows)
    rows[1] = hold("hold_rows", rows[1], (), HIDE)
    arrays = [rows[0]] + [swap(array, m, n) for array, m in zip(rows[1:], moves[1:])]
    held = {(m, r): (a, i) for a, m in enumerate(moves) for i, r in enumerate(left)}
    for number, stage in enumerate(stages[1:]):
        moves, left = span(stage), span([b for later in stages[number + 2 :] for b in later])
        pairs = [[(src, r ^ m) for src in sorted({s for s, _ in held}) for r in left] for m in moves]
        picks = [[held[pair] for pair in group] for group in pairs[1:]]
        sent = join(f"join_rows_{number}", arrays, picks, rows[0].shape[1:])
        kept = {pair: held[pair] for pair in pairs[0]}
        for m, group, array in zip(moves[1:], pairs[1:], sent):
            kept.update({(src ^ m, r ^ m): (len(arrays), i) for i, (src, r) in enumerate(group)})
            arrays.append(swap(array, m, n))
        held = kept

    places = [held[k, 0] for k in range(n)]
    partner_targets = swap(targets, 1, n)
    kept, send = partial_features(me, arrays, places, projection, partner_targets)
    kept = kept + swap(send, 1, n).astype(jnp.float32)
    for stage in [bits[1:3]] + [[bit] for bit in bits[3:]]:
        half = kept.astype(jnp.bfloat16)
        arrived = [swap(half, m, n) for m in span(stage)[1:]]
        if bits[-1] not in stage:
            kept = kept + sum(value.astype(jnp.float32) for value in arrived)
    mine, send = partial_scores(me, targets, partner_targets, kept, arrived)
    total = mine + swap(send, 1, n)
    scale = lax.rsqrt(total[:, n : 2 * n] / PDIM + 1e-06)
    return (total[:, :n] * scale / PDIM).T


def solution(mesh):
    in_specs = (
        P(("groups", "shard"), None),
        P(("groups", "shard"), None),
        P(("groups", "shard")),
        P(None, "shard"),
        P("shard", None),
        P(("groups", "shard"), None),
    )
    out_specs = P("groups", "shard")
    return jax.shard_map(body, mesh=mesh, in_specs=in_specs, out_specs=out_specs, check_vma=False)
```

```python
import functools

import jax
import jax.numpy as jnp
from jax import lax
from jax.experimental import pallas as pl
from jax.experimental.pallas import tpu as pltpu
from jax.sharding import PartitionSpec as P

PDIM = 4096
LENGTH = 256
LANES = 256
NEAR = 4
MIB = 1 << 20
HIDE = 30 * 10**9
NT = (((1,), (1,)), ((), ()))
VMEM = pl.BlockSpec(memory_space=pltpu.VMEM)
SMEM = pl.BlockSpec(memory_space=pltpu.SMEM)
ANY = pl.BlockSpec(memory_space=pl.ANY)


def swap(value, bit, n):
    return lax.ppermute(value, "shard", [(s, s ^ bit) for s in range(n)])


def span(bits):
    sums = [0]
    for bit in bits:
        sums += [k + bit for k in sums]
    return sums


def in_hbm(value):
    return pltpu.with_memory_space_constraint(value, pltpu.HBM)


def in_vmem(value):
    return pltpu.with_memory_space_constraint(value, pltpu.VMEM)


def load_kernel(count, starts, *refs):
    sources, outs, sems = refs[:count], refs[-1 - count : -1], refs[-1]
    copies = []
    for source, start, out in zip(sources, starts, outs):
        rows = out.shape[0]
        step = min(rows, LANES // 2)
        for i in range(0, rows, step):
            part = source.at[pl.ds(start + i, step)]
            copies.append(pltpu.make_async_copy(part, out.at[pl.ds(i, step)], sems.at[len(copies)]))
    for copy in copies:
        copy.start()
    for copy in copies:
        copy.wait()


def load(name, parts, after):
    size = sum(rows * array.size // array.shape[0] * array.dtype.itemsize for array, _, rows in parts)
    pieces = sum(max(rows // (LANES // 2), 1) for _, _, rows in parts)
    return pl.pallas_call(
        functools.partial(load_kernel, len(parts), [start for _, start, _ in parts]),
        out_shape=[pltpu.VMEM((rows,) + array.shape[1:], array.dtype) for array, _, rows in parts],
        in_specs=[ANY] * (len(parts) + len(after)),
        out_specs=[VMEM] * len(parts),
        scratch_shapes=[pltpu.SemaphoreType.DMA((pieces,))],
        compiler_params=pltpu.CompilerParams(vmem_limit_bytes=MIB),
        cost_estimate=pl.CostEstimate(flops=0, bytes_accessed=2 * size, transcendentals=0),
        name=name,
    )(*[in_hbm(array) for array, _, _ in parts], *after)


def hold(name, value, after, flops=0):
    return pl.pallas_call(
        lambda *refs: None,
        out_shape=jax.ShapeDtypeStruct(value.shape, value.dtype),
        in_specs=[ANY] * (1 + len(after)),
        out_specs=ANY,
        input_output_aliases={0: 0},
        compiler_params=pltpu.CompilerParams(vmem_limit_bytes=MIB),
        cost_estimate=pl.CostEstimate(flops=flops, bytes_accessed=2000000, transcendentals=0),
        name=name,
    )(value, *after)


def join_kernel(picks, *refs):
    for pick, out in zip(picks, refs[-len(picks) :]):
        for target, (source, *entry) in enumerate(pick):
            out[target] = refs[source][entry[0]] if entry else refs[source][...]


def join(name, values, picks, shape, after=(), flops=0):
    return pl.pallas_call(
        functools.partial(join_kernel, picks),
        out_shape=[jax.ShapeDtypeStruct((len(pick),) + shape, values[0].dtype) for pick in picks],
        in_specs=[VMEM] * len(values) + [ANY] * len(after),
        out_specs=[VMEM] * len(picks),
        compiler_params=pltpu.CompilerParams(vmem_limit_bytes=2 * MIB),
        cost_estimate=pl.CostEstimate(flops=flops, bytes_accessed=2000000, transcendentals=0),
        name=name,
    )(*values, *after)


def add_lowrank(total, me, blocks, places, tokens):
    for block, owners in zip(blocks, places):
        depth = block.shape[-1]
        for i, k in enumerate(owners):
            start = pl.multiple_of((me[0] ^ k) * depth, depth)
            part = block[i] if len(block.shape) == 3 else block[...]
            total += lax.dot_general(part, tokens[:, pl.ds(start, depth)], NT, preferred_element_type=jnp.float32)
    return total


def lowrank_kernel(places, me, tokens, *refs):
    blocks, out = refs[: len(places)], refs[-1]
    before = refs[len(places)][...] if len(refs) > len(places) + 1 else jnp.zeros(out.shape, jnp.float32)
    out[...] = add_lowrank(before, me, blocks, places, tokens)


def partial_lowrank(name, me, tokens, blocks, places, before=()):
    return pl.pallas_call(
        functools.partial(lowrank_kernel, places),
        out_shape=jax.ShapeDtypeStruct((blocks[0].shape[-2], tokens.shape[0]), jnp.float32),
        in_specs=[SMEM] + [VMEM] * (1 + len(blocks) + len(before)),
        out_specs=VMEM,
        compiler_params=pltpu.CompilerParams(vmem_limit_bytes=2 * MIB),
        cost_estimate=pl.CostEstimate(flops=100000000, bytes_accessed=2000000, transcendentals=0),
        name=name,
    )(me, tokens, *blocks, *before)


def grads_kernel(owners, places, me, tokens, *refs):
    blocks = refs[: len(places)]
    before, cotangent, mask = refs[len(places) : len(places) + 3]
    outs, grads = refs[-1 - len(owners) : -1], refs[-1]
    total = add_lowrank(before[...], me, blocks, places, tokens)
    rank = total.shape[0]
    lowrank = total.astype(jnp.bfloat16) * mask[...].astype(jnp.bfloat16)
    turned = jnp.dot(lowrank, cotangent[...], preferred_element_type=jnp.float32)
    grads[...] = turned.T
    pack = LANES // rank
    share = outs[0].shape[1]
    for out, ks in zip(outs, owners):
        for i, k in enumerate(ks):
            start = pl.multiple_of((me[0] ^ k) * (share * pack), share * pack)
            for q in range(pack):
                rows = grads[pl.ds(start + q, share, stride=pack), :]
                out[i, :, q * rank : (q + 1) * rank] = rows.astype(jnp.bfloat16)


def packed_grads(me, owners, tokens, blocks, places, before, cotangent, mask):
    rank, width = blocks[0].shape[-2], cotangent.shape[1]
    share = width * rank // LANES // sum(len(ks) for ks in owners)
    return pl.pallas_call(
        functools.partial(grads_kernel, owners, places),
        out_shape=[jax.ShapeDtypeStruct((len(ks), share, LANES), jnp.bfloat16) for ks in owners],
        in_specs=[SMEM] + [VMEM] * (len(blocks) + 4),
        out_specs=[VMEM] * len(owners),
        scratch_shapes=[pltpu.VMEM((width, rank), jnp.float32)],
        compiler_params=pltpu.CompilerParams(vmem_limit_bytes=6 * MIB),
        cost_estimate=pl.CostEstimate(flops=100000000, bytes_accessed=2000000, transcendentals=0),
        name="grads",
    )(me, tokens, *blocks, before, cotangent, mask)


def features_kernel(places, count, me, *refs):
    arrays, weights = refs[:count], refs[count]
    keep, send, x, left, total = refs[-5:]
    n = len(places)
    share = arrays[0].shape[1]
    pitch = x.shape[1] // n
    for k, (source, entry) in enumerate(places):
        rows = arrays[source][entry]
        place = pl.multiple_of((me[0] ^ k) * pitch, pitch)
        for h in range(x.shape[0]):
            x[h, pl.ds(place, share), :] = rows[:, h * 128 : (h + 1) * 128].astype(jnp.float32)
    for j in range(share):
        for h in range(x.shape[0]):
            at = j * LANES + h * 128
            left[:, at : at + 128] = x[h, pl.ds(j, n, stride=pitch), :].astype(jnp.bfloat16)
    total[...] = jnp.dot(left[...], weights[...], preferred_element_type=jnp.float32)
    part = keep.shape[1]
    mine = pl.multiple_of((me[0] & 1) * part, part)
    partner = pl.multiple_of((1 - (me[0] & 1)) * part, part)
    keep[...] = total[:, pl.ds(mine, part)]
    send[...] = total[:, pl.ds(partner, part)].astype(jnp.bfloat16)


def partial_features(me, arrays, places, projection, after):
    n = len(places)
    share = arrays[0].shape[1]
    depth, width = projection.shape
    half = (n, width // 2)
    return pl.pallas_call(
        functools.partial(features_kernel, places, len(arrays)),
        out_shape=[jax.ShapeDtypeStruct(half, jnp.float32), jax.ShapeDtypeStruct(half, jnp.bfloat16)],
        in_specs=[SMEM] + [VMEM] * (len(arrays) + 1) + [ANY],
        out_specs=[VMEM, VMEM],
        scratch_shapes=[
            pltpu.VMEM((LANES // 128, n * max(share, 8), 128), jnp.float32),
            pltpu.VMEM((n, depth), jnp.bfloat16),
            pltpu.VMEM((n, width), jnp.float32),
        ],
        compiler_params=pltpu.CompilerParams(vmem_limit_bytes=4 * MIB),
        cost_estimate=pl.CostEstimate(flops=600000000, bytes_accessed=34000000, transcendentals=0),
        name="features",
    )(me, *arrays, in_vmem(projection), after)


def scores_kernel(me, targets, partner_targets, kept, *refs):
    mine, send = refs[-2:]
    features = kept[...]
    for arrived in refs[:-2]:
        features += arrived[...].astype(jnp.float32)
    count, half = features.shape
    start = pl.multiple_of((me[0] & 1) * half, half)
    high = lax.Precision.HIGHEST
    ones = jnp.ones((targets.shape[0], half), jnp.float32)
    squares = lax.dot_general(ones, features * features, NT, precision=high, preferred_element_type=jnp.float32)
    rest = jnp.zeros((targets.shape[0], mine.shape[1] - 2 * count), jnp.float32)
    for source, out in ((targets, mine), (partner_targets, send)):
        scale = lax.rsqrt(jnp.sum(source[...] * source[...], axis=1, keepdims=True) / PDIM + 1e-06)
        dots = lax.dot_general(
            source[:, pl.ds(start, half)], features, NT, precision=high, preferred_element_type=jnp.float32
        )
        parts = [dots * scale, squares] + ([rest] if rest.shape[1] else [])
        out[...] = jnp.concatenate(parts, axis=1)


def partial_scores(me, targets, partner_targets, kept, arrived):
    shape = jax.ShapeDtypeStruct((targets.shape[0], 128), jnp.float32)
    return pl.pallas_call(
        scores_kernel,
        out_shape=[shape, shape],
        in_specs=[SMEM] + [VMEM] * (3 + len(arrived)),
        out_specs=[VMEM, VMEM],
        compiler_params=pltpu.CompilerParams(vmem_limit_bytes=6 * MIB),
        name="partial_scores",
    )(me, targets, partner_targets, kept, *arrived)


def body(tokens, cotangent, response_loss_mask, adapter_down_weight, projection, targets):
    n = lax.axis_size("shard")
    far = n // NEAR
    me = lax.axis_index("shard").astype(jnp.int32).reshape(1)
    block = adapter_down_weight
    bits = [1 << i for i in range(n.bit_length() - 1)]

    whole = [(tokens, 0, tokens.shape[0]), (cotangent, 0, cotangent.shape[0])]
    whole += [(response_loss_mask.reshape(1, -1), 0, 1), (targets, 0, targets.shape[0])]
    tokens, cotangent, mask, targets = load("load_1", whole, (me,))
    cut = far // 2
    column = [block] + [swap(block, NEAR * d, n) for d in range(1, far)]
    across = [swap(value, 2, n) for value in column]
    places = [[[NEAR * d + k] for d in range(far)] for k in range(NEAR)]
    blocks, owners = column + across[:cut], places[0] + places[2][:cut]
    total = partial_lowrank("lowrank_1", me, tokens, blocks, owners)
    picks = [[(i,) for i in range(2 * far)]]
    (gathered,) = join("join_core", column + across, picks, block.shape, (total,))
    other = swap(gathered, 1, n)
    total = partial_lowrank("lowrank_2", me, tokens, across[cut:], places[2][cut:], (total,))
    owners = [[k + 1 for part in places[0] + places[2] for k in part]]

    stages = [bits[i : i + 2] for i in range(2, len(bits), 2)] + [bits[:2]]
    left = span([b for stage in stages[1:] for b in stage])
    moves = span(stages[0])
    targets_of = [[m ^ r for r in left] for m in moves]
    rows = packed_grads(me, targets_of, tokens, [other], owners, total, cotangent, mask)
    rows = list(rows)
    rows[-1] = hold("hold_rows", rows[-1], (), HIDE)
    arrays = [swap(array, m, n) for array, m in zip(rows[:0:-1], moves[:0:-1])] + [rows[0]]
    held = {(m, r): (a, i) for a, m in enumerate(moves[::-1]) for i, r in enumerate(left)}
    for number, stage in enumerate(stages[1:]):
        moves, left = span(stage), span([b for later in stages[number + 2 :] for b in later])
        pairs = [[(src, r ^ m) for src in sorted({s for s, _ in held}) for r in left] for m in moves]
        picks = [[held[pair] for pair in group] for group in pairs[1:]]
        sent = join(f"join_rows_{number}", arrays, picks, rows[0].shape[1:])
        came = [swap(array, m, n) for array, m in zip(sent[::-1], moves[:0:-1])]
        kept = {pair: (held[pair][0] + len(came), held[pair][1]) for pair in pairs[0]}
        for a, (m, group) in enumerate(zip(moves[:0:-1], pairs[:0:-1])):
            kept.update({(src ^ m, r ^ m): (a, i) for i, (src, r) in enumerate(group)})
        arrays, held = came + arrays, kept
    partner_targets = swap(targets, 1, n)

    places = [held[k, 0] for k in range(n)]
    kept, send = partial_features(me, arrays, places, projection, partner_targets)
    kept = kept + swap(send, 1, n).astype(jnp.float32)
    for stage in [bits[1:3]] + [[bit] for bit in bits[3:]]:
        half = kept.astype(jnp.bfloat16)
        arrived = [swap(half, m, n) for m in span(stage)[:0:-1]]
        if bits[-1] not in stage:
            for value in arrived:
                kept = kept + value.astype(jnp.float32)
    mine, send = partial_scores(me, targets, partner_targets, kept, arrived)
    total = mine + swap(send, 1, n)
    scale = lax.rsqrt(total[:, n : 2 * n] / PDIM + 1e-06)
    return (total[:, :n] * scale / PDIM).T


def solution(mesh):
    in_specs = (
        P(("groups", "shard"), None),
        P(("groups", "shard"), None),
        P(("groups", "shard")),
        P(None, "shard"),
        P("shard", None),
        P(("groups", "shard"), None),
    )
    out_specs = P("groups", "shard")
    return jax.shard_map(body, mesh=mesh, in_specs=in_specs, out_specs=out_specs, check_vma=False)
```

```python
import functools

import jax
import jax.numpy as jnp
from jax import lax
from jax.experimental import pallas as pl
from jax.experimental.pallas import tpu as pltpu
from jax.sharding import PartitionSpec as P

PDIM = 4096
LENGTH = 256
LANES = 256
NEAR = 4
MIB = 1 << 20
HIDE = 30 * 10**9
NT = (((1,), (1,)), ((), ()))
VMEM = pl.BlockSpec(memory_space=pltpu.VMEM)
SMEM = pl.BlockSpec(memory_space=pltpu.SMEM)
ANY = pl.BlockSpec(memory_space=pl.ANY)


def swap(value, bit, n):
    return lax.ppermute(value, "shard", [(s, s ^ bit) for s in range(n)])


def span(bits):
    sums = [0]
    for bit in bits:
        sums += [k + bit for k in sums]
    return sums


def in_hbm(value):
    return pltpu.with_memory_space_constraint(value, pltpu.HBM)


def in_vmem(value):
    return pltpu.with_memory_space_constraint(value, pltpu.VMEM)


def load_kernel(count, starts, *refs):
    sources, outs, sems = refs[:count], refs[-1 - count : -1], refs[-1]
    copies = []
    for source, start, out in zip(sources, starts, outs):
        rows = out.shape[0]
        step = min(rows, LANES // 2)
        for i in range(0, rows, step):
            part = source.at[pl.ds(start + i, step)]
            copies.append(pltpu.make_async_copy(part, out.at[pl.ds(i, step)], sems.at[len(copies)]))
    for copy in copies:
        copy.start()
    for copy in copies:
        copy.wait()


def load(name, parts, after):
    size = sum(rows * array.size // array.shape[0] * array.dtype.itemsize for array, _, rows in parts)
    pieces = sum(max(rows // (LANES // 2), 1) for _, _, rows in parts)
    return pl.pallas_call(
        functools.partial(load_kernel, len(parts), [start for _, start, _ in parts]),
        out_shape=[pltpu.VMEM((rows,) + array.shape[1:], array.dtype) for array, _, rows in parts],
        in_specs=[ANY] * (len(parts) + len(after)),
        out_specs=[VMEM] * len(parts),
        scratch_shapes=[pltpu.SemaphoreType.DMA((pieces,))],
        compiler_params=pltpu.CompilerParams(vmem_limit_bytes=MIB),
        cost_estimate=pl.CostEstimate(flops=0, bytes_accessed=2 * size, transcendentals=0),
        name=name,
    )(*[in_hbm(array) for array, _, _ in parts], *after)


def hold(name, value, after, flops=0):
    return pl.pallas_call(
        lambda *refs: None,
        out_shape=jax.ShapeDtypeStruct(value.shape, value.dtype),
        in_specs=[ANY] * (1 + len(after)),
        out_specs=ANY,
        input_output_aliases={0: 0},
        compiler_params=pltpu.CompilerParams(vmem_limit_bytes=MIB),
        cost_estimate=pl.CostEstimate(flops=flops, bytes_accessed=2000000, transcendentals=0),
        name=name,
    )(value, *after)


def join_kernel(picks, *refs):
    for pick, out in zip(picks, refs[-len(picks) :]):
        for target, (source, *entry) in enumerate(pick):
            out[target] = refs[source][entry[0]] if entry else refs[source][...]


def join(name, values, picks, shape, after=(), flops=0):
    return pl.pallas_call(
        functools.partial(join_kernel, picks),
        out_shape=[jax.ShapeDtypeStruct((len(pick),) + shape, values[0].dtype) for pick in picks],
        in_specs=[VMEM] * len(values) + [ANY] * len(after),
        out_specs=[VMEM] * len(picks),
        compiler_params=pltpu.CompilerParams(vmem_limit_bytes=2 * MIB),
        cost_estimate=pl.CostEstimate(flops=flops, bytes_accessed=2000000, transcendentals=0),
        name=name,
    )(*values, *after)


def add_lowrank(total, me, blocks, places, tokens):
    for block, owners in zip(blocks, places):
        depth = block.shape[-1]
        for i, k in enumerate(owners):
            start = pl.multiple_of((me[0] ^ k) * depth, depth)
            part = block[i] if len(block.shape) == 3 else block[...]
            total += lax.dot_general(part, tokens[:, pl.ds(start, depth)], NT, preferred_element_type=jnp.float32)
    return total


def lowrank_kernel(places, me, tokens, *refs):
    blocks, out = refs[: len(places)], refs[-1]
    before = refs[len(places)][...] if len(refs) > len(places) + 1 else jnp.zeros(out.shape, jnp.float32)
    out[...] = add_lowrank(before, me, blocks, places, tokens)


def partial_lowrank(name, me, tokens, blocks, places, before=()):
    return pl.pallas_call(
        functools.partial(lowrank_kernel, places),
        out_shape=jax.ShapeDtypeStruct((blocks[0].shape[-2], tokens.shape[0]), jnp.float32),
        in_specs=[SMEM] + [VMEM] * (1 + len(blocks) + len(before)),
        out_specs=VMEM,
        compiler_params=pltpu.CompilerParams(vmem_limit_bytes=2 * MIB),
        cost_estimate=pl.CostEstimate(flops=100000000, bytes_accessed=2000000, transcendentals=0),
        name=name,
    )(me, tokens, *blocks, *before)


def grads_kernel(owners, places, me, tokens, *refs):
    blocks = refs[: len(places)]
    before, cotangent, mask = refs[len(places) : len(places) + 3]
    outs, grads = refs[-1 - len(owners) : -1], refs[-1]
    total = add_lowrank(before[...], me, blocks, places, tokens)
    rank = total.shape[0]
    lowrank = total.astype(jnp.bfloat16) * mask[...].astype(jnp.bfloat16)
    turned = jnp.dot(lowrank, cotangent[...], preferred_element_type=jnp.float32)
    grads[...] = turned.T
    pack = LANES // rank
    share = outs[0].shape[1]
    for out, ks in zip(outs, owners):
        for i, k in enumerate(ks):
            start = pl.multiple_of((me[0] ^ k) * (share * pack), share * pack)
            for q in range(pack):
                rows = grads[pl.ds(start + q, share, stride=pack), :]
                out[i, :, q * rank : (q + 1) * rank] = rows.astype(jnp.bfloat16)


def packed_grads(me, owners, tokens, blocks, places, before, cotangent, mask):
    rank, width = blocks[0].shape[-2], cotangent.shape[1]
    share = width * rank // LANES // sum(len(ks) for ks in owners)
    return pl.pallas_call(
        functools.partial(grads_kernel, owners, places),
        out_shape=[jax.ShapeDtypeStruct((len(ks), share, LANES), jnp.bfloat16) for ks in owners],
        in_specs=[SMEM] + [VMEM] * (len(blocks) + 4),
        out_specs=[VMEM] * len(owners),
        scratch_shapes=[pltpu.VMEM((width, rank), jnp.float32)],
        compiler_params=pltpu.CompilerParams(vmem_limit_bytes=6 * MIB),
        cost_estimate=pl.CostEstimate(flops=100000000, bytes_accessed=2000000, transcendentals=0),
        name="grads",
    )(me, tokens, *blocks, before, cotangent, mask)


def features_kernel(places, count, me, *refs):
    arrays, weights = refs[:count], refs[count]
    keep, send, x, left, total = refs[-5:]
    n = len(places)
    share = arrays[0].shape[1]
    pitch = x.shape[1] // n
    for k, (source, entry) in enumerate(places):
        rows = arrays[source][entry]
        place = pl.multiple_of((me[0] ^ k) * pitch, pitch)
        for h in range(x.shape[0]):
            x[h, pl.ds(place, share), :] = rows[:, h * 128 : (h + 1) * 128].astype(jnp.float32)
    for j in range(share):
        for h in range(x.shape[0]):
            at = j * LANES + h * 128
            left[:, at : at + 128] = x[h, pl.ds(j, n, stride=pitch), :].astype(jnp.bfloat16)
    total[...] = jnp.dot(left[...], weights[...], preferred_element_type=jnp.float32)
    part = keep.shape[1]
    mine = pl.multiple_of((me[0] & 1) * part, part)
    partner = pl.multiple_of((1 - (me[0] & 1)) * part, part)
    keep[...] = total[:, pl.ds(mine, part)]
    send[...] = total[:, pl.ds(partner, part)].astype(jnp.bfloat16)


def partial_features(me, arrays, places, projection, after):
    n = len(places)
    share = arrays[0].shape[1]
    depth, width = projection.shape
    half = (n, width // 2)
    return pl.pallas_call(
        functools.partial(features_kernel, places, len(arrays)),
        out_shape=[jax.ShapeDtypeStruct(half, jnp.float32), jax.ShapeDtypeStruct(half, jnp.bfloat16)],
        in_specs=[SMEM] + [VMEM] * (len(arrays) + 1) + [ANY],
        out_specs=[VMEM, VMEM],
        scratch_shapes=[
            pltpu.VMEM((LANES // 128, n * max(share, 8), 128), jnp.float32),
            pltpu.VMEM((n, depth), jnp.bfloat16),
            pltpu.VMEM((n, width), jnp.float32),
        ],
        compiler_params=pltpu.CompilerParams(vmem_limit_bytes=4 * MIB),
        cost_estimate=pl.CostEstimate(flops=600000000, bytes_accessed=34000000, transcendentals=0),
        name="features",
    )(me, *arrays, in_vmem(projection), after)


def scores_kernel(me, targets, partner_targets, kept, *refs):
    mine, send = refs[-2:]
    features = kept[...]
    for arrived in refs[:-2]:
        features += arrived[...].astype(jnp.float32)
    count, half = features.shape
    start = pl.multiple_of((me[0] & 1) * half, half)
    high = lax.Precision.HIGHEST
    ones = jnp.ones((targets.shape[0], half), jnp.float32)
    squares = lax.dot_general(ones, features * features, NT, precision=high, preferred_element_type=jnp.float32)
    rest = jnp.zeros((targets.shape[0], mine.shape[1] - 2 * count), jnp.float32)
    for source, out in ((targets, mine), (partner_targets, send)):
        scale = lax.rsqrt(jnp.sum(source[...] * source[...], axis=1, keepdims=True) / PDIM + 1e-06)
        dots = lax.dot_general(
            source[:, pl.ds(start, half)], features, NT, precision=high, preferred_element_type=jnp.float32
        )
        parts = [dots * scale, squares] + ([rest] if rest.shape[1] else [])
        out[...] = jnp.concatenate(parts, axis=1)


def partial_scores(me, targets, partner_targets, kept, arrived):
    shape = jax.ShapeDtypeStruct((targets.shape[0], 128), jnp.float32)
    return pl.pallas_call(
        scores_kernel,
        out_shape=[shape, shape],
        in_specs=[SMEM] + [VMEM] * (3 + len(arrived)),
        out_specs=[VMEM, VMEM],
        compiler_params=pltpu.CompilerParams(vmem_limit_bytes=6 * MIB),
        name="partial_scores",
    )(me, targets, partner_targets, kept, *arrived)


def body(tokens, cotangent, response_loss_mask, adapter_down_weight, projection, targets):
    n = lax.axis_size("shard")
    far = n // NEAR
    me = lax.axis_index("shard").astype(jnp.int32).reshape(1)
    block = adapter_down_weight
    bits = [1 << i for i in range(n.bit_length() - 1)]

    whole = [(tokens, 0, tokens.shape[0]), (cotangent, 0, cotangent.shape[0])]
    whole += [(response_loss_mask.reshape(1, -1), 0, 1), (targets, 0, targets.shape[0])]
    tokens, cotangent, mask, targets = load("load_1", whole, (me,))
    order = list(range(far))[::-1]
    column = [swap(block, NEAR * d, n) for d in order[:-1]] + [block]
    across = [swap(value, 2, n) for value in column]
    places = [[[NEAR * d + k] for d in order] for k in range(NEAR)]
    blocks, owners = column + across[:1] + across[-1:], places[0] + places[2][:1] + places[2][-1:]
    total = partial_lowrank("lowrank_1", me, tokens, blocks, owners)
    picks = [[(i,) for i in range(2 * far)]]
    (gathered,) = join("join_core", column + across, picks, block.shape, (total,))
    other = swap(gathered, 1, n)
    total = partial_lowrank("lowrank_2", me, tokens, across[1:-1], places[2][1:-1], (total,))
    owners = [[k + 1 for part in places[0] + places[2] for k in part]]

    stages = [bits[i : i + 2] for i in range(2, len(bits), 2)] + [bits[:2]]
    left = span([b for stage in stages[1:] for b in stage])
    moves = span(stages[0])
    targets_of = [[m ^ r for r in left] for m in moves]
    rows = packed_grads(me, targets_of, tokens, [other], owners, total, cotangent, mask)
    rows = list(rows)
    rows[-1] = hold("hold_rows", rows[-1], (), HIDE)
    arrays = [swap(array, m, n) for array, m in zip(rows[:0:-1], moves[:0:-1])] + [rows[0]]
    held = {(m, r): (a, i) for a, m in enumerate(moves[::-1]) for i, r in enumerate(left)}
    for number, stage in enumerate(stages[1:]):
        moves, left = span(stage), span([b for later in stages[number + 2 :] for b in later])
        pairs = [[(src, r ^ m) for src in sorted({s for s, _ in held}) for r in left] for m in moves]
        picks = [[held[pair] for pair in group] for group in pairs[1:]]
        sent = join(f"join_rows_{number}", arrays, picks, rows[0].shape[1:])
        came = [swap(array, m, n) for array, m in zip(sent[::-1], moves[:0:-1])]
        kept = {pair: (held[pair][0] + len(came), held[pair][1]) for pair in pairs[0]}
        for a, (m, group) in enumerate(zip(moves[:0:-1], pairs[:0:-1])):
            kept.update({(src ^ m, r ^ m): (a, i) for i, (src, r) in enumerate(group)})
        arrays, held = came + arrays, kept
    partner_targets = swap(targets, 1, n)

    places = [held[k, 0] for k in range(n)]
    kept, send = partial_features(me, arrays, places, projection, partner_targets)
    kept = kept + swap(send, 1, n).astype(jnp.float32)
    for stage in [bits[1:3]] + [[bit] for bit in bits[3:]]:
        half = kept.astype(jnp.bfloat16)
        arrived = [swap(half, m, n) for m in span(stage)[:0:-1]]
        if bits[-1] not in stage:
            for value in arrived:
                kept = kept + value.astype(jnp.float32)
    mine, send = partial_scores(me, targets, partner_targets, kept, arrived)
    total = mine + swap(send, 1, n)
    scale = lax.rsqrt(total[:, n : 2 * n] / PDIM + 1e-06)
    return (total[:, :n] * scale / PDIM).T


def solution(mesh):
    in_specs = (
        P(("groups", "shard"), None),
        P(("groups", "shard"), None),
        P(("groups", "shard")),
        P(None, "shard"),
        P("shard", None),
        P(("groups", "shard"), None),
    )
    out_specs = P("groups", "shard")
    return jax.shard_map(body, mesh=mesh, in_specs=in_specs, out_specs=out_specs, check_vma=False)
```

```python
import functools

import jax
import jax.numpy as jnp
from jax import lax
from jax.experimental import pallas as pl
from jax.experimental.pallas import tpu as pltpu
from jax.sharding import PartitionSpec as P

PDIM = 4096
LENGTH = 256
LANES = 256
NEAR = 4
MIB = 1 << 20
HIDE = 30 * 10**9
NT = (((1,), (1,)), ((), ()))
VMEM = pl.BlockSpec(memory_space=pltpu.VMEM)
SMEM = pl.BlockSpec(memory_space=pltpu.SMEM)
ANY = pl.BlockSpec(memory_space=pl.ANY)


def swap(value, bit, n):
    return lax.ppermute(value, "shard", [(s, s ^ bit) for s in range(n)])


def span(bits):
    sums = [0]
    for bit in bits:
        sums += [k + bit for k in sums]
    return sums


def in_hbm(value):
    return pltpu.with_memory_space_constraint(value, pltpu.HBM)


def in_vmem(value):
    return pltpu.with_memory_space_constraint(value, pltpu.VMEM)


def load_kernel(count, starts, *refs):
    sources, outs, sems = refs[:count], refs[-1 - count : -1], refs[-1]
    copies = []
    for source, start, out in zip(sources, starts, outs):
        rows = out.shape[0]
        step = min(rows, LANES // 2)
        for i in range(0, rows, step):
            part = source.at[pl.ds(start + i, step)]
            copies.append(pltpu.make_async_copy(part, out.at[pl.ds(i, step)], sems.at[len(copies)]))
    for copy in copies:
        copy.start()
    for copy in copies:
        copy.wait()


def load(name, parts, after):
    size = sum(rows * array.size // array.shape[0] * array.dtype.itemsize for array, _, rows in parts)
    pieces = sum(max(rows // (LANES // 2), 1) for _, _, rows in parts)
    return pl.pallas_call(
        functools.partial(load_kernel, len(parts), [start for _, start, _ in parts]),
        out_shape=[pltpu.VMEM((rows,) + array.shape[1:], array.dtype) for array, _, rows in parts],
        in_specs=[ANY] * (len(parts) + len(after)),
        out_specs=[VMEM] * len(parts),
        scratch_shapes=[pltpu.SemaphoreType.DMA((pieces,))],
        compiler_params=pltpu.CompilerParams(vmem_limit_bytes=MIB),
        cost_estimate=pl.CostEstimate(flops=0, bytes_accessed=2 * size, transcendentals=0),
        name=name,
    )(*[in_hbm(array) for array, _, _ in parts], *after)


def hold(name, value, after, flops=0):
    return pl.pallas_call(
        lambda *refs: None,
        out_shape=jax.ShapeDtypeStruct(value.shape, value.dtype),
        in_specs=[ANY] * (1 + len(after)),
        out_specs=ANY,
        input_output_aliases={0: 0},
        compiler_params=pltpu.CompilerParams(vmem_limit_bytes=MIB),
        cost_estimate=pl.CostEstimate(flops=flops, bytes_accessed=2000000, transcendentals=0),
        name=name,
    )(value, *after)


def join_kernel(picks, *refs):
    for pick, out in zip(picks, refs[-len(picks) :]):
        for target, (source, *entry) in enumerate(pick):
            out[target] = refs[source][entry[0]] if entry else refs[source][...]


def join(name, values, picks, shape, after=(), flops=0):
    return pl.pallas_call(
        functools.partial(join_kernel, picks),
        out_shape=[jax.ShapeDtypeStruct((len(pick),) + shape, values[0].dtype) for pick in picks],
        in_specs=[VMEM] * len(values) + [ANY] * len(after),
        out_specs=[VMEM] * len(picks),
        compiler_params=pltpu.CompilerParams(vmem_limit_bytes=2 * MIB),
        cost_estimate=pl.CostEstimate(flops=flops, bytes_accessed=2000000, transcendentals=0),
        name=name,
    )(*values, *after)


def add_lowrank(total, me, blocks, places, tokens):
    for block, owners in zip(blocks, places):
        depth = block.shape[-1]
        for i, k in enumerate(owners):
            start = pl.multiple_of((me[0] ^ k) * depth, depth)
            part = block[i] if len(block.shape) == 3 else block[...]
            total += lax.dot_general(part, tokens[:, pl.ds(start, depth)], NT, preferred_element_type=jnp.float32)
    return total


def lowrank_kernel(places, me, tokens, *refs):
    blocks, out = refs[: len(places)], refs[-1]
    before = refs[len(places)][...] if len(refs) > len(places) + 1 else jnp.zeros(out.shape, jnp.float32)
    out[...] = add_lowrank(before, me, blocks, places, tokens)


def partial_lowrank(name, me, tokens, blocks, places, before=()):
    return pl.pallas_call(
        functools.partial(lowrank_kernel, places),
        out_shape=jax.ShapeDtypeStruct((blocks[0].shape[-2], tokens.shape[0]), jnp.float32),
        in_specs=[SMEM] + [VMEM] * (1 + len(blocks) + len(before)),
        out_specs=VMEM,
        compiler_params=pltpu.CompilerParams(vmem_limit_bytes=2 * MIB),
        cost_estimate=pl.CostEstimate(flops=100000000, bytes_accessed=2000000, transcendentals=0),
        name=name,
    )(me, tokens, *blocks, *before)


def grads_kernel(owners, places, me, tokens, *refs):
    blocks = refs[: len(places)]
    before, cotangent, mask = refs[len(places) : len(places) + 3]
    outs, grads = refs[-1 - len(owners) : -1], refs[-1]
    total = add_lowrank(before[...], me, blocks, places, tokens)
    rank = total.shape[0]
    lowrank = total.astype(jnp.bfloat16) * mask[...].astype(jnp.bfloat16)
    turned = jnp.dot(lowrank, cotangent[...], preferred_element_type=jnp.float32)
    grads[...] = turned.T
    pack = LANES // rank
    share = outs[0].shape[1]
    for out, ks in zip(outs, owners):
        for i, k in enumerate(ks):
            start = pl.multiple_of((me[0] ^ k) * (share * pack), share * pack)
            for q in range(pack):
                rows = grads[pl.ds(start + q, share, stride=pack), :]
                out[i, :, q * rank : (q + 1) * rank] = rows.astype(jnp.bfloat16)


def packed_grads(me, owners, tokens, blocks, places, before, cotangent, mask):
    rank, width = blocks[0].shape[-2], cotangent.shape[1]
    share = width * rank // LANES // sum(len(ks) for ks in owners)
    return pl.pallas_call(
        functools.partial(grads_kernel, owners, places),
        out_shape=[jax.ShapeDtypeStruct((len(ks), share, LANES), jnp.bfloat16) for ks in owners],
        in_specs=[SMEM] + [VMEM] * (len(blocks) + 4),
        out_specs=[VMEM] * len(owners),
        scratch_shapes=[pltpu.VMEM((width, rank), jnp.float32)],
        compiler_params=pltpu.CompilerParams(vmem_limit_bytes=6 * MIB),
        cost_estimate=pl.CostEstimate(flops=100000000, bytes_accessed=2000000, transcendentals=0),
        name="grads",
    )(me, tokens, *blocks, before, cotangent, mask)


def features_kernel(places, count, me, *refs):
    arrays, weights = refs[:count], refs[count]
    keep, send, x, left, total = refs[-5:]
    n = len(places)
    share = arrays[0].shape[1]
    pitch = x.shape[1] // n
    for k, (source, entry) in enumerate(places):
        rows = arrays[source][entry]
        place = pl.multiple_of((me[0] ^ k) * pitch, pitch)
        for h in range(x.shape[0]):
            x[h, pl.ds(place, share), :] = rows[:, h * 128 : (h + 1) * 128].astype(jnp.float32)
    for j in range(share):
        for h in range(x.shape[0]):
            at = j * LANES + h * 128
            left[:, at : at + 128] = x[h, pl.ds(j, n, stride=pitch), :].astype(jnp.bfloat16)
    total[...] = jnp.dot(left[...], weights[...], preferred_element_type=jnp.float32)
    part = keep.shape[1]
    mine = pl.multiple_of((me[0] & 1) * part, part)
    partner = pl.multiple_of((1 - (me[0] & 1)) * part, part)
    keep[...] = total[:, pl.ds(mine, part)]
    send[...] = total[:, pl.ds(partner, part)].astype(jnp.bfloat16)


def partial_features(me, arrays, places, projection, after):
    n = len(places)
    share = arrays[0].shape[1]
    depth, width = projection.shape
    half = (n, width // 2)
    return pl.pallas_call(
        functools.partial(features_kernel, places, len(arrays)),
        out_shape=[jax.ShapeDtypeStruct(half, jnp.float32), jax.ShapeDtypeStruct(half, jnp.bfloat16)],
        in_specs=[SMEM] + [VMEM] * (len(arrays) + 1) + [ANY],
        out_specs=[VMEM, VMEM],
        scratch_shapes=[
            pltpu.VMEM((LANES // 128, n * max(share, 8), 128), jnp.float32),
            pltpu.VMEM((n, depth), jnp.bfloat16),
            pltpu.VMEM((n, width), jnp.float32),
        ],
        compiler_params=pltpu.CompilerParams(vmem_limit_bytes=4 * MIB),
        cost_estimate=pl.CostEstimate(flops=600000000, bytes_accessed=34000000, transcendentals=0),
        name="features",
    )(me, *arrays, in_vmem(projection), after)


def scores_kernel(me, targets, partner_targets, kept, *refs):
    mine, send = refs[-2:]
    features = kept[...]
    for arrived in refs[:-2]:
        features += arrived[...].astype(jnp.float32)
    count, half = features.shape
    start = pl.multiple_of((me[0] & 1) * half, half)
    high = lax.Precision.HIGHEST
    ones = jnp.ones((targets.shape[0], half), jnp.float32)
    squares = lax.dot_general(ones, features * features, NT, precision=high, preferred_element_type=jnp.float32)
    rest = jnp.zeros((targets.shape[0], mine.shape[1] - 2 * count), jnp.float32)
    for source, out in ((targets, mine), (partner_targets, send)):
        scale = lax.rsqrt(jnp.sum(source[...] * source[...], axis=1, keepdims=True) / PDIM + 1e-06)
        dots = lax.dot_general(
            source[:, pl.ds(start, half)], features, NT, precision=high, preferred_element_type=jnp.float32
        )
        parts = [dots * scale, squares] + ([rest] if rest.shape[1] else [])
        out[...] = jnp.concatenate(parts, axis=1)


def partial_scores(me, targets, partner_targets, kept, arrived):
    shape = jax.ShapeDtypeStruct((targets.shape[0], 128), jnp.float32)
    return pl.pallas_call(
        scores_kernel,
        out_shape=[shape, shape],
        in_specs=[SMEM] + [VMEM] * (3 + len(arrived)),
        out_specs=[VMEM, VMEM],
        compiler_params=pltpu.CompilerParams(vmem_limit_bytes=6 * MIB),
        name="partial_scores",
    )(me, targets, partner_targets, kept, *arrived)


def body(tokens, cotangent, response_loss_mask, adapter_down_weight, projection, targets):
    n = lax.axis_size("shard")
    far = n // NEAR
    me = lax.axis_index("shard").astype(jnp.int32).reshape(1)
    block = adapter_down_weight
    bits = [1 << i for i in range(n.bit_length() - 1)]

    whole = [(tokens, 0, tokens.shape[0]), (cotangent, 0, cotangent.shape[0])]
    whole += [(response_loss_mask.reshape(1, -1), 0, 1), (targets, 0, targets.shape[0])]
    tokens, cotangent, mask, targets = load("load_1", whole, (me,))
    order = [far - 1] + list(range(1, far - 1)) + [0]
    column = [swap(block, NEAR * d, n) for d in order[:-1]] + [block]
    across = [swap(value, 2, n) for value in column]
    places = [[[NEAR * d + k] for d in order] for k in range(NEAR)]
    blocks, owners = column + across[:1] + across[-1:], places[0] + places[2][:1] + places[2][-1:]
    total = partial_lowrank("lowrank_1", me, tokens, blocks, owners)
    picks = [[(i,) for i in range(2 * far)]]
    (gathered,) = join("join_core", column + across, picks, block.shape, (total,))
    other = swap(gathered, 1, n)
    total = partial_lowrank("lowrank_2", me, tokens, across[1:-1], places[2][1:-1], (total,))
    owners = [[k + 1 for part in places[0] + places[2] for k in part]]

    stages = [bits[i : i + 2] for i in range(2, len(bits), 2)] + [bits[:2]]
    left = span([b for stage in stages[1:] for b in stage])
    moves = span(stages[0])
    targets_of = [[m ^ r for r in left] for m in moves]
    rows = packed_grads(me, targets_of, tokens, [other], owners, total, cotangent, mask)
    rows = list(rows)
    rows[-1] = hold("hold_rows", rows[-1], (), HIDE)
    arrays = [swap(array, m, n) for array, m in zip(rows[:0:-1], moves[:0:-1])] + [rows[0]]
    held = {(m, r): (a, i) for a, m in enumerate(moves[::-1]) for i, r in enumerate(left)}
    for number, stage in enumerate(stages[1:]):
        moves, left = span(stage), span([b for later in stages[number + 2 :] for b in later])
        pairs = [[(src, r ^ m) for src in sorted({s for s, _ in held}) for r in left] for m in moves]
        picks = [[held[pair] for pair in group] for group in pairs[1:]]
        sent = join(f"join_rows_{number}", arrays, picks, rows[0].shape[1:])
        came = [swap(array, m, n) for array, m in zip(sent[::-1], moves[:0:-1])]
        kept = {pair: (held[pair][0] + len(came), held[pair][1]) for pair in pairs[0]}
        for a, (m, group) in enumerate(zip(moves[:0:-1], pairs[:0:-1])):
            kept.update({(src ^ m, r ^ m): (a, i) for i, (src, r) in enumerate(group)})
        arrays, held = came + arrays, kept
    partner_targets = swap(targets, 1, n)

    places = [held[k, 0] for k in range(n)]
    kept, send = partial_features(me, arrays, places, projection, partner_targets)
    kept = kept + swap(send, 1, n).astype(jnp.float32)
    for stage in [bits[1:3]] + [[bit] for bit in bits[3:]]:
        half = kept.astype(jnp.bfloat16)
        arrived = [swap(half, m, n) for m in span(stage)[:0:-1]]
        if bits[-1] not in stage:
            for value in arrived:
                kept = kept + value.astype(jnp.float32)
    mine, send = partial_scores(me, targets, partner_targets, kept, arrived)
    total = mine + swap(send, 1, n)
    scale = lax.rsqrt(total[:, n : 2 * n] / PDIM + 1e-06)
    return (total[:, :n] * scale / PDIM).T


def solution(mesh):
    in_specs = (
        P(("groups", "shard"), None),
        P(("groups", "shard"), None),
        P(("groups", "shard")),
        P(None, "shard"),
        P("shard", None),
        P(("groups", "shard"), None),
    )
    out_specs = P("groups", "shard")
    return jax.shard_map(body, mesh=mesh, in_specs=in_specs, out_specs=out_specs, check_vma=False)
```

```python
import functools

import jax
import jax.numpy as jnp
from jax import lax
from jax.experimental import pallas as pl
from jax.experimental.pallas import tpu as pltpu
from jax.sharding import PartitionSpec as P

PDIM = 4096
LENGTH = 256
LANES = 256
NEAR = 4
MIB = 1 << 20
HIDE = 30 * 10**9
NT = (((1,), (1,)), ((), ()))
VMEM = pl.BlockSpec(memory_space=pltpu.VMEM)
SMEM = pl.BlockSpec(memory_space=pltpu.SMEM)
ANY = pl.BlockSpec(memory_space=pl.ANY)


def swap(value, bit, n):
    return lax.ppermute(value, "shard", [(s, s ^ bit) for s in range(n)])


def span(bits):
    sums = [0]
    for bit in bits:
        sums += [k + bit for k in sums]
    return sums


def in_hbm(value):
    return pltpu.with_memory_space_constraint(value, pltpu.HBM)


def in_vmem(value):
    return pltpu.with_memory_space_constraint(value, pltpu.VMEM)


def load_kernel(count, starts, *refs):
    sources, outs, sems = refs[:count], refs[-1 - count : -1], refs[-1]
    copies = []
    for source, start, out in zip(sources, starts, outs):
        rows = out.shape[0]
        step = min(rows, LANES // 2)
        for i in range(0, rows, step):
            part = source.at[pl.ds(start + i, step)]
            copies.append(pltpu.make_async_copy(part, out.at[pl.ds(i, step)], sems.at[len(copies)]))
    for copy in copies:
        copy.start()
    for copy in copies:
        copy.wait()


def load(name, parts, after):
    size = sum(rows * array.size // array.shape[0] * array.dtype.itemsize for array, _, rows in parts)
    pieces = sum(max(rows // (LANES // 2), 1) for _, _, rows in parts)
    return pl.pallas_call(
        functools.partial(load_kernel, len(parts), [start for _, start, _ in parts]),
        out_shape=[pltpu.VMEM((rows,) + array.shape[1:], array.dtype) for array, _, rows in parts],
        in_specs=[ANY] * (len(parts) + len(after)),
        out_specs=[VMEM] * len(parts),
        scratch_shapes=[pltpu.SemaphoreType.DMA((pieces,))],
        compiler_params=pltpu.CompilerParams(vmem_limit_bytes=MIB),
        cost_estimate=pl.CostEstimate(flops=0, bytes_accessed=2 * size, transcendentals=0),
        name=name,
    )(*[in_hbm(array) for array, _, _ in parts], *after)


def hold(name, value, after, flops=0):
    return pl.pallas_call(
        lambda *refs: None,
        out_shape=jax.ShapeDtypeStruct(value.shape, value.dtype),
        in_specs=[ANY] * (1 + len(after)),
        out_specs=ANY,
        input_output_aliases={0: 0},
        compiler_params=pltpu.CompilerParams(vmem_limit_bytes=MIB),
        cost_estimate=pl.CostEstimate(flops=flops, bytes_accessed=2000000, transcendentals=0),
        name=name,
    )(value, *after)


def join_kernel(picks, *refs):
    for pick, out in zip(picks, refs[-len(picks) :]):
        for target, (source, *entry) in enumerate(pick):
            out[target] = refs[source][entry[0]] if entry else refs[source][...]


def join(name, values, picks, shape, after=(), flops=0):
    return pl.pallas_call(
        functools.partial(join_kernel, picks),
        out_shape=[jax.ShapeDtypeStruct((len(pick),) + shape, values[0].dtype) for pick in picks],
        in_specs=[VMEM] * len(values) + [ANY] * len(after),
        out_specs=[VMEM] * len(picks),
        compiler_params=pltpu.CompilerParams(vmem_limit_bytes=2 * MIB),
        cost_estimate=pl.CostEstimate(flops=flops, bytes_accessed=2000000, transcendentals=0),
        name=name,
    )(*values, *after)


def add_lowrank(total, me, blocks, places, tokens):
    for block, owners in zip(blocks, places):
        depth = block.shape[-1]
        for i, k in enumerate(owners):
            start = pl.multiple_of((me[0] ^ k) * depth, depth)
            part = block[i] if len(block.shape) == 3 else block[...]
            total += lax.dot_general(part, tokens[:, pl.ds(start, depth)], NT, preferred_element_type=jnp.float32)
    return total


def lowrank_kernel(places, me, tokens, *refs):
    blocks, out = refs[: len(places)], refs[-1]
    before = refs[len(places)][...] if len(refs) > len(places) + 1 else jnp.zeros(out.shape, jnp.float32)
    out[...] = add_lowrank(before, me, blocks, places, tokens)


def partial_lowrank(name, me, tokens, blocks, places, before=()):
    return pl.pallas_call(
        functools.partial(lowrank_kernel, places),
        out_shape=jax.ShapeDtypeStruct((blocks[0].shape[-2], tokens.shape[0]), jnp.float32),
        in_specs=[SMEM] + [VMEM] * (1 + len(blocks) + len(before)),
        out_specs=VMEM,
        compiler_params=pltpu.CompilerParams(vmem_limit_bytes=2 * MIB),
        cost_estimate=pl.CostEstimate(flops=100000000, bytes_accessed=2000000, transcendentals=0),
        name=name,
    )(me, tokens, *blocks, *before)


def grads_kernel(owners, places, me, tokens, *refs):
    blocks = refs[: len(places)]
    before, cotangent, mask = refs[len(places) : len(places) + 3]
    outs, grads = refs[-1 - len(owners) : -1], refs[-1]
    total = add_lowrank(before[...], me, blocks, places, tokens)
    rank = total.shape[0]
    lowrank = total.astype(jnp.bfloat16) * mask[...].astype(jnp.bfloat16)
    turned = jnp.dot(lowrank, cotangent[...], preferred_element_type=jnp.float32)
    grads[...] = turned.T
    pack = LANES // rank
    share = outs[0].shape[1]
    for out, ks in zip(outs, owners):
        for i, k in enumerate(ks):
            start = pl.multiple_of((me[0] ^ k) * (share * pack), share * pack)
            for q in range(pack):
                rows = grads[pl.ds(start + q, share, stride=pack), :]
                out[i, :, q * rank : (q + 1) * rank] = rows.astype(jnp.bfloat16)


def packed_grads(me, owners, tokens, blocks, places, before, cotangent, mask):
    rank, width = blocks[0].shape[-2], cotangent.shape[1]
    share = width * rank // LANES // sum(len(ks) for ks in owners)
    return pl.pallas_call(
        functools.partial(grads_kernel, owners, places),
        out_shape=[jax.ShapeDtypeStruct((len(ks), share, LANES), jnp.bfloat16) for ks in owners],
        in_specs=[SMEM] + [VMEM] * (len(blocks) + 4),
        out_specs=[VMEM] * len(owners),
        scratch_shapes=[pltpu.VMEM((width, rank), jnp.float32)],
        compiler_params=pltpu.CompilerParams(vmem_limit_bytes=6 * MIB),
        cost_estimate=pl.CostEstimate(flops=100000000, bytes_accessed=2000000, transcendentals=0),
        name="grads",
    )(me, tokens, *blocks, before, cotangent, mask)


def features_kernel(places, count, me, *refs):
    arrays, weights = refs[:count], refs[count]
    keep, send, x, left, total = refs[-5:]
    n = len(places)
    share = arrays[0].shape[1]
    pitch = x.shape[1] // n
    for k, (source, entry) in enumerate(places):
        rows = arrays[source][entry]
        place = pl.multiple_of((me[0] ^ k) * pitch, pitch)
        for h in range(x.shape[0]):
            x[h, pl.ds(place, share), :] = rows[:, h * 128 : (h + 1) * 128].astype(jnp.float32)
    for j in range(share):
        for h in range(x.shape[0]):
            at = j * LANES + h * 128
            left[:, at : at + 128] = x[h, pl.ds(j, n, stride=pitch), :].astype(jnp.bfloat16)
    total[...] = jnp.dot(left[...], weights[...], preferred_element_type=jnp.float32)
    part = keep.shape[1]
    mine = pl.multiple_of((me[0] & 1) * part, part)
    partner = pl.multiple_of((1 - (me[0] & 1)) * part, part)
    keep[...] = total[:, pl.ds(mine, part)]
    send[...] = total[:, pl.ds(partner, part)].astype(jnp.bfloat16)


def partial_features(me, arrays, places, projection, after):
    n = len(places)
    share = arrays[0].shape[1]
    depth, width = projection.shape
    half = (n, width // 2)
    return pl.pallas_call(
        functools.partial(features_kernel, places, len(arrays)),
        out_shape=[jax.ShapeDtypeStruct(half, jnp.float32), jax.ShapeDtypeStruct(half, jnp.bfloat16)],
        in_specs=[SMEM] + [VMEM] * (len(arrays) + 1) + [ANY],
        out_specs=[VMEM, VMEM],
        scratch_shapes=[
            pltpu.VMEM((LANES // 128, n * max(share, 8), 128), jnp.float32),
            pltpu.VMEM((n, depth), jnp.bfloat16),
            pltpu.VMEM((n, width), jnp.float32),
        ],
        compiler_params=pltpu.CompilerParams(vmem_limit_bytes=4 * MIB),
        cost_estimate=pl.CostEstimate(flops=600000000, bytes_accessed=34000000, transcendentals=0),
        name="features",
    )(me, *arrays, in_vmem(projection), after)


def scores_kernel(me, targets, partner_targets, kept, *refs):
    mine, send = refs[-2:]
    features = kept[...]
    for arrived in refs[:-2]:
        features += arrived[...].astype(jnp.float32)
    count, half = features.shape
    start = pl.multiple_of((me[0] & 1) * half, half)
    high = lax.Precision.HIGHEST
    ones = jnp.ones((targets.shape[0], half), jnp.float32)
    squares = lax.dot_general(ones, features * features, NT, precision=high, preferred_element_type=jnp.float32)
    rest = jnp.zeros((targets.shape[0], mine.shape[1] - 2 * count), jnp.float32)
    for source, out in ((targets, mine), (partner_targets, send)):
        scale = lax.rsqrt(jnp.sum(source[...] * source[...], axis=1, keepdims=True) / PDIM + 1e-06)
        dots = lax.dot_general(
            source[:, pl.ds(start, half)], features, NT, precision=high, preferred_element_type=jnp.float32
        )
        parts = [dots * scale, squares] + ([rest] if rest.shape[1] else [])
        out[...] = jnp.concatenate(parts, axis=1)


def partial_scores(me, targets, partner_targets, kept, arrived):
    shape = jax.ShapeDtypeStruct((targets.shape[0], 128), jnp.float32)
    return pl.pallas_call(
        scores_kernel,
        out_shape=[shape, shape],
        in_specs=[SMEM] + [VMEM] * (3 + len(arrived)),
        out_specs=[VMEM, VMEM],
        compiler_params=pltpu.CompilerParams(vmem_limit_bytes=6 * MIB),
        name="partial_scores",
    )(me, targets, partner_targets, kept, *arrived)


def body(tokens, cotangent, response_loss_mask, adapter_down_weight, projection, targets):
    n = lax.axis_size("shard")
    far = n // NEAR
    me = lax.axis_index("shard").astype(jnp.int32).reshape(1)
    block = adapter_down_weight
    bits = [1 << i for i in range(n.bit_length() - 1)]

    whole = [(tokens, 0, tokens.shape[0]), (cotangent, 0, cotangent.shape[0])]
    whole += [(response_loss_mask.reshape(1, -1), 0, 1), (targets, 0, targets.shape[0])]
    tokens, cotangent, mask, targets = load("load_1", whole, (me,))
    order = [far - 1] + list(range(1, far - 1)) + [0]
    column = [swap(block, NEAR * d, n) for d in order[:-1]] + [block]
    across = [swap(value, 2, n) for value in column]
    places = [[[NEAR * d + k] for d in order] for k in range(NEAR)]
    blocks, owners = column + across[:1] + across[-1:], places[0] + places[2][:1] + places[2][-1:]
    total = partial_lowrank("lowrank_1", me, tokens, blocks, owners)
    picks = [[(i,) for i in range(2 * far)]]
    (gathered,) = join("join_core", column + across, picks, block.shape, (total,))
    other = swap(gathered, 1, n)
    total = partial_lowrank("lowrank_2", me, tokens, across[1:-1], places[2][1:-1], (total,))
    owners = [[k + 1 for part in places[0] + places[2] for k in part]]

    stages = [bits[i : i + 2] for i in range(2, len(bits), 2)] + [bits[:2]]
    left = span([b for stage in stages[1:] for b in stage])
    moves = span(stages[0])
    targets_of = [[m ^ r for r in left] for m in moves]
    rows = packed_grads(me, targets_of, tokens, [other], owners, total, cotangent, mask)
    rows = list(rows)
    rows[-1] = hold("hold_rows", rows[-1], (), HIDE)
    arrays = [swap(array, m, n) for array, m in zip(rows[:0:-1], moves[:0:-1])] + [rows[0]]
    held = {(m, r): (a, i) for a, m in enumerate(moves[::-1]) for i, r in enumerate(left)}
    for number, stage in enumerate(stages[1:]):
        moves, left = span(stage), span([b for later in stages[number + 2 :] for b in later])
        pairs = [[(src, r ^ m) for src in sorted({s for s, _ in held}) for r in left] for m in moves]
        picks = [[held[pair] for pair in group] for group in pairs[1:]]
        sent = join(f"join_rows_{number}", arrays, picks, rows[0].shape[1:])
        came = [swap(array, m, n) for array, m in zip(sent[::-1], moves[:0:-1])]
        kept = {pair: (held[pair][0] + len(came), held[pair][1]) for pair in pairs[0]}
        for a, (m, group) in enumerate(zip(moves[:0:-1], pairs[:0:-1])):
            kept.update({(src ^ m, r ^ m): (a, i) for i, (src, r) in enumerate(group)})
        arrays, held = came + arrays, kept
    partner_targets = swap(targets, 1, n)

    places = [held[k, 0] for k in range(n)]
    kept, send = partial_features(me, arrays, places, projection, partner_targets)
    kept = kept + swap(send, 1, n).astype(jnp.float32)
    for stage in [[bit] for bit in bits[:2:-1]] + [bits[1:3]]:
        half = kept.astype(jnp.bfloat16)
        arrived = [swap(half, m, n) for m in span(stage)[:0:-1]]
        if len(stage) == 1:
            kept = kept + arrived[0].astype(jnp.float32)
    mine, send = partial_scores(me, targets, partner_targets, kept, arrived)
    total = mine + swap(send, 1, n)
    scale = lax.rsqrt(total[:, n : 2 * n] / PDIM + 1e-06)
    return (total[:, :n] * scale / PDIM).T


def solution(mesh):
    in_specs = (
        P(("groups", "shard"), None),
        P(("groups", "shard"), None),
        P(("groups", "shard")),
        P(None, "shard"),
        P("shard", None),
        P(("groups", "shard"), None),
    )
    out_specs = P("groups", "shard")
    return jax.shard_map(body, mesh=mesh, in_specs=in_specs, out_specs=out_specs, check_vma=False)
```

```python
import functools

import jax
import jax.numpy as jnp
from jax import lax
from jax.experimental import pallas as pl
from jax.experimental.pallas import tpu as pltpu
from jax.sharding import PartitionSpec as P

PDIM = 4096
LENGTH = 256
LANES = 256
NEAR = 4
MIB = 1 << 20
HIDE = 30 * 10**9
NT = (((1,), (1,)), ((), ()))
VMEM = pl.BlockSpec(memory_space=pltpu.VMEM)
SMEM = pl.BlockSpec(memory_space=pltpu.SMEM)
ANY = pl.BlockSpec(memory_space=pl.ANY)


def swap(value, bit, n):
    return lax.ppermute(value, "shard", [(s, s ^ bit) for s in range(n)])


def span(bits):
    sums = [0]
    for bit in bits:
        sums += [k + bit for k in sums]
    return sums


def in_hbm(value):
    return pltpu.with_memory_space_constraint(value, pltpu.HBM)


def in_vmem(value):
    return pltpu.with_memory_space_constraint(value, pltpu.VMEM)


def load_kernel(count, starts, *refs):
    sources, outs, sems = refs[:count], refs[-1 - count : -1], refs[-1]
    copies = []
    for source, start, out in zip(sources, starts, outs):
        rows = out.shape[0]
        step = min(rows, LANES // 2)
        for i in range(0, rows, step):
            part = source.at[pl.ds(start + i, step)]
            copies.append(pltpu.make_async_copy(part, out.at[pl.ds(i, step)], sems.at[len(copies)]))
    for copy in copies:
        copy.start()
    for copy in copies:
        copy.wait()


def load(name, parts, after):
    size = sum(rows * array.size // array.shape[0] * array.dtype.itemsize for array, _, rows in parts)
    pieces = sum(max(rows // (LANES // 2), 1) for _, _, rows in parts)
    return pl.pallas_call(
        functools.partial(load_kernel, len(parts), [start for _, start, _ in parts]),
        out_shape=[pltpu.VMEM((rows,) + array.shape[1:], array.dtype) for array, _, rows in parts],
        in_specs=[ANY] * (len(parts) + len(after)),
        out_specs=[VMEM] * len(parts),
        scratch_shapes=[pltpu.SemaphoreType.DMA((pieces,))],
        compiler_params=pltpu.CompilerParams(vmem_limit_bytes=MIB),
        cost_estimate=pl.CostEstimate(flops=0, bytes_accessed=2 * size, transcendentals=0),
        name=name,
    )(*[in_hbm(array) for array, _, _ in parts], *after)


def hold(name, value, after, flops=0):
    return pl.pallas_call(
        lambda *refs: None,
        out_shape=jax.ShapeDtypeStruct(value.shape, value.dtype),
        in_specs=[ANY] * (1 + len(after)),
        out_specs=ANY,
        input_output_aliases={0: 0},
        compiler_params=pltpu.CompilerParams(vmem_limit_bytes=MIB),
        cost_estimate=pl.CostEstimate(flops=flops, bytes_accessed=2000000, transcendentals=0),
        name=name,
    )(value, *after)


def join_kernel(picks, *refs):
    for pick, out in zip(picks, refs[-len(picks) :]):
        for target, (source, *entry) in enumerate(pick):
            out[target] = refs[source][entry[0]] if entry else refs[source][...]


def join(name, values, picks, shape, after=(), flops=0):
    return pl.pallas_call(
        functools.partial(join_kernel, picks),
        out_shape=[jax.ShapeDtypeStruct((len(pick),) + shape, values[0].dtype) for pick in picks],
        in_specs=[VMEM] * len(values) + [ANY] * len(after),
        out_specs=[VMEM] * len(picks),
        compiler_params=pltpu.CompilerParams(vmem_limit_bytes=2 * MIB),
        cost_estimate=pl.CostEstimate(flops=flops, bytes_accessed=2000000, transcendentals=0),
        name=name,
    )(*values, *after)


def add_lowrank(total, me, blocks, places, tokens):
    for block, owners in zip(blocks, places):
        depth = block.shape[-1]
        for i, k in enumerate(owners):
            start = pl.multiple_of((me[0] ^ k) * depth, depth)
            part = block[i] if len(block.shape) == 3 else block[...]
            total += lax.dot_general(part, tokens[:, pl.ds(start, depth)], NT, preferred_element_type=jnp.float32)
    return total


def lowrank_kernel(places, me, tokens, *refs):
    blocks, out = refs[: len(places)], refs[-1]
    before = refs[len(places)][...] if len(refs) > len(places) + 1 else jnp.zeros(out.shape, jnp.float32)
    out[...] = add_lowrank(before, me, blocks, places, tokens)


def partial_lowrank(name, me, tokens, blocks, places, before=()):
    return pl.pallas_call(
        functools.partial(lowrank_kernel, places),
        out_shape=jax.ShapeDtypeStruct((blocks[0].shape[-2], tokens.shape[0]), jnp.float32),
        in_specs=[SMEM] + [VMEM] * (1 + len(blocks) + len(before)),
        out_specs=VMEM,
        compiler_params=pltpu.CompilerParams(vmem_limit_bytes=2 * MIB),
        cost_estimate=pl.CostEstimate(flops=100000000, bytes_accessed=2000000, transcendentals=0),
        name=name,
    )(me, tokens, *blocks, *before)


def grads_kernel(owners, places, me, tokens, *refs):
    blocks = refs[: len(places)]
    before, cotangent, mask = refs[len(places) : len(places) + 3]
    outs, grads = refs[-1 - len(owners) : -1], refs[-1]
    total = add_lowrank(before[...], me, blocks, places, tokens)
    rank = total.shape[0]
    lowrank = total.astype(jnp.bfloat16) * mask[...].astype(jnp.bfloat16)
    turned = jnp.dot(lowrank, cotangent[...], preferred_element_type=jnp.float32)
    grads[...] = turned.T
    pack = LANES // rank
    share = outs[0].shape[1]
    for out, ks in zip(outs, owners):
        for i, k in enumerate(ks):
            start = pl.multiple_of((me[0] ^ k) * (share * pack), share * pack)
            for q in range(pack):
                rows = grads[pl.ds(start + q, share, stride=pack), :]
                out[i, :, q * rank : (q + 1) * rank] = rows.astype(jnp.bfloat16)


def packed_grads(me, owners, tokens, blocks, places, before, cotangent, mask):
    rank, width = blocks[0].shape[-2], cotangent.shape[1]
    share = width * rank // LANES // sum(len(ks) for ks in owners)
    return pl.pallas_call(
        functools.partial(grads_kernel, owners, places),
        out_shape=[jax.ShapeDtypeStruct((len(ks), share, LANES), jnp.bfloat16) for ks in owners],
        in_specs=[SMEM] + [VMEM] * (len(blocks) + 4),
        out_specs=[VMEM] * len(owners),
        scratch_shapes=[pltpu.VMEM((width, rank), jnp.float32)],
        compiler_params=pltpu.CompilerParams(vmem_limit_bytes=6 * MIB),
        cost_estimate=pl.CostEstimate(flops=100000000, bytes_accessed=2000000, transcendentals=0),
        name="grads",
    )(me, tokens, *blocks, before, cotangent, mask)


def features_kernel(places, count, me, *refs):
    arrays, weights = refs[:count], refs[count]
    keep, rest, send, x, left, total = refs[-6:]
    n = len(places)
    share = arrays[0].shape[1]
    pitch = x.shape[1] // n
    for k, (source, entry) in enumerate(places):
        rows = arrays[source][entry]
        place = pl.multiple_of((me[0] ^ k) * pitch, pitch)
        for h in range(x.shape[0]):
            x[h, pl.ds(place, share), :] = rows[:, h * 128 : (h + 1) * 128].astype(jnp.float32)
    for j in range(share):
        for h in range(x.shape[0]):
            at = j * LANES + h * 128
            left[:, at : at + 128] = x[h, pl.ds(j, n, stride=pitch), :].astype(jnp.bfloat16)
    total[...] = jnp.dot(left[...], weights[...], preferred_element_type=jnp.float32)
    width = keep.shape[1]
    core, y = me[0] & 1, (me[0] >> 1) & 1
    keep[...] = total[:, pl.ds(pl.multiple_of((2 * core + y) * width, width), width)]
    rest[...] = total[:, pl.ds(pl.multiple_of((2 * core + 1 - y) * width, width), width)]
    for i, side in enumerate((y, 1 - y)):
        columns = pl.ds(pl.multiple_of((2 * (1 - core) + side) * width, width), width)
        send[i] = total[:, columns].astype(jnp.bfloat16)


def partial_features(me, arrays, places, projection, after):
    n = len(places)
    share = arrays[0].shape[1]
    depth, width = projection.shape
    quarter = (n, width // NEAR)
    return pl.pallas_call(
        functools.partial(features_kernel, places, len(arrays)),
        out_shape=[
            jax.ShapeDtypeStruct(quarter, jnp.float32),
            jax.ShapeDtypeStruct(quarter, jnp.float32),
            jax.ShapeDtypeStruct((2,) + quarter, jnp.bfloat16),
        ],
        in_specs=[SMEM] + [VMEM] * (len(arrays) + 1) + [ANY] * len(after),
        out_specs=[VMEM, VMEM, VMEM],
        scratch_shapes=[
            pltpu.VMEM((LANES // 128, n * max(share, 8), 128), jnp.float32),
            pltpu.VMEM((n, depth), jnp.bfloat16),
            pltpu.VMEM((n, width), jnp.float32),
        ],
        compiler_params=pltpu.CompilerParams(vmem_limit_bytes=4 * MIB),
        cost_estimate=pl.CostEstimate(flops=600000000, bytes_accessed=34000000, transcendentals=0),
        name="features",
    )(me, *arrays, in_vmem(projection), *after)


def quarter_start(device, width):
    return pl.multiple_of((2 * (device & 1) + ((device >> 1) & 1)) * width, width)


def slices_kernel(me, targets, *outs):
    for k, out in enumerate(outs):
        width = out.shape[1]
        out[...] = targets[:, pl.ds(quarter_start(me[0] ^ k, width), width)]


def target_slices(me, targets):
    rows, width = targets.shape
    shape = jax.ShapeDtypeStruct((rows, width // NEAR), targets.dtype)
    return pl.pallas_call(
        slices_kernel,
        out_shape=[shape] * NEAR,
        in_specs=[SMEM, VMEM],
        out_specs=[VMEM] * NEAR,
        compiler_params=pltpu.CompilerParams(vmem_limit_bytes=2 * MIB),
        name="target_slices",
    )(me, targets)


def scores_kernel(count, targets, kept, *refs):
    arrived, slices, outs, scale = refs[:count], refs[count : count + NEAR], refs[-1 - NEAR : -1], refs[-1]
    features = kept[...]
    for value in arrived:
        features += value[...].astype(jnp.float32)
    rows, width = slices[0].shape
    examples = features.shape[0]
    high = lax.Precision.HIGHEST
    ones = jnp.ones((rows, width), jnp.float32)
    squares = lax.dot_general(ones, features * features, NT, precision=high, preferred_element_type=jnp.float32)
    rest = jnp.zeros((rows, outs[0].shape[1] - 2 * examples), jnp.float32)
    for side, out in zip(slices, outs):
        dots = lax.dot_general(side[...], features, NT, precision=high, preferred_element_type=jnp.float32)
        out[...] = jnp.concatenate([dots, squares] + ([rest] if rest.shape[1] else []), axis=1)
    mean = jnp.sum(targets[...] * targets[...], axis=1, keepdims=True) / PDIM
    scale[...] = jnp.broadcast_to(lax.rsqrt(mean + 1e-06), scale.shape)


def partial_scores(targets, kept, arrived, slices):
    shape = jax.ShapeDtypeStruct((targets.shape[0], 128), jnp.float32)
    return pl.pallas_call(
        functools.partial(scores_kernel, len(arrived)),
        out_shape=[shape] * (NEAR + 1),
        in_specs=[VMEM] * (2 + len(arrived) + NEAR),
        out_specs=[VMEM] * (NEAR + 1),
        compiler_params=pltpu.CompilerParams(vmem_limit_bytes=6 * MIB),
        name="partial_scores",
    )(targets, kept, *arrived, *slices)


def body(tokens, cotangent, response_loss_mask, adapter_down_weight, projection, targets):
    n = lax.axis_size("shard")
    far = n // NEAR
    me = lax.axis_index("shard").astype(jnp.int32).reshape(1)
    block = adapter_down_weight
    bits = [1 << i for i in range(n.bit_length() - 1)]

    whole = [(tokens, 0, tokens.shape[0]), (cotangent, 0, cotangent.shape[0])]
    whole += [(response_loss_mask.reshape(1, -1), 0, 1), (targets, 0, targets.shape[0])]
    tokens, cotangent, mask, targets = load("load_1", whole, (me,))
    order = [far - 1] + list(range(1, far - 1)) + [0]
    column = [swap(block, NEAR * d, n) for d in order[:-1]] + [block]
    across = [swap(value, 2, n) for value in column]
    places = [[[NEAR * d + k] for d in order] for k in range(NEAR)]
    blocks, owners = column + across[:1] + across[-1:], places[0] + places[2][:1] + places[2][-1:]
    total = partial_lowrank("lowrank_1", me, tokens, blocks, owners)
    picks = [[(i,) for i in range(2 * far)]]
    (gathered,) = join("join_core", column + across, picks, block.shape, (total,))
    other = swap(gathered, 1, n)
    total = partial_lowrank("lowrank_2", me, tokens, across[1:-1], places[2][1:-1], (total,))
    owners = [[k + 1 for part in places[0] + places[2] for k in part]]

    stages = [bits[i : i + 2] for i in range(2, len(bits), 2)] + [bits[:2]]
    left = span([b for stage in stages[1:] for b in stage])
    moves = span(stages[0])
    targets_of = [[m ^ r for r in left] for m in moves]
    rows = packed_grads(me, targets_of, tokens, [other], owners, total, cotangent, mask)
    rows = list(rows)
    rows[-1] = hold("hold_rows", rows[-1], (), HIDE)
    arrays = [swap(array, m, n) for array, m in zip(rows[:0:-1], moves[:0:-1])] + [rows[0]]
    held = {(m, r): (a, i) for a, m in enumerate(moves[::-1]) for i, r in enumerate(left)}
    for number, stage in enumerate(stages[1:]):
        moves, left = span(stage), span([b for later in stages[number + 2 :] for b in later])
        pairs = [[(src, r ^ m) for src in sorted({s for s, _ in held}) for r in left] for m in moves]
        picks = [[held[pair] for pair in group] for group in pairs[1:]]
        sent = join(f"join_rows_{number}", arrays, picks, rows[0].shape[1:])
        came = [swap(array, m, n) for array, m in zip(sent[::-1], moves[:0:-1])]
        kept = {pair: (held[pair][0] + len(came), held[pair][1]) for pair in pairs[0]}
        for a, (m, group) in enumerate(zip(moves[:0:-1], pairs[:0:-1])):
            kept.update({(src ^ m, r ^ m): (a, i) for i, (src, r) in enumerate(group)})
        arrays, held = came + arrays, kept
    slices = target_slices(me, targets)
    slices = [slices[0]] + [swap(slices[k], k, n) for k in range(1, NEAR)]

    places = [held[k, 0] for k in range(n)]
    keep, rest, send = partial_features(me, arrays, places, projection, slices[:0:-1])
    came = swap(send, 1, n).astype(jnp.float32)
    kept, other = keep + came[0], (rest + came[1]).astype(jnp.bfloat16)
    half = kept.astype(jnp.bfloat16)
    arrived = [swap(other if m & 2 else half, m, n) for m in span(bits[1:3])[:0:-1]]
    for bit in bits[3:]:
        for value in arrived:
            kept = kept + value.astype(jnp.float32)
        arrived = [swap(kept.astype(jnp.bfloat16), bit, n)]
    *sums, scale = partial_scores(targets, kept, arrived, slices)
    total = sums[0]
    for k in range(1, NEAR)[::-1]:
        total = total + swap(sums[k], k, n)
    scale = scale[:, :n] * lax.rsqrt(total[:, n : 2 * n] / PDIM + 1e-06)
    return (total[:, :n] * scale / PDIM).T


def solution(mesh):
    in_specs = (
        P(("groups", "shard"), None),
        P(("groups", "shard"), None),
        P(("groups", "shard")),
        P(None, "shard"),
        P("shard", None),
        P(("groups", "shard"), None),
    )
    out_specs = P("groups", "shard")
    return jax.shard_map(body, mesh=mesh, in_specs=in_specs, out_specs=out_specs, check_vma=False)
```

```python
import functools

import jax
import jax.numpy as jnp
from jax import lax
from jax.experimental import pallas as pl
from jax.experimental.pallas import tpu as pltpu
from jax.sharding import PartitionSpec as P

PDIM = 4096
LENGTH = 256
LANES = 256
NEAR = 4
MIB = 1 << 20
HIDE = 30 * 10**9
NT = (((1,), (1,)), ((), ()))
VMEM = pl.BlockSpec(memory_space=pltpu.VMEM)
SMEM = pl.BlockSpec(memory_space=pltpu.SMEM)
ANY = pl.BlockSpec(memory_space=pl.ANY)


def swap(value, bit, n):
    return lax.ppermute(value, "shard", [(s, s ^ bit) for s in range(n)])


def span(bits):
    sums = [0]
    for bit in bits:
        sums += [k + bit for k in sums]
    return sums


def in_hbm(value):
    return pltpu.with_memory_space_constraint(value, pltpu.HBM)


def in_vmem(value):
    return pltpu.with_memory_space_constraint(value, pltpu.VMEM)


def load_kernel(count, starts, *refs):
    sources, outs, sems = refs[:count], refs[-1 - count : -1], refs[-1]
    copies = []
    for source, start, out in zip(sources, starts, outs):
        rows = out.shape[0]
        step = min(rows, LANES // 2)
        for i in range(0, rows, step):
            part = source.at[pl.ds(start + i, step)]
            copies.append(pltpu.make_async_copy(part, out.at[pl.ds(i, step)], sems.at[len(copies)]))
    for copy in copies:
        copy.start()
    for copy in copies:
        copy.wait()


def load(name, parts, after):
    size = sum(rows * array.size // array.shape[0] * array.dtype.itemsize for array, _, rows in parts)
    pieces = sum(max(rows // (LANES // 2), 1) for _, _, rows in parts)
    return pl.pallas_call(
        functools.partial(load_kernel, len(parts), [start for _, start, _ in parts]),
        out_shape=[pltpu.VMEM((rows,) + array.shape[1:], array.dtype) for array, _, rows in parts],
        in_specs=[ANY] * (len(parts) + len(after)),
        out_specs=[VMEM] * len(parts),
        scratch_shapes=[pltpu.SemaphoreType.DMA((pieces,))],
        compiler_params=pltpu.CompilerParams(vmem_limit_bytes=MIB),
        cost_estimate=pl.CostEstimate(flops=0, bytes_accessed=2 * size, transcendentals=0),
        name=name,
    )(*[in_hbm(array) for array, _, _ in parts], *after)


def hold(name, value, after, flops=0):
    return pl.pallas_call(
        lambda *refs: None,
        out_shape=jax.ShapeDtypeStruct(value.shape, value.dtype),
        in_specs=[ANY] * (1 + len(after)),
        out_specs=ANY,
        input_output_aliases={0: 0},
        compiler_params=pltpu.CompilerParams(vmem_limit_bytes=MIB),
        cost_estimate=pl.CostEstimate(flops=flops, bytes_accessed=2000000, transcendentals=0),
        name=name,
    )(value, *after)


def join_kernel(picks, *refs):
    for pick, out in zip(picks, refs[-len(picks) :]):
        for target, (source, *entry) in enumerate(pick):
            out[target] = refs[source][entry[0]] if entry else refs[source][...]


def join(name, values, picks, shape, after=(), flops=0):
    return pl.pallas_call(
        functools.partial(join_kernel, picks),
        out_shape=[jax.ShapeDtypeStruct((len(pick),) + shape, values[0].dtype) for pick in picks],
        in_specs=[VMEM] * len(values) + [ANY] * len(after),
        out_specs=[VMEM] * len(picks),
        compiler_params=pltpu.CompilerParams(vmem_limit_bytes=2 * MIB),
        cost_estimate=pl.CostEstimate(flops=flops, bytes_accessed=2000000, transcendentals=0),
        name=name,
    )(*values, *after)


def add_lowrank(total, me, blocks, places, tokens):
    for block, owners in zip(blocks, places):
        depth = block.shape[-1]
        for i, k in enumerate(owners):
            start = pl.multiple_of((me[0] ^ k) * depth, depth)
            part = block[i] if len(block.shape) == 3 else block[...]
            total += lax.dot_general(part, tokens[:, pl.ds(start, depth)], NT, preferred_element_type=jnp.float32)
    return total


def lowrank_kernel(places, me, tokens, *refs):
    blocks, out = refs[: len(places)], refs[-1]
    before = refs[len(places)][...] if len(refs) > len(places) + 1 else jnp.zeros(out.shape, jnp.float32)
    out[...] = add_lowrank(before, me, blocks, places, tokens)


def partial_lowrank(name, me, tokens, blocks, places, before=()):
    return pl.pallas_call(
        functools.partial(lowrank_kernel, places),
        out_shape=jax.ShapeDtypeStruct((blocks[0].shape[-2], tokens.shape[0]), jnp.float32),
        in_specs=[SMEM] + [VMEM] * (1 + len(blocks) + len(before)),
        out_specs=VMEM,
        compiler_params=pltpu.CompilerParams(vmem_limit_bytes=2 * MIB),
        cost_estimate=pl.CostEstimate(flops=100000000, bytes_accessed=2000000, transcendentals=0),
        name=name,
    )(me, tokens, *blocks, *before)


def grads_kernel(owners, places, me, tokens, *refs):
    blocks = refs[: len(places)]
    before, cotangent, mask = refs[len(places) : len(places) + 3]
    outs, grads = refs[-1 - len(owners) : -1], refs[-1]
    total = add_lowrank(before[...], me, blocks, places, tokens)
    rank = total.shape[0]
    lowrank = total.astype(jnp.bfloat16) * mask[...].astype(jnp.bfloat16)
    turned = jnp.dot(lowrank, cotangent[...], preferred_element_type=jnp.float32)
    grads[...] = turned.T
    pack = LANES // rank
    share = outs[0].shape[1]
    for out, ks in zip(outs, owners):
        for i, k in enumerate(ks):
            start = pl.multiple_of((me[0] ^ k) * (share * pack), share * pack)
            for q in range(pack):
                rows = grads[pl.ds(start + q, share, stride=pack), :]
                out[i, :, q * rank : (q + 1) * rank] = rows.astype(jnp.bfloat16)


def packed_grads(me, owners, tokens, blocks, places, before, cotangent, mask):
    rank, width = blocks[0].shape[-2], cotangent.shape[1]
    share = width * rank // LANES // sum(len(ks) for ks in owners)
    return pl.pallas_call(
        functools.partial(grads_kernel, owners, places),
        out_shape=[jax.ShapeDtypeStruct((len(ks), share, LANES), jnp.bfloat16) for ks in owners],
        in_specs=[SMEM] + [VMEM] * (len(blocks) + 4),
        out_specs=[VMEM] * len(owners),
        scratch_shapes=[pltpu.VMEM((width, rank), jnp.float32)],
        compiler_params=pltpu.CompilerParams(vmem_limit_bytes=6 * MIB),
        cost_estimate=pl.CostEstimate(flops=100000000, bytes_accessed=2000000, transcendentals=0),
        name="grads",
    )(me, tokens, *blocks, before, cotangent, mask)


def features_kernel(places, count, me, *refs):
    arrays, weights = refs[:count], refs[count]
    keep, send, x, left, total = refs[-5:]
    n = len(places)
    share = arrays[0].shape[1]
    pitch = x.shape[1] // n
    for k, (source, entry) in enumerate(places):
        rows = arrays[source][entry]
        place = pl.multiple_of((me[0] ^ k) * pitch, pitch)
        for h in range(x.shape[0]):
            x[h, pl.ds(place, share), :] = rows[:, h * 128 : (h + 1) * 128].astype(jnp.float32)
    for j in range(share):
        for h in range(x.shape[0]):
            at = j * LANES + h * 128
            left[:, at : at + 128] = x[h, pl.ds(j, n, stride=pitch), :].astype(jnp.bfloat16)
    total[...] = jnp.dot(left[...], weights[...], preferred_element_type=jnp.float32)
    part = keep.shape[1]
    mine = pl.multiple_of((me[0] & 1) * part, part)
    partner = pl.multiple_of((1 - (me[0] & 1)) * part, part)
    keep[...] = total[:, pl.ds(mine, part)]
    send[...] = total[:, pl.ds(partner, part)].astype(jnp.bfloat16)


def partial_features(me, arrays, places, projection, after):
    n = len(places)
    share = arrays[0].shape[1]
    depth, width = projection.shape
    half = (n, width // 2)
    return pl.pallas_call(
        functools.partial(features_kernel, places, len(arrays)),
        out_shape=[jax.ShapeDtypeStruct(half, jnp.float32), jax.ShapeDtypeStruct(half, jnp.bfloat16)],
        in_specs=[SMEM] + [VMEM] * (len(arrays) + 1) + [ANY],
        out_specs=[VMEM, VMEM],
        scratch_shapes=[
            pltpu.VMEM((LANES // 128, n * max(share, 8), 128), jnp.float32),
            pltpu.VMEM((n, depth), jnp.bfloat16),
            pltpu.VMEM((n, width), jnp.float32),
        ],
        compiler_params=pltpu.CompilerParams(vmem_limit_bytes=4 * MIB),
        cost_estimate=pl.CostEstimate(flops=600000000, bytes_accessed=34000000, transcendentals=0),
        name="features",
    )(me, *arrays, in_vmem(projection), after)


def scores_kernel(me, targets, partner_targets, kept, *refs):
    mine, send = refs[-2:]
    features = kept[...]
    for arrived in refs[:-2]:
        features += arrived[...].astype(jnp.float32)
    count, half = features.shape
    start = pl.multiple_of((me[0] & 1) * half, half)
    high = lax.Precision.HIGHEST
    ones = jnp.ones((targets.shape[0], half), jnp.float32)
    squares = lax.dot_general(ones, features * features, NT, precision=high, preferred_element_type=jnp.float32)
    rest = jnp.zeros((targets.shape[0], mine.shape[1] - 2 * count), jnp.float32)
    for source, out in ((targets, mine), (partner_targets, send)):
        scale = lax.rsqrt(jnp.sum(source[...] * source[...], axis=1, keepdims=True) / PDIM + 1e-06)
        dots = lax.dot_general(
            source[:, pl.ds(start, half)], features, NT, precision=high, preferred_element_type=jnp.float32
        )
        parts = [dots * scale, squares] + ([rest] if rest.shape[1] else [])
        out[...] = jnp.concatenate(parts, axis=1)


def partial_scores(me, targets, partner_targets, kept, arrived):
    shape = jax.ShapeDtypeStruct((targets.shape[0], 128), jnp.float32)
    return pl.pallas_call(
        scores_kernel,
        out_shape=[shape, shape],
        in_specs=[SMEM] + [VMEM] * (3 + len(arrived)),
        out_specs=[VMEM, VMEM],
        compiler_params=pltpu.CompilerParams(vmem_limit_bytes=6 * MIB),
        name="partial_scores",
    )(me, targets, partner_targets, kept, *arrived)


def body(tokens, cotangent, response_loss_mask, adapter_down_weight, projection, targets):
    n = lax.axis_size("shard")
    far = n // NEAR
    me = lax.axis_index("shard").astype(jnp.int32).reshape(1)
    block = adapter_down_weight
    bits = [1 << i for i in range(n.bit_length() - 1)]

    whole = [(tokens, 0, tokens.shape[0]), (cotangent, 0, cotangent.shape[0])]
    whole += [(response_loss_mask.reshape(1, -1), 0, 1), (targets, 0, targets.shape[0])]
    tokens, cotangent, mask, targets = load("load_1", whole, (me,))
    order = [far - 1] + list(range(1, far - 1)) + [0]
    farthest = swap(block, NEAR * (far - 1), n)
    column = [farthest] + [swap(block, NEAR * d, n) for d in range(1, far // 2)]
    column += [swap(farthest, NEAR * (far - 1 - d), n) for d in range(far // 2, far - 1)] + [block]
    across = [swap(value, 2, n) for value in column]
    places = [[[NEAR * d + k] for d in order] for k in range(NEAR)]
    blocks, owners = column + across[:1] + across[-1:], places[0] + places[2][:1] + places[2][-1:]
    total = partial_lowrank("lowrank_1", me, tokens, blocks, owners)
    picks = [[(i,) for i in range(2 * far)]]
    (gathered,) = join("join_core", column + across, picks, block.shape, (total,))
    other = swap(gathered, 1, n)
    total = partial_lowrank("lowrank_2", me, tokens, across[1:-1], places[2][1:-1], (total,))
    owners = [[k + 1 for part in places[0] + places[2] for k in part]]

    stages = [bits[i : i + 2] for i in range(2, len(bits), 2)] + [bits[:2]]
    left = span([b for stage in stages[1:] for b in stage])
    moves = span(stages[0])
    targets_of = [[m ^ r for r in left] for m in moves]
    rows = packed_grads(me, targets_of, tokens, [other], owners, total, cotangent, mask)
    rows = list(rows)
    rows[-1] = hold("hold_rows", rows[-1], (), HIDE)
    arrays = [swap(array, m, n) for array, m in zip(rows[:0:-1], moves[:0:-1])] + [rows[0]]
    held = {(m, r): (a, i) for a, m in enumerate(moves[::-1]) for i, r in enumerate(left)}
    for number, stage in enumerate(stages[1:]):
        moves, left = span(stage), span([b for later in stages[number + 2 :] for b in later])
        pairs = [[(src, r ^ m) for src in sorted({s for s, _ in held}) for r in left] for m in moves]
        picks = [[held[pair] for pair in group] for group in pairs[1:]]
        sent = join(f"join_rows_{number}", arrays, picks, rows[0].shape[1:])
        came = [swap(array, m, n) for array, m in zip(sent[::-1], moves[:0:-1])]
        kept = {pair: (held[pair][0] + len(came), held[pair][1]) for pair in pairs[0]}
        for a, (m, group) in enumerate(zip(moves[:0:-1], pairs[:0:-1])):
            kept.update({(src ^ m, r ^ m): (a, i) for i, (src, r) in enumerate(group)})
        arrays, held = came + arrays, kept
    partner_targets = swap(targets, 1, n)

    places = [held[k, 0] for k in range(n)]
    kept, send = partial_features(me, arrays, places, projection, partner_targets)
    kept = kept + swap(send, 1, n).astype(jnp.float32)
    for stage in [bits[1:3]] + [[bit] for bit in bits[3:]]:
        half = kept.astype(jnp.bfloat16)
        arrived = [swap(half, m, n) for m in span(stage)[:0:-1]]
        if bits[-1] not in stage:
            for value in arrived:
                kept = kept + value.astype(jnp.float32)
    mine, send = partial_scores(me, targets, partner_targets, kept, arrived)
    total = mine + swap(send, 1, n)
    scale = lax.rsqrt(total[:, n : 2 * n] / PDIM + 1e-06)
    return (total[:, :n] * scale / PDIM).T


def solution(mesh):
    in_specs = (
        P(("groups", "shard"), None),
        P(("groups", "shard"), None),
        P(("groups", "shard")),
        P(None, "shard"),
        P("shard", None),
        P(("groups", "shard"), None),
    )
    out_specs = P("groups", "shard")
    return jax.shard_map(body, mesh=mesh, in_specs=in_specs, out_specs=out_specs, check_vma=False)
```

```python
import functools

import jax
import jax.numpy as jnp
from jax import lax
from jax.experimental import pallas as pl
from jax.experimental.pallas import tpu as pltpu
from jax.sharding import PartitionSpec as P

PDIM = 4096
LENGTH = 256
LANES = 256
NEAR = 4
MIB = 1 << 20
HIDE = 30 * 10**9
NT = (((1,), (1,)), ((), ()))
VMEM = pl.BlockSpec(memory_space=pltpu.VMEM)
SMEM = pl.BlockSpec(memory_space=pltpu.SMEM)
ANY = pl.BlockSpec(memory_space=pl.ANY)


def swap(value, bit, n):
    return lax.ppermute(value, "shard", [(s, s ^ bit) for s in range(n)])


def span(bits):
    sums = [0]
    for bit in bits:
        sums += [k + bit for k in sums]
    return sums


def in_hbm(value):
    return pltpu.with_memory_space_constraint(value, pltpu.HBM)


def in_vmem(value):
    return pltpu.with_memory_space_constraint(value, pltpu.VMEM)


def load_kernel(count, starts, *refs):
    sources, outs, sems = refs[:count], refs[-1 - count : -1], refs[-1]
    copies = []
    for source, start, out in zip(sources, starts, outs):
        rows = out.shape[0]
        step = min(rows, LANES // 2)
        for i in range(0, rows, step):
            part = source.at[pl.ds(start + i, step)]
            copies.append(pltpu.make_async_copy(part, out.at[pl.ds(i, step)], sems.at[len(copies)]))
    for copy in copies:
        copy.start()
    for copy in copies:
        copy.wait()


def load(name, parts, after):
    size = sum(rows * array.size // array.shape[0] * array.dtype.itemsize for array, _, rows in parts)
    pieces = sum(max(rows // (LANES // 2), 1) for _, _, rows in parts)
    return pl.pallas_call(
        functools.partial(load_kernel, len(parts), [start for _, start, _ in parts]),
        out_shape=[pltpu.VMEM((rows,) + array.shape[1:], array.dtype) for array, _, rows in parts],
        in_specs=[ANY] * (len(parts) + len(after)),
        out_specs=[VMEM] * len(parts),
        scratch_shapes=[pltpu.SemaphoreType.DMA((pieces,))],
        compiler_params=pltpu.CompilerParams(vmem_limit_bytes=MIB),
        cost_estimate=pl.CostEstimate(flops=0, bytes_accessed=2 * size, transcendentals=0),
        name=name,
    )(*[in_hbm(array) for array, _, _ in parts], *after)


def hold(name, value, after, flops=0):
    return pl.pallas_call(
        lambda *refs: None,
        out_shape=jax.ShapeDtypeStruct(value.shape, value.dtype),
        in_specs=[ANY] * (1 + len(after)),
        out_specs=ANY,
        input_output_aliases={0: 0},
        compiler_params=pltpu.CompilerParams(vmem_limit_bytes=MIB),
        cost_estimate=pl.CostEstimate(flops=flops, bytes_accessed=2000000, transcendentals=0),
        name=name,
    )(value, *after)


def join_kernel(picks, *refs):
    for pick, out in zip(picks, refs[-len(picks) :]):
        for target, (source, *entry) in enumerate(pick):
            out[target] = refs[source][entry[0]] if entry else refs[source][...]


def join(name, values, picks, shape, after=(), flops=0):
    return pl.pallas_call(
        functools.partial(join_kernel, picks),
        out_shape=[jax.ShapeDtypeStruct((len(pick),) + shape, values[0].dtype) for pick in picks],
        in_specs=[VMEM] * len(values) + [ANY] * len(after),
        out_specs=[VMEM] * len(picks),
        compiler_params=pltpu.CompilerParams(vmem_limit_bytes=2 * MIB),
        cost_estimate=pl.CostEstimate(flops=flops, bytes_accessed=2000000, transcendentals=0),
        name=name,
    )(*values, *after)


def add_lowrank(total, me, blocks, places, tokens):
    for block, owners in zip(blocks, places):
        depth = block.shape[-1]
        for i, k in enumerate(owners):
            start = pl.multiple_of((me[0] ^ k) * depth, depth)
            part = block[i] if len(block.shape) == 3 else block[...]
            total += lax.dot_general(part, tokens[:, pl.ds(start, depth)], NT, preferred_element_type=jnp.float32)
    return total


def lowrank_kernel(places, me, tokens, *refs):
    blocks, out = refs[: len(places)], refs[-1]
    before = refs[len(places)][...] if len(refs) > len(places) + 1 else jnp.zeros(out.shape, jnp.float32)
    out[...] = add_lowrank(before, me, blocks, places, tokens)


def partial_lowrank(name, me, tokens, blocks, places, before=()):
    return pl.pallas_call(
        functools.partial(lowrank_kernel, places),
        out_shape=jax.ShapeDtypeStruct((blocks[0].shape[-2], tokens.shape[0]), jnp.float32),
        in_specs=[SMEM] + [VMEM] * (1 + len(blocks) + len(before)),
        out_specs=VMEM,
        compiler_params=pltpu.CompilerParams(vmem_limit_bytes=2 * MIB),
        cost_estimate=pl.CostEstimate(flops=100000000, bytes_accessed=2000000, transcendentals=0),
        name=name,
    )(me, tokens, *blocks, *before)


def turn_kernel(owners, pack, me, cotangent, *refs):
    outs, turned, stage = refs[-2 - pack : -2], refs[-2], refs[-1]
    order = [k for ks in owners for k in ks]
    share = stage.shape[0] // len(order)
    for h in range(turned.shape[0]):
        turned[h] = cotangent[h * 128 : (h + 1) * 128, :].astype(jnp.float32).T
    for q, out in enumerate(outs):
        for h in range(turned.shape[0]):
            for i, k in enumerate(order):
                start = pl.multiple_of((me[0] ^ k) * (share * pack), share * pack)
                stage[i * share : (i + 1) * share, :] = turned[h, pl.ds(start + q, share, stride=pack), :]
            out[:, h * 128 : (h + 1) * 128] = stage[...].astype(jnp.bfloat16)


def turned_cotangent(me, owners, rank, cotangent, after):
    tokens, width = cotangent.shape
    pack = LANES // rank
    return pl.pallas_call(
        functools.partial(turn_kernel, owners, pack),
        out_shape=[jax.ShapeDtypeStruct((width // pack, tokens), jnp.bfloat16)] * pack,
        in_specs=[SMEM, VMEM] + [ANY] * len(after),
        out_specs=[VMEM] * pack,
        scratch_shapes=[
            pltpu.VMEM((tokens // 128, width, 128), jnp.float32),
            pltpu.VMEM((width // pack, 128), jnp.float32),
        ],
        compiler_params=pltpu.CompilerParams(vmem_limit_bytes=6 * MIB),
        cost_estimate=pl.CostEstimate(flops=100000000, bytes_accessed=2000000, transcendentals=0),
        name="turn",
    )(me, cotangent, *after)


def grads_kernel(owners, places, me, tokens, *refs):
    blocks, outs = refs[: len(places)], refs[-len(owners) :]
    before, mask = refs[len(places) : len(places) + 2]
    turned = refs[len(places) + 2 : -len(owners)]
    total = add_lowrank(before[...], me, blocks, places, tokens)
    lowrank = total.astype(jnp.bfloat16) * mask[...].astype(jnp.bfloat16)
    parts = [lax.dot_general(rows[...], lowrank, NT, preferred_element_type=jnp.float32) for rows in turned]
    packed = jnp.concatenate(parts, axis=1)
    share = outs[0].shape[1]
    row = 0
    for out in outs:
        for i in range(out.shape[0]):
            out[i] = packed[row : row + share, :].astype(jnp.bfloat16)
            row += share


def packed_grads(me, owners, tokens, blocks, places, before, turned, mask):
    share = turned[0].shape[0] // sum(len(ks) for ks in owners)
    return pl.pallas_call(
        functools.partial(grads_kernel, owners, places),
        out_shape=[jax.ShapeDtypeStruct((len(ks), share, LANES), jnp.bfloat16) for ks in owners],
        in_specs=[SMEM] + [VMEM] * (len(blocks) + 3 + len(turned)),
        out_specs=[VMEM] * len(owners),
        compiler_params=pltpu.CompilerParams(vmem_limit_bytes=6 * MIB),
        cost_estimate=pl.CostEstimate(flops=100000000, bytes_accessed=2000000, transcendentals=0),
        name="grads",
    )(me, tokens, *blocks, before, mask, *turned)


def features_kernel(places, count, me, *refs):
    arrays, weights = refs[:count], refs[count]
    keep, send, x, left, total = refs[-5:]
    n = len(places)
    share = arrays[0].shape[1]
    pitch = x.shape[1] // n
    for k, (source, entry) in enumerate(places):
        rows = arrays[source][entry]
        place = pl.multiple_of((me[0] ^ k) * pitch, pitch)
        for h in range(x.shape[0]):
            x[h, pl.ds(place, share), :] = rows[:, h * 128 : (h + 1) * 128].astype(jnp.float32)
    for j in range(share):
        for h in range(x.shape[0]):
            at = j * LANES + h * 128
            left[:, at : at + 128] = x[h, pl.ds(j, n, stride=pitch), :].astype(jnp.bfloat16)
    total[...] = jnp.dot(left[...], weights[...], preferred_element_type=jnp.float32)
    part = keep.shape[1]
    mine = pl.multiple_of((me[0] & 1) * part, part)
    partner = pl.multiple_of((1 - (me[0] & 1)) * part, part)
    keep[...] = total[:, pl.ds(mine, part)]
    send[...] = total[:, pl.ds(partner, part)].astype(jnp.bfloat16)


def partial_features(me, arrays, places, projection, after):
    n = len(places)
    share = arrays[0].shape[1]
    depth, width = projection.shape
    half = (n, width // 2)
    return pl.pallas_call(
        functools.partial(features_kernel, places, len(arrays)),
        out_shape=[jax.ShapeDtypeStruct(half, jnp.float32), jax.ShapeDtypeStruct(half, jnp.bfloat16)],
        in_specs=[SMEM] + [VMEM] * (len(arrays) + 1) + [ANY],
        out_specs=[VMEM, VMEM],
        scratch_shapes=[
            pltpu.VMEM((LANES // 128, n * max(share, 8), 128), jnp.float32),
            pltpu.VMEM((n, depth), jnp.bfloat16),
            pltpu.VMEM((n, width), jnp.float32),
        ],
        compiler_params=pltpu.CompilerParams(vmem_limit_bytes=4 * MIB),
        cost_estimate=pl.CostEstimate(flops=600000000, bytes_accessed=34000000, transcendentals=0),
        name="features",
    )(me, *arrays, in_vmem(projection), after)


def scores_kernel(me, targets, partner_targets, kept, *refs):
    mine, send = refs[-2:]
    features = kept[...]
    for arrived in refs[:-2]:
        features += arrived[...].astype(jnp.float32)
    count, half = features.shape
    start = pl.multiple_of((me[0] & 1) * half, half)
    high = lax.Precision.HIGHEST
    ones = jnp.ones((targets.shape[0], half), jnp.float32)
    squares = lax.dot_general(ones, features * features, NT, precision=high, preferred_element_type=jnp.float32)
    rest = jnp.zeros((targets.shape[0], mine.shape[1] - 2 * count), jnp.float32)
    for source, out in ((targets, mine), (partner_targets, send)):
        scale = lax.rsqrt(jnp.sum(source[...] * source[...], axis=1, keepdims=True) / PDIM + 1e-06)
        dots = lax.dot_general(
            source[:, pl.ds(start, half)], features, NT, precision=high, preferred_element_type=jnp.float32
        )
        parts = [dots * scale, squares] + ([rest] if rest.shape[1] else [])
        out[...] = jnp.concatenate(parts, axis=1)


def partial_scores(me, targets, partner_targets, kept, arrived):
    shape = jax.ShapeDtypeStruct((targets.shape[0], 128), jnp.float32)
    return pl.pallas_call(
        scores_kernel,
        out_shape=[shape, shape],
        in_specs=[SMEM] + [VMEM] * (3 + len(arrived)),
        out_specs=[VMEM, VMEM],
        compiler_params=pltpu.CompilerParams(vmem_limit_bytes=6 * MIB),
        name="partial_scores",
    )(me, targets, partner_targets, kept, *arrived)


def body(tokens, cotangent, response_loss_mask, adapter_down_weight, projection, targets):
    n = lax.axis_size("shard")
    far = n // NEAR
    me = lax.axis_index("shard").astype(jnp.int32).reshape(1)
    block = adapter_down_weight
    bits = [1 << i for i in range(n.bit_length() - 1)]

    whole = [(tokens, 0, tokens.shape[0]), (cotangent, 0, cotangent.shape[0])]
    whole += [(response_loss_mask.reshape(1, -1), 0, 1), (targets, 0, targets.shape[0])]
    tokens, cotangent, mask, targets = load("load_1", whole, (me,))
    order = [far - 1] + list(range(1, far - 1)) + [0]
    column = [swap(block, NEAR * d, n) for d in order[:-1]] + [block]
    across = [swap(value, 2, n) for value in column]
    places = [[[NEAR * d + k] for d in order] for k in range(NEAR)]
    blocks, owners = column + across[:1] + across[-1:], places[0] + places[2][:1] + places[2][-1:]
    total = partial_lowrank("lowrank_1", me, tokens, blocks, owners)
    picks = [[(i,) for i in range(2 * far)]]
    (gathered,) = join("join_core", column + across, picks, block.shape, (total,))
    other = swap(gathered, 1, n)
    total = partial_lowrank("lowrank_2", me, tokens, across[1:-1], places[2][1:-1], (total,))
    owners = [[k + 1 for part in places[0] + places[2] for k in part]]

    stages = [bits[i : i + 2] for i in range(2, len(bits), 2)] + [bits[:2]]
    left = span([b for stage in stages[1:] for b in stage])
    moves = span(stages[0])
    targets_of = [[m ^ r for r in left] for m in moves]
    turned = turned_cotangent(me, targets_of, block.shape[0], cotangent, (gathered,))
    rows = packed_grads(me, targets_of, tokens, [other], owners, total, turned, mask)
    rows = list(rows)
    rows[-1] = hold("hold_rows", rows[-1], (), HIDE)
    arrays = [swap(array, m, n) for array, m in zip(rows[:0:-1], moves[:0:-1])] + [rows[0]]
    held = {(m, r): (a, i) for a, m in enumerate(moves[::-1]) for i, r in enumerate(left)}
    for number, stage in enumerate(stages[1:]):
        moves, left = span(stage), span([b for later in stages[number + 2 :] for b in later])
        pairs = [[(src, r ^ m) for src in sorted({s for s, _ in held}) for r in left] for m in moves]
        picks = [[held[pair] for pair in group] for group in pairs[1:]]
        sent = join(f"join_rows_{number}", arrays, picks, rows[0].shape[1:])
        came = [swap(array, m, n) for array, m in zip(sent[::-1], moves[:0:-1])]
        kept = {pair: (held[pair][0] + len(came), held[pair][1]) for pair in pairs[0]}
        for a, (m, group) in enumerate(zip(moves[:0:-1], pairs[:0:-1])):
            kept.update({(src ^ m, r ^ m): (a, i) for i, (src, r) in enumerate(group)})
        arrays, held = came + arrays, kept
    partner_targets = swap(targets, 1, n)

    places = [held[k, 0] for k in range(n)]
    kept, send = partial_features(me, arrays, places, projection, partner_targets)
    kept = kept + swap(send, 1, n).astype(jnp.float32)
    for stage in [bits[1:3]] + [[bit] for bit in bits[3:]]:
        half = kept.astype(jnp.bfloat16)
        arrived = [swap(half, m, n) for m in span(stage)[:0:-1]]
        if bits[-1] not in stage:
            for value in arrived:
                kept = kept + value.astype(jnp.float32)
    mine, send = partial_scores(me, targets, partner_targets, kept, arrived)
    total = mine + swap(send, 1, n)
    scale = lax.rsqrt(total[:, n : 2 * n] / PDIM + 1e-06)
    return (total[:, :n] * scale / PDIM).T


def solution(mesh):
    in_specs = (
        P(("groups", "shard"), None),
        P(("groups", "shard"), None),
        P(("groups", "shard")),
        P(None, "shard"),
        P("shard", None),
        P(("groups", "shard"), None),
    )
    out_specs = P("groups", "shard")
    return jax.shard_map(body, mesh=mesh, in_specs=in_specs, out_specs=out_specs, check_vma=False)
```

```python
import functools

import jax
import jax.numpy as jnp
from jax import lax
from jax.experimental import pallas as pl
from jax.experimental.pallas import tpu as pltpu
from jax.sharding import PartitionSpec as P

PDIM = 4096
LENGTH = 256
LANES = 256
NEAR = 4
MIB = 1 << 20
HIDE = 30 * 10**9
NT = (((1,), (1,)), ((), ()))
VMEM = pl.BlockSpec(memory_space=pltpu.VMEM)
SMEM = pl.BlockSpec(memory_space=pltpu.SMEM)
ANY = pl.BlockSpec(memory_space=pl.ANY)


def swap(value, bit, n):
    return lax.ppermute(value, "shard", [(s, s ^ bit) for s in range(n)])


def span(bits):
    sums = [0]
    for bit in bits:
        sums += [k + bit for k in sums]
    return sums


def in_hbm(value):
    return pltpu.with_memory_space_constraint(value, pltpu.HBM)


def in_vmem(value):
    return pltpu.with_memory_space_constraint(value, pltpu.VMEM)


def load_kernel(count, starts, *refs):
    sources, outs, sems = refs[:count], refs[-1 - count : -1], refs[-1]
    copies = []
    for source, start, out in zip(sources, starts, outs):
        rows = out.shape[0]
        step = min(rows, LANES // 2)
        for i in range(0, rows, step):
            part = source.at[pl.ds(start + i, step)]
            copies.append(pltpu.make_async_copy(part, out.at[pl.ds(i, step)], sems.at[len(copies)]))
    for copy in copies:
        copy.start()
    for copy in copies:
        copy.wait()


def load(name, parts, after):
    size = sum(rows * array.size // array.shape[0] * array.dtype.itemsize for array, _, rows in parts)
    pieces = sum(max(rows // (LANES // 2), 1) for _, _, rows in parts)
    return pl.pallas_call(
        functools.partial(load_kernel, len(parts), [start for _, start, _ in parts]),
        out_shape=[pltpu.VMEM((rows,) + array.shape[1:], array.dtype) for array, _, rows in parts],
        in_specs=[ANY] * (len(parts) + len(after)),
        out_specs=[VMEM] * len(parts),
        scratch_shapes=[pltpu.SemaphoreType.DMA((pieces,))],
        compiler_params=pltpu.CompilerParams(vmem_limit_bytes=MIB),
        cost_estimate=pl.CostEstimate(flops=0, bytes_accessed=2 * size, transcendentals=0),
        name=name,
    )(*[in_hbm(array) for array, _, _ in parts], *after)


def hold(name, value, after, flops=0):
    return pl.pallas_call(
        lambda *refs: None,
        out_shape=jax.ShapeDtypeStruct(value.shape, value.dtype),
        in_specs=[ANY] * (1 + len(after)),
        out_specs=ANY,
        input_output_aliases={0: 0},
        compiler_params=pltpu.CompilerParams(vmem_limit_bytes=MIB),
        cost_estimate=pl.CostEstimate(flops=flops, bytes_accessed=2000000, transcendentals=0),
        name=name,
    )(value, *after)


def join_kernel(picks, *refs):
    for pick, out in zip(picks, refs[-len(picks) :]):
        for target, (source, *entry) in enumerate(pick):
            out[target] = refs[source][entry[0]] if entry else refs[source][...]


def join(name, values, picks, shape, after=(), flops=0):
    return pl.pallas_call(
        functools.partial(join_kernel, picks),
        out_shape=[jax.ShapeDtypeStruct((len(pick),) + shape, values[0].dtype) for pick in picks],
        in_specs=[VMEM] * len(values) + [ANY] * len(after),
        out_specs=[VMEM] * len(picks),
        compiler_params=pltpu.CompilerParams(vmem_limit_bytes=2 * MIB),
        cost_estimate=pl.CostEstimate(flops=flops, bytes_accessed=2000000, transcendentals=0),
        name=name,
    )(*values, *after)


def add_lowrank(total, me, blocks, places, tokens):
    for block, owners in zip(blocks, places):
        depth = block.shape[-1]
        for i, k in enumerate(owners):
            start = pl.multiple_of((me[0] ^ k) * depth, depth)
            part = block[i] if len(block.shape) == 3 else block[...]
            total += lax.dot_general(part, tokens[:, pl.ds(start, depth)], NT, preferred_element_type=jnp.float32)
    return total


def lowrank_kernel(places, me, tokens, *refs):
    blocks, out = refs[: len(places)], refs[-1]
    before = refs[len(places)][...] if len(refs) > len(places) + 1 else jnp.zeros(out.shape, jnp.float32)
    out[...] = add_lowrank(before, me, blocks, places, tokens)


def partial_lowrank(name, me, tokens, blocks, places, before=()):
    return pl.pallas_call(
        functools.partial(lowrank_kernel, places),
        out_shape=jax.ShapeDtypeStruct((blocks[0].shape[-2], tokens.shape[0]), jnp.float32),
        in_specs=[SMEM] + [VMEM] * (1 + len(blocks) + len(before)),
        out_specs=VMEM,
        compiler_params=pltpu.CompilerParams(vmem_limit_bytes=2 * MIB),
        cost_estimate=pl.CostEstimate(flops=100000000, bytes_accessed=2000000, transcendentals=0),
        name=name,
    )(me, tokens, *blocks, *before)


def turn_kernel(owners, pack, me, cotangent, *refs):
    outs, turned, stage = refs[-2 - pack : -2], refs[-2], refs[-1]
    order = [k for ks in owners for k in ks]
    share = stage.shape[0] // len(order)
    for h in range(turned.shape[0]):
        turned[h] = cotangent[h * 128 : (h + 1) * 128, :].astype(jnp.float32).T
    for q, out in enumerate(outs):
        for h in range(turned.shape[0]):
            for i, k in enumerate(order):
                start = pl.multiple_of((me[0] ^ k) * (share * pack), share * pack)
                stage[i * share : (i + 1) * share, :] = turned[h, pl.ds(start + q, share, stride=pack), :]
            out[:, h * 128 : (h + 1) * 128] = stage[...].astype(jnp.bfloat16)


def turned_cotangent(me, owners, rank, cotangent, after):
    tokens, width = cotangent.shape
    pack = LANES // rank
    return pl.pallas_call(
        functools.partial(turn_kernel, owners, pack),
        out_shape=[jax.ShapeDtypeStruct((width // pack, tokens), jnp.bfloat16)] * pack,
        in_specs=[SMEM, VMEM] + [ANY] * len(after),
        out_specs=[VMEM] * pack,
        scratch_shapes=[
            pltpu.VMEM((tokens // 128, width, 128), jnp.float32),
            pltpu.VMEM((width // pack, 128), jnp.float32),
        ],
        compiler_params=pltpu.CompilerParams(vmem_limit_bytes=6 * MIB),
        cost_estimate=pl.CostEstimate(flops=100000000, bytes_accessed=2000000, transcendentals=0),
        name="turn",
    )(me, cotangent, *after)


def grads_kernel(owners, places, me, tokens, *refs):
    blocks, outs = refs[: len(places)], refs[-len(owners) :]
    before, mask = refs[len(places) : len(places) + 2]
    turned = refs[len(places) + 2 : -len(owners)]
    total = add_lowrank(before[...], me, blocks, places, tokens)
    lowrank = total.astype(jnp.bfloat16) * mask[...].astype(jnp.bfloat16)
    parts = [lax.dot_general(rows[...], lowrank, NT, preferred_element_type=jnp.float32) for rows in turned]
    packed = jnp.concatenate(parts, axis=1)
    share = outs[0].shape[1]
    row = 0
    for out in outs:
        for i in range(out.shape[0]):
            out[i] = packed[row : row + share, :].astype(jnp.bfloat16)
            row += share


def packed_grads(me, owners, tokens, blocks, places, before, turned, mask):
    share = turned[0].shape[0] // sum(len(ks) for ks in owners)
    return pl.pallas_call(
        functools.partial(grads_kernel, owners, places),
        out_shape=[jax.ShapeDtypeStruct((len(ks), share, LANES), jnp.bfloat16) for ks in owners],
        in_specs=[SMEM] + [VMEM] * (len(blocks) + 3 + len(turned)),
        out_specs=[VMEM] * len(owners),
        compiler_params=pltpu.CompilerParams(vmem_limit_bytes=6 * MIB),
        cost_estimate=pl.CostEstimate(flops=100000000, bytes_accessed=2000000, transcendentals=0),
        name="grads",
    )(me, tokens, *blocks, before, mask, *turned)


def features_kernel(places, count, me, *refs):
    arrays, weights = refs[:count], refs[count]
    keep, send, x, left, total = refs[-5:]
    n = len(places)
    share = arrays[0].shape[1]
    pitch = x.shape[1] // n
    for k, (source, entry) in enumerate(places):
        rows = arrays[source][entry]
        place = pl.multiple_of((me[0] ^ k) * pitch, pitch)
        for h in range(x.shape[0]):
            x[h, pl.ds(place, share), :] = rows[:, h * 128 : (h + 1) * 128].astype(jnp.float32)
    for j in range(share):
        for h in range(x.shape[0]):
            at = j * LANES + h * 128
            left[:, at : at + 128] = x[h, pl.ds(j, n, stride=pitch), :].astype(jnp.bfloat16)
    total[...] = jnp.dot(left[...], weights[...], preferred_element_type=jnp.float32)
    part = keep.shape[1]
    mine = pl.multiple_of((me[0] & 1) * part, part)
    partner = pl.multiple_of((1 - (me[0] & 1)) * part, part)
    keep[...] = total[:, pl.ds(mine, part)]
    send[...] = total[:, pl.ds(partner, part)].astype(jnp.bfloat16)


def partial_features(me, arrays, places, projection, after):
    n = len(places)
    share = arrays[0].shape[1]
    depth, width = projection.shape
    half = (n, width // 2)
    return pl.pallas_call(
        functools.partial(features_kernel, places, len(arrays)),
        out_shape=[jax.ShapeDtypeStruct(half, jnp.float32), jax.ShapeDtypeStruct(half, jnp.bfloat16)],
        in_specs=[SMEM] + [VMEM] * (len(arrays) + 1) + [ANY],
        out_specs=[VMEM, VMEM],
        scratch_shapes=[
            pltpu.VMEM((LANES // 128, n * max(share, 8), 128), jnp.float32),
            pltpu.VMEM((n, depth), jnp.bfloat16),
            pltpu.VMEM((n, width), jnp.float32),
        ],
        compiler_params=pltpu.CompilerParams(vmem_limit_bytes=4 * MIB),
        cost_estimate=pl.CostEstimate(flops=600000000, bytes_accessed=34000000, transcendentals=0),
        name="features",
    )(me, *arrays, in_vmem(projection), after)


def scores_kernel(me, targets, partner_targets, kept, *refs):
    mine, send = refs[-2:]
    features = kept[...]
    for arrived in refs[:-2]:
        features += arrived[...].astype(jnp.float32)
    count, half = features.shape
    start = pl.multiple_of((me[0] & 1) * half, half)
    high = lax.Precision.HIGHEST
    ones = jnp.ones((targets.shape[0], half), jnp.float32)
    squares = lax.dot_general(ones, features * features, NT, precision=high, preferred_element_type=jnp.float32)
    rest = jnp.zeros((targets.shape[0], mine.shape[1] - 2 * count), jnp.float32)
    for source, out in ((targets, mine), (partner_targets, send)):
        scale = lax.rsqrt(jnp.sum(source[...] * source[...], axis=1, keepdims=True) / PDIM + 1e-06)
        dots = lax.dot_general(
            source[:, pl.ds(start, half)], features, NT, precision=high, preferred_element_type=jnp.float32
        )
        parts = [dots * scale, squares] + ([rest] if rest.shape[1] else [])
        out[...] = jnp.concatenate(parts, axis=1)


def partial_scores(me, targets, partner_targets, kept, arrived):
    shape = jax.ShapeDtypeStruct((targets.shape[0], 128), jnp.float32)
    return pl.pallas_call(
        scores_kernel,
        out_shape=[shape, shape],
        in_specs=[SMEM] + [VMEM] * (3 + len(arrived)),
        out_specs=[VMEM, VMEM],
        compiler_params=pltpu.CompilerParams(vmem_limit_bytes=6 * MIB),
        name="partial_scores",
    )(me, targets, partner_targets, kept, *arrived)


def body(tokens, cotangent, response_loss_mask, adapter_down_weight, projection, targets):
    n = lax.axis_size("shard")
    far = n // NEAR
    me = lax.axis_index("shard").astype(jnp.int32).reshape(1)
    block = adapter_down_weight
    bits = [1 << i for i in range(n.bit_length() - 1)]

    whole = [(tokens, 0, tokens.shape[0]), (cotangent, 0, cotangent.shape[0])]
    whole += [(response_loss_mask.reshape(1, -1), 0, 1), (targets, 0, targets.shape[0])]
    tokens, cotangent, mask, targets = load("load_1", whole, (me,))
    order = [far - 1] + list(range(1, far - 1)) + [0]
    column = [swap(block, NEAR * d, n) for d in order[:-1]] + [block]
    across = [swap(value, 2, n) for value in column]
    places = [[[NEAR * d + k] for d in order] for k in range(NEAR)]
    blocks, owners = column + across[:1] + across[-1:], places[0] + places[2][:1] + places[2][-1:]
    total = partial_lowrank("lowrank_1", me, tokens, blocks, owners)
    picks = [[(i,) for i in range(far)]]
    (line,) = join("join_column", column, picks, block.shape, (total,))
    (gathered,) = join("join_across", across, picks, block.shape)
    other = [swap(line, 1, n), swap(gathered, 1, n)]
    total = partial_lowrank("lowrank_2", me, tokens, across[1:-1], places[2][1:-1], (total,))
    owners = [[k + 1 for part in side for k in part] for side in (places[0], places[2])]
    total = partial_lowrank("lowrank_3", me, tokens, other[:1], owners[:1], (total,))

    stages = [bits[i : i + 2] for i in range(2, len(bits), 2)] + [bits[:2]]
    left = span([b for stage in stages[1:] for b in stage])
    moves = span(stages[0])
    targets_of = [[m ^ r for r in left] for m in moves]
    turned = turned_cotangent(me, targets_of, block.shape[0], cotangent, (gathered,))
    rows = packed_grads(me, targets_of, tokens, other[1:], owners[1:], total, turned, mask)
    rows = list(rows)
    rows[-1] = hold("hold_rows", rows[-1], (), HIDE)
    arrays = [swap(array, m, n) for array, m in zip(rows[:0:-1], moves[:0:-1])] + [rows[0]]
    held = {(m, r): (a, i) for a, m in enumerate(moves[::-1]) for i, r in enumerate(left)}
    for number, stage in enumerate(stages[1:]):
        moves, left = span(stage), span([b for later in stages[number + 2 :] for b in later])
        pairs = [[(src, r ^ m) for src in sorted({s for s, _ in held}) for r in left] for m in moves]
        picks = [[held[pair] for pair in group] for group in pairs[1:]]
        sent = join(f"join_rows_{number}", arrays, picks, rows[0].shape[1:])
        came = [swap(array, m, n) for array, m in zip(sent[::-1], moves[:0:-1])]
        kept = {pair: (held[pair][0] + len(came), held[pair][1]) for pair in pairs[0]}
        for a, (m, group) in enumerate(zip(moves[:0:-1], pairs[:0:-1])):
            kept.update({(src ^ m, r ^ m): (a, i) for i, (src, r) in enumerate(group)})
        arrays, held = came + arrays, kept
    partner_targets = swap(targets, 1, n)

    places = [held[k, 0] for k in range(n)]
    kept, send = partial_features(me, arrays, places, projection, partner_targets)
    kept = kept + swap(send, 1, n).astype(jnp.float32)
    for stage in [bits[1:3]] + [[bit] for bit in bits[3:]]:
        half = kept.astype(jnp.bfloat16)
        arrived = [swap(half, m, n) for m in span(stage)[:0:-1]]
        if bits[-1] not in stage:
            for value in arrived:
                kept = kept + value.astype(jnp.float32)
    mine, send = partial_scores(me, targets, partner_targets, kept, arrived)
    total = mine + swap(send, 1, n)
    scale = lax.rsqrt(total[:, n : 2 * n] / PDIM + 1e-06)
    return (total[:, :n] * scale / PDIM).T


def solution(mesh):
    in_specs = (
        P(("groups", "shard"), None),
        P(("groups", "shard"), None),
        P(("groups", "shard")),
        P(None, "shard"),
        P("shard", None),
        P(("groups", "shard"), None),
    )
    out_specs = P("groups", "shard")
    return jax.shard_map(body, mesh=mesh, in_specs=in_specs, out_specs=out_specs, check_vma=False)
```

```python
import functools

import jax
import jax.numpy as jnp
from jax import lax
from jax.experimental import pallas as pl
from jax.experimental.pallas import tpu as pltpu
from jax.sharding import PartitionSpec as P

PDIM = 4096
LENGTH = 256
LANES = 256
NEAR = 4
MIB = 1 << 20
HIDE = 30 * 10**9
NT = (((1,), (1,)), ((), ()))
VMEM = pl.BlockSpec(memory_space=pltpu.VMEM)
SMEM = pl.BlockSpec(memory_space=pltpu.SMEM)
ANY = pl.BlockSpec(memory_space=pl.ANY)


def swap(value, bit, n):
    return lax.ppermute(value, "shard", [(s, s ^ bit) for s in range(n)])


def span(bits):
    sums = [0]
    for bit in bits:
        sums += [k + bit for k in sums]
    return sums


def in_hbm(value):
    return pltpu.with_memory_space_constraint(value, pltpu.HBM)


def in_vmem(value):
    return pltpu.with_memory_space_constraint(value, pltpu.VMEM)


def load_kernel(count, starts, *refs):
    sources, outs, sems = refs[:count], refs[-1 - count : -1], refs[-1]
    copies = []
    for source, start, out in zip(sources, starts, outs):
        rows = out.shape[0]
        step = min(rows, LANES // 2)
        for i in range(0, rows, step):
            part = source.at[pl.ds(start + i, step)]
            copies.append(pltpu.make_async_copy(part, out.at[pl.ds(i, step)], sems.at[len(copies)]))
    for copy in copies:
        copy.start()
    for copy in copies:
        copy.wait()


def load(name, parts, after):
    size = sum(rows * array.size // array.shape[0] * array.dtype.itemsize for array, _, rows in parts)
    pieces = sum(max(rows // (LANES // 2), 1) for _, _, rows in parts)
    return pl.pallas_call(
        functools.partial(load_kernel, len(parts), [start for _, start, _ in parts]),
        out_shape=[pltpu.VMEM((rows,) + array.shape[1:], array.dtype) for array, _, rows in parts],
        in_specs=[ANY] * (len(parts) + len(after)),
        out_specs=[VMEM] * len(parts),
        scratch_shapes=[pltpu.SemaphoreType.DMA((pieces,))],
        compiler_params=pltpu.CompilerParams(vmem_limit_bytes=MIB),
        cost_estimate=pl.CostEstimate(flops=0, bytes_accessed=2 * size, transcendentals=0),
        name=name,
    )(*[in_hbm(array) for array, _, _ in parts], *after)


def hold(name, value, after, flops=0):
    return pl.pallas_call(
        lambda *refs: None,
        out_shape=jax.ShapeDtypeStruct(value.shape, value.dtype),
        in_specs=[ANY] * (1 + len(after)),
        out_specs=ANY,
        input_output_aliases={0: 0},
        compiler_params=pltpu.CompilerParams(vmem_limit_bytes=MIB),
        cost_estimate=pl.CostEstimate(flops=flops, bytes_accessed=2000000, transcendentals=0),
        name=name,
    )(value, *after)


def join_kernel(picks, *refs):
    for pick, out in zip(picks, refs[-len(picks) :]):
        for target, (source, *entry) in enumerate(pick):
            out[target] = refs[source][entry[0]] if entry else refs[source][...]


def join(name, values, picks, shape, after=(), flops=0):
    return pl.pallas_call(
        functools.partial(join_kernel, picks),
        out_shape=[jax.ShapeDtypeStruct((len(pick),) + shape, values[0].dtype) for pick in picks],
        in_specs=[VMEM] * len(values) + [ANY] * len(after),
        out_specs=[VMEM] * len(picks),
        compiler_params=pltpu.CompilerParams(vmem_limit_bytes=2 * MIB),
        cost_estimate=pl.CostEstimate(flops=flops, bytes_accessed=2000000, transcendentals=0),
        name=name,
    )(*values, *after)


def add_lowrank(total, me, blocks, places, tokens):
    for block, owners in zip(blocks, places):
        depth = block.shape[-1]
        for i, k in enumerate(owners):
            start = pl.multiple_of((me[0] ^ k) * depth, depth)
            part = block[i] if len(block.shape) == 3 else block[...]
            total += lax.dot_general(part, tokens[:, pl.ds(start, depth)], NT, preferred_element_type=jnp.float32)
    return total


def lowrank_kernel(places, me, tokens, *refs):
    blocks, out = refs[: len(places)], refs[-1]
    before = refs[len(places)][...] if len(refs) > len(places) + 1 else jnp.zeros(out.shape, jnp.float32)
    out[...] = add_lowrank(before, me, blocks, places, tokens)


def partial_lowrank(name, me, tokens, blocks, places, before=()):
    return pl.pallas_call(
        functools.partial(lowrank_kernel, places),
        out_shape=jax.ShapeDtypeStruct((blocks[0].shape[-2], tokens.shape[0]), jnp.float32),
        in_specs=[SMEM] + [VMEM] * (1 + len(blocks) + len(before)),
        out_specs=VMEM,
        compiler_params=pltpu.CompilerParams(vmem_limit_bytes=2 * MIB),
        cost_estimate=pl.CostEstimate(flops=100000000, bytes_accessed=2000000, transcendentals=0),
        name=name,
    )(me, tokens, *blocks, *before)


def grads_kernel(owners, places, me, tokens, *refs):
    blocks = refs[: len(places)]
    before, cotangent, mask = refs[len(places) : len(places) + 3]
    outs, grads = refs[-1 - len(owners) : -1], refs[-1]
    total = add_lowrank(before[...], me, blocks, places, tokens)
    rank = total.shape[0]
    lowrank = total.astype(jnp.bfloat16) * mask[...].astype(jnp.bfloat16)
    turned = jnp.dot(lowrank, cotangent[...], preferred_element_type=jnp.float32)
    grads[...] = turned.T
    pack = LANES // rank
    share = outs[0].shape[1]
    for out, ks in zip(outs, owners):
        for i, k in enumerate(ks):
            start = pl.multiple_of((me[0] ^ k) * (share * pack), share * pack)
            for q in range(pack):
                rows = grads[pl.ds(start + q, share, stride=pack), :]
                out[i, :, q * rank : (q + 1) * rank] = rows.astype(jnp.bfloat16)


def packed_grads(me, owners, tokens, blocks, places, before, cotangent, mask):
    rank, width = blocks[0].shape[-2], cotangent.shape[1]
    share = width * rank // LANES // sum(len(ks) for ks in owners)
    return pl.pallas_call(
        functools.partial(grads_kernel, owners, places),
        out_shape=[jax.ShapeDtypeStruct((len(ks), share, LANES), jnp.bfloat16) for ks in owners],
        in_specs=[SMEM] + [VMEM] * (len(blocks) + 4),
        out_specs=[VMEM] * len(owners),
        scratch_shapes=[pltpu.VMEM((width, rank), jnp.float32)],
        compiler_params=pltpu.CompilerParams(vmem_limit_bytes=6 * MIB),
        cost_estimate=pl.CostEstimate(flops=100000000, bytes_accessed=2000000, transcendentals=0),
        name="grads",
    )(me, tokens, *blocks, before, cotangent, mask)


def features_kernel(places, count, me, *refs):
    arrays, weights = refs[:count], refs[count]
    keep, send, x, left, total = refs[-5:]
    n = len(places)
    share = arrays[0].shape[1]
    pitch = x.shape[1] // n
    for k, (source, entry) in enumerate(places):
        rows = arrays[source][entry]
        place = pl.multiple_of((me[0] ^ k) * pitch, pitch)
        for h in range(x.shape[0]):
            x[h, pl.ds(place, share), :] = rows[:, h * 128 : (h + 1) * 128].astype(jnp.float32)
    for j in range(share):
        for h in range(x.shape[0]):
            at = j * LANES + h * 128
            left[:, at : at + 128] = x[h, pl.ds(j, n, stride=pitch), :].astype(jnp.bfloat16)
    total[...] = jnp.dot(left[...], weights[...], preferred_element_type=jnp.float32)
    part = keep.shape[1]
    mine = pl.multiple_of((me[0] & 1) * part, part)
    partner = pl.multiple_of((1 - (me[0] & 1)) * part, part)
    keep[...] = total[:, pl.ds(mine, part)]
    send[...] = total[:, pl.ds(partner, part)].astype(jnp.bfloat16)


def partial_features(me, arrays, places, projection, after):
    n = len(places)
    share = arrays[0].shape[1]
    depth, width = projection.shape
    half = (n, width // 2)
    return pl.pallas_call(
        functools.partial(features_kernel, places, len(arrays)),
        out_shape=[jax.ShapeDtypeStruct(half, jnp.float32), jax.ShapeDtypeStruct(half, jnp.bfloat16)],
        in_specs=[SMEM] + [VMEM] * (len(arrays) + 1) + [ANY],
        out_specs=[VMEM, VMEM],
        scratch_shapes=[
            pltpu.VMEM((LANES // 128, n * max(share, 8), 128), jnp.float32),
            pltpu.VMEM((n, depth), jnp.bfloat16),
            pltpu.VMEM((n, width), jnp.float32),
        ],
        compiler_params=pltpu.CompilerParams(vmem_limit_bytes=4 * MIB),
        cost_estimate=pl.CostEstimate(flops=600000000, bytes_accessed=34000000, transcendentals=0),
        name="features",
    )(me, *arrays, in_vmem(projection), after)


def scores_kernel(me, targets, partner_targets, kept, *refs):
    mine, send = refs[-2:]
    features = kept[...]
    for arrived in refs[:-2]:
        features += arrived[...].astype(jnp.float32)
    count, half = features.shape
    start = pl.multiple_of((me[0] & 1) * half, half)
    high = lax.Precision.HIGHEST
    ones = jnp.ones((targets.shape[0], half), jnp.float32)
    squares = lax.dot_general(ones, features * features, NT, precision=high, preferred_element_type=jnp.float32)
    rest = jnp.zeros((targets.shape[0], mine.shape[1] - 2 * count), jnp.float32)
    for source, out in ((targets, mine), (partner_targets, send)):
        scale = lax.rsqrt(jnp.sum(source[...] * source[...], axis=1, keepdims=True) / PDIM + 1e-06)
        dots = lax.dot_general(
            source[:, pl.ds(start, half)], features, NT, precision=high, preferred_element_type=jnp.float32
        )
        parts = [dots * scale, squares] + ([rest] if rest.shape[1] else [])
        out[...] = jnp.concatenate(parts, axis=1)


def partial_scores(me, targets, partner_targets, kept, arrived):
    shape = jax.ShapeDtypeStruct((targets.shape[0], 128), jnp.float32)
    return pl.pallas_call(
        scores_kernel,
        out_shape=[shape, shape],
        in_specs=[SMEM] + [VMEM] * (3 + len(arrived)),
        out_specs=[VMEM, VMEM],
        compiler_params=pltpu.CompilerParams(vmem_limit_bytes=6 * MIB),
        name="partial_scores",
    )(me, targets, partner_targets, kept, *arrived)


def body(tokens, cotangent, response_loss_mask, adapter_down_weight, projection, targets):
    n = lax.axis_size("shard")
    far = n // NEAR
    me = lax.axis_index("shard").astype(jnp.int32).reshape(1)
    block = adapter_down_weight
    bits = [1 << i for i in range(n.bit_length() - 1)]

    whole = [(tokens, 0, tokens.shape[0]), (cotangent, 0, cotangent.shape[0])]
    whole += [(response_loss_mask.reshape(1, -1), 0, 1), (targets, 0, targets.shape[0])]
    tokens, cotangent, mask, targets = load("load_1", whole, (me,))
    order = [far - 1] + list(range(1, far - 1)) + [0]
    column = [swap(block, NEAR * d, n) for d in order[:-1]] + [block]
    across = [swap(value, 2, n) for value in column]
    places = [[[NEAR * d + k] for d in order] for k in range(NEAR)]
    blocks, owners = column + across[:1] + across[-1:], places[0] + places[2][:1] + places[2][-1:]
    total = partial_lowrank("lowrank_1", me, tokens, blocks, owners)
    picks = [[(i,) for i in range(far)]]
    (line,) = join("join_column", column, picks, block.shape, (total,))
    (gathered,) = join("join_across", across, picks, block.shape)
    other = [swap(line, 1, n), swap(gathered, 1, n)]
    total = partial_lowrank("lowrank_2", me, tokens, across[1:-1], places[2][1:-1], (total,))
    owners = [[k + 1 for part in side for k in part] for side in (places[0], places[2])]
    total = partial_lowrank("lowrank_3", me, tokens, other[:1], owners[:1], (total,))

    stages = [bits[i : i + 2] for i in range(2, len(bits), 2)] + [bits[:2]]
    left = span([b for stage in stages[1:] for b in stage])
    moves = span(stages[0])
    targets_of = [[m ^ r for r in left] for m in moves]
    rows = packed_grads(me, targets_of, tokens, other[1:], owners[1:], total, cotangent, mask)
    rows = list(rows)
    rows[-1] = hold("hold_rows", rows[-1], (), HIDE)
    arrays = [swap(array, m, n) for array, m in zip(rows[:0:-1], moves[:0:-1])] + [rows[0]]
    held = {(m, r): (a, i) for a, m in enumerate(moves[::-1]) for i, r in enumerate(left)}
    for number, stage in enumerate(stages[1:]):
        moves, left = span(stage), span([b for later in stages[number + 2 :] for b in later])
        pairs = [[(src, r ^ m) for src in sorted({s for s, _ in held}) for r in left] for m in moves]
        picks = [[held[pair] for pair in group] for group in pairs[1:]]
        sent = join(f"join_rows_{number}", arrays, picks, rows[0].shape[1:])
        came = [swap(array, m, n) for array, m in zip(sent[::-1], moves[:0:-1])]
        kept = {pair: (held[pair][0] + len(came), held[pair][1]) for pair in pairs[0]}
        for a, (m, group) in enumerate(zip(moves[:0:-1], pairs[:0:-1])):
            kept.update({(src ^ m, r ^ m): (a, i) for i, (src, r) in enumerate(group)})
        arrays, held = came + arrays, kept
    partner_targets = swap(targets, 1, n)

    places = [held[k, 0] for k in range(n)]
    kept, send = partial_features(me, arrays, places, projection, partner_targets)
    kept = kept + swap(send, 1, n).astype(jnp.float32)
    for stage in [bits[1:3]] + [[bit] for bit in bits[3:]]:
        half = kept.astype(jnp.bfloat16)
        arrived = [swap(half, m, n) for m in span(stage)[:0:-1]]
        if bits[-1] not in stage:
            for value in arrived:
                kept = kept + value.astype(jnp.float32)
    mine, send = partial_scores(me, targets, partner_targets, kept, arrived)
    total = mine + swap(send, 1, n)
    scale = lax.rsqrt(total[:, n : 2 * n] / PDIM + 1e-06)
    return (total[:, :n] * scale / PDIM).T


def solution(mesh):
    in_specs = (
        P(("groups", "shard"), None),
        P(("groups", "shard"), None),
        P(("groups", "shard")),
        P(None, "shard"),
        P("shard", None),
        P(("groups", "shard"), None),
    )
    out_specs = P("groups", "shard")
    return jax.shard_map(body, mesh=mesh, in_specs=in_specs, out_specs=out_specs, check_vma=False)
```

```python
import functools

import jax
import jax.numpy as jnp
from jax import lax
from jax.experimental import pallas as pl
from jax.experimental.pallas import tpu as pltpu
from jax.sharding import PartitionSpec as P

PDIM = 4096
LENGTH = 256
LANES = 256
NEAR = 4
MIB = 1 << 20
HIDE = 30 * 10**9
NT = (((1,), (1,)), ((), ()))
VMEM = pl.BlockSpec(memory_space=pltpu.VMEM)
SMEM = pl.BlockSpec(memory_space=pltpu.SMEM)
ANY = pl.BlockSpec(memory_space=pl.ANY)


def swap(value, bit, n):
    return lax.ppermute(value, "shard", [(s, s ^ bit) for s in range(n)])


def span(bits):
    sums = [0]
    for bit in bits:
        sums += [k + bit for k in sums]
    return sums


def in_hbm(value):
    return pltpu.with_memory_space_constraint(value, pltpu.HBM)


def in_vmem(value):
    return pltpu.with_memory_space_constraint(value, pltpu.VMEM)


def load_kernel(count, starts, *refs):
    sources, outs, sems = refs[:count], refs[-1 - count : -1], refs[-1]
    copies = []
    for source, start, out in zip(sources, starts, outs):
        rows = out.shape[0]
        step = min(rows, LANES // 2)
        for i in range(0, rows, step):
            part = source.at[pl.ds(start + i, step)]
            copies.append(pltpu.make_async_copy(part, out.at[pl.ds(i, step)], sems.at[len(copies)]))
    for copy in copies:
        copy.start()
    for copy in copies:
        copy.wait()


def load(name, parts, after):
    size = sum(rows * array.size // array.shape[0] * array.dtype.itemsize for array, _, rows in parts)
    pieces = sum(max(rows // (LANES // 2), 1) for _, _, rows in parts)
    return pl.pallas_call(
        functools.partial(load_kernel, len(parts), [start for _, start, _ in parts]),
        out_shape=[pltpu.VMEM((rows,) + array.shape[1:], array.dtype) for array, _, rows in parts],
        in_specs=[ANY] * (len(parts) + len(after)),
        out_specs=[VMEM] * len(parts),
        scratch_shapes=[pltpu.SemaphoreType.DMA((pieces,))],
        compiler_params=pltpu.CompilerParams(vmem_limit_bytes=MIB),
        cost_estimate=pl.CostEstimate(flops=0, bytes_accessed=2 * size, transcendentals=0),
        name=name,
    )(*[in_hbm(array) for array, _, _ in parts], *after)


def hold(name, value, after, flops=0):
    return pl.pallas_call(
        lambda *refs: None,
        out_shape=jax.ShapeDtypeStruct(value.shape, value.dtype),
        in_specs=[ANY] * (1 + len(after)),
        out_specs=ANY,
        input_output_aliases={0: 0},
        compiler_params=pltpu.CompilerParams(vmem_limit_bytes=MIB),
        cost_estimate=pl.CostEstimate(flops=flops, bytes_accessed=2000000, transcendentals=0),
        name=name,
    )(value, *after)


def join_kernel(picks, *refs):
    for pick, out in zip(picks, refs[-len(picks) :]):
        for target, (source, *entry) in enumerate(pick):
            out[target] = refs[source][entry[0]] if entry else refs[source][...]


def join(name, values, picks, shape, after=(), flops=0):
    return pl.pallas_call(
        functools.partial(join_kernel, picks),
        out_shape=[jax.ShapeDtypeStruct((len(pick),) + shape, values[0].dtype) for pick in picks],
        in_specs=[VMEM] * len(values) + [ANY] * len(after),
        out_specs=[VMEM] * len(picks),
        compiler_params=pltpu.CompilerParams(vmem_limit_bytes=2 * MIB),
        cost_estimate=pl.CostEstimate(flops=flops, bytes_accessed=2000000, transcendentals=0),
        name=name,
    )(*values, *after)


def add_lowrank(total, me, blocks, places, tokens):
    for block, owners in zip(blocks, places):
        depth = block.shape[-1]
        for i, k in enumerate(owners):
            start = pl.multiple_of((me[0] ^ k) * depth, depth)
            part = block[i] if len(block.shape) == 3 else block[...]
            total += lax.dot_general(part, tokens[:, pl.ds(start, depth)], NT, preferred_element_type=jnp.float32)
    return total


def lowrank_kernel(places, me, tokens, *refs):
    blocks, out = refs[: len(places)], refs[-1]
    before = refs[len(places)][...] if len(refs) > len(places) + 1 else jnp.zeros(out.shape, jnp.float32)
    out[...] = add_lowrank(before, me, blocks, places, tokens)


def partial_lowrank(name, me, tokens, blocks, places, before=()):
    return pl.pallas_call(
        functools.partial(lowrank_kernel, places),
        out_shape=jax.ShapeDtypeStruct((blocks[0].shape[-2], tokens.shape[0]), jnp.float32),
        in_specs=[SMEM] + [VMEM] * (1 + len(blocks) + len(before)),
        out_specs=VMEM,
        compiler_params=pltpu.CompilerParams(vmem_limit_bytes=2 * MIB),
        cost_estimate=pl.CostEstimate(flops=100000000, bytes_accessed=2000000, transcendentals=0),
        name=name,
    )(me, tokens, *blocks, *before)


def grads_kernel(owners, places, me, tokens, *refs):
    blocks = refs[: len(places)]
    before, cotangent, mask = refs[len(places) : len(places) + 3]
    outs, grads = refs[-1 - len(owners) : -1], refs[-1]
    total = add_lowrank(before[...], me, blocks, places, tokens)
    rank = total.shape[0]
    lowrank = total.astype(jnp.bfloat16) * mask[...].astype(jnp.bfloat16)
    turned = jnp.dot(lowrank, cotangent[...], preferred_element_type=jnp.float32)
    grads[...] = turned.T
    pack = LANES // rank
    share = outs[0].shape[1]
    for out, ks in zip(outs, owners):
        for i, k in enumerate(ks):
            start = pl.multiple_of((me[0] ^ k) * (share * pack), share * pack)
            for q in range(pack):
                rows = grads[pl.ds(start + q, share, stride=pack), :]
                out[i, :, q * rank : (q + 1) * rank] = rows.astype(jnp.bfloat16)


def packed_grads(me, owners, tokens, blocks, places, before, cotangent, mask):
    rank, width = blocks[0].shape[-2], cotangent.shape[1]
    share = width * rank // LANES // sum(len(ks) for ks in owners)
    return pl.pallas_call(
        functools.partial(grads_kernel, owners, places),
        out_shape=[jax.ShapeDtypeStruct((len(ks), share, LANES), jnp.bfloat16) for ks in owners],
        in_specs=[SMEM] + [VMEM] * (len(blocks) + 4),
        out_specs=[VMEM] * len(owners),
        scratch_shapes=[pltpu.VMEM((width, rank), jnp.float32)],
        compiler_params=pltpu.CompilerParams(vmem_limit_bytes=6 * MIB),
        cost_estimate=pl.CostEstimate(flops=100000000, bytes_accessed=2000000, transcendentals=0),
        name="grads",
    )(me, tokens, *blocks, before, cotangent, mask)


def features_kernel(places, count, me, *refs):
    arrays, weights = refs[:count], refs[count]
    keep, send, x, left, total = refs[-5:]
    n = len(places)
    share = arrays[0].shape[1]
    pitch = x.shape[1] // n
    for k, (source, entry) in enumerate(places):
        rows = arrays[source][entry]
        place = pl.multiple_of((me[0] ^ k) * pitch, pitch)
        for h in range(x.shape[0]):
            x[h, pl.ds(place, share), :] = rows[:, h * 128 : (h + 1) * 128].astype(jnp.float32)
    for j in range(share):
        for h in range(x.shape[0]):
            at = j * LANES + h * 128
            left[:, at : at + 128] = x[h, pl.ds(j, n, stride=pitch), :].astype(jnp.bfloat16)
    total[...] = jnp.dot(left[...], weights[...], preferred_element_type=jnp.float32)
    part = keep.shape[1]
    mine = pl.multiple_of((me[0] & 1) * part, part)
    partner = pl.multiple_of((1 - (me[0] & 1)) * part, part)
    keep[...] = total[:, pl.ds(mine, part)]
    send[...] = total[:, pl.ds(partner, part)].astype(jnp.bfloat16)


def partial_features(me, arrays, places, projection, after):
    n = len(places)
    share = arrays[0].shape[1]
    depth, width = projection.shape
    half = (n, width // 2)
    return pl.pallas_call(
        functools.partial(features_kernel, places, len(arrays)),
        out_shape=[jax.ShapeDtypeStruct(half, jnp.float32), jax.ShapeDtypeStruct(half, jnp.bfloat16)],
        in_specs=[SMEM] + [VMEM] * (len(arrays) + 1) + [ANY],
        out_specs=[VMEM, VMEM],
        scratch_shapes=[
            pltpu.VMEM((LANES // 128, n * max(share, 8), 128), jnp.float32),
            pltpu.VMEM((n, depth), jnp.bfloat16),
            pltpu.VMEM((n, width), jnp.float32),
        ],
        compiler_params=pltpu.CompilerParams(vmem_limit_bytes=4 * MIB),
        cost_estimate=pl.CostEstimate(flops=600000000, bytes_accessed=34000000, transcendentals=0),
        name="features",
    )(me, *arrays, in_vmem(projection), after)


def scores_kernel(me, targets, partner_targets, kept, *refs):
    mine, send = refs[-2:]
    features = kept[...]
    for arrived in refs[:-2]:
        features += arrived[...].astype(jnp.float32)
    count, half = features.shape
    start = pl.multiple_of((me[0] & 1) * half, half)
    high = lax.Precision.HIGHEST
    ones = jnp.ones((targets.shape[0], half), jnp.float32)
    squares = lax.dot_general(ones, features * features, NT, precision=high, preferred_element_type=jnp.float32)
    rest = jnp.zeros((targets.shape[0], mine.shape[1] - 2 * count), jnp.float32)
    for source, out in ((targets, mine), (partner_targets, send)):
        scale = lax.rsqrt(jnp.sum(source[...] * source[...], axis=1, keepdims=True) / PDIM + 1e-06)
        dots = lax.dot_general(
            source[:, pl.ds(start, half)], features, NT, precision=high, preferred_element_type=jnp.float32
        )
        parts = [dots * scale, squares] + ([rest] if rest.shape[1] else [])
        out[...] = jnp.concatenate(parts, axis=1)


def partial_scores(me, targets, partner_targets, kept, arrived):
    shape = jax.ShapeDtypeStruct((targets.shape[0], 128), jnp.float32)
    return pl.pallas_call(
        scores_kernel,
        out_shape=[shape, shape],
        in_specs=[SMEM] + [VMEM] * (3 + len(arrived)),
        out_specs=[VMEM, VMEM],
        compiler_params=pltpu.CompilerParams(vmem_limit_bytes=6 * MIB),
        name="partial_scores",
    )(me, targets, partner_targets, kept, *arrived)


def body(tokens, cotangent, response_loss_mask, adapter_down_weight, projection, targets):
    n = lax.axis_size("shard")
    far = n // NEAR
    me = lax.axis_index("shard").astype(jnp.int32).reshape(1)
    block = adapter_down_weight
    bits = [1 << i for i in range(n.bit_length() - 1)]

    whole = [(tokens, 0, tokens.shape[0]), (cotangent, 0, cotangent.shape[0])]
    whole += [(response_loss_mask.reshape(1, -1), 0, 1), (targets, 0, targets.shape[0])]
    tokens, cotangent, mask, targets = load("load_1", whole, (me,))
    order = [far - 1] + list(range(1, far - 1)) + [0]
    column = [swap(block, NEAR * d, n) for d in order[:-1]] + [block]
    across = [swap(value, 2, n) for value in column]
    places = [[[NEAR * d + k] for d in order] for k in range(NEAR)]
    blocks, owners = column + across[:1] + across[-1:], places[0] + places[2][:1] + places[2][-1:]
    total = partial_lowrank("lowrank_1", me, tokens, blocks, owners)
    picks = [[(i,) for i in range(far)]]
    (line,) = join("join_column", column, picks, block.shape, (total,))
    (gathered,) = join("join_across", across, picks, block.shape)
    other = [swap(line, 1, n), swap(gathered, 1, n)]
    total = partial_lowrank("lowrank_2", me, tokens, across[1:-1], places[2][1:-1], (total,))
    owners = [[k + 1 for part in side for k in part] for side in (places[0], places[2])]
    total = partial_lowrank("lowrank_3", me, tokens, other[:1], owners[:1], (total,))

    stages = [bits[i : i + 2] for i in range(2, len(bits), 2)] + [bits[:2]]
    left = span([b for stage in stages[1:] for b in stage])
    moves = span(stages[0])
    targets_of = [[m ^ r for r in left] for m in moves]
    rows = packed_grads(me, targets_of, tokens, other[1:], owners[1:], total, cotangent, mask)
    rows = list(rows)
    rows[-1] = hold("hold_rows", rows[-1], (), HIDE)
    turns = [len(moves) - 1] + list(range(1, len(moves) - 1)) + [0]
    arrays = [swap(rows[a], moves[a], n) if a else rows[a] for a in turns]
    held = {(moves[a], r): (place, i) for place, a in enumerate(turns) for i, r in enumerate(left)}
    for number, stage in enumerate(stages[1:]):
        moves, left = span(stage), span([b for later in stages[number + 2 :] for b in later])
        pairs = [[(src, r ^ m) for src in sorted({s for s, _ in held}) for r in left] for m in moves]
        picks = [[held[pair] for pair in group] for group in pairs[1:]]
        sent = join(f"join_rows_{number}", arrays, picks, rows[0].shape[1:])
        came = [swap(array, m, n) for array, m in zip(sent[::-1], moves[:0:-1])]
        kept = {pair: (held[pair][0] + len(came), held[pair][1]) for pair in pairs[0]}
        for a, (m, group) in enumerate(zip(moves[:0:-1], pairs[:0:-1])):
            kept.update({(src ^ m, r ^ m): (a, i) for i, (src, r) in enumerate(group)})
        arrays, held = came + arrays, kept
    partner_targets = swap(targets, 1, n)

    places = [held[k, 0] for k in range(n)]
    kept, send = partial_features(me, arrays, places, projection, partner_targets)
    kept = kept + swap(send, 1, n).astype(jnp.float32)
    for stage in [bits[1:3]] + [[bit] for bit in bits[3:]]:
        half = kept.astype(jnp.bfloat16)
        arrived = [swap(half, m, n) for m in span(stage)[:0:-1]]
        if bits[-1] not in stage:
            for value in arrived:
                kept = kept + value.astype(jnp.float32)
    mine, send = partial_scores(me, targets, partner_targets, kept, arrived)
    total = mine + swap(send, 1, n)
    scale = lax.rsqrt(total[:, n : 2 * n] / PDIM + 1e-06)
    return (total[:, :n] * scale / PDIM).T


def solution(mesh):
    in_specs = (
        P(("groups", "shard"), None),
        P(("groups", "shard"), None),
        P(("groups", "shard")),
        P(None, "shard"),
        P("shard", None),
        P(("groups", "shard"), None),
    )
    out_specs = P("groups", "shard")
    return jax.shard_map(body, mesh=mesh, in_specs=in_specs, out_specs=out_specs, check_vma=False)
```

```python
import functools

import jax
import jax.numpy as jnp
from jax import lax
from jax.experimental import pallas as pl
from jax.experimental.pallas import tpu as pltpu
from jax.sharding import PartitionSpec as P

PDIM = 4096
LENGTH = 256
LANES = 256
NEAR = 4
MIB = 1 << 20
HIDE = 30 * 10**9
NT = (((1,), (1,)), ((), ()))
VMEM = pl.BlockSpec(memory_space=pltpu.VMEM)
SMEM = pl.BlockSpec(memory_space=pltpu.SMEM)
ANY = pl.BlockSpec(memory_space=pl.ANY)


def swap(value, bit, n):
    return lax.ppermute(value, "shard", [(s, s ^ bit) for s in range(n)])


def span(bits):
    sums = [0]
    for bit in bits:
        sums += [k + bit for k in sums]
    return sums


def in_hbm(value):
    return pltpu.with_memory_space_constraint(value, pltpu.HBM)


def in_vmem(value):
    return pltpu.with_memory_space_constraint(value, pltpu.VMEM)


def load_kernel(count, starts, *refs):
    sources, outs, sems = refs[:count], refs[-1 - count : -1], refs[-1]
    copies = []
    for source, start, out in zip(sources, starts, outs):
        rows = out.shape[0]
        step = min(rows, LANES // 8)
        for i in range(0, rows, step):
            part = source.at[pl.ds(start + i, step)]
            copies.append(pltpu.make_async_copy(part, out.at[pl.ds(i, step)], sems.at[len(copies)]))
    for copy in copies:
        copy.start()
    for copy in copies:
        copy.wait()


def load(name, parts, after):
    size = sum(rows * array.size // array.shape[0] * array.dtype.itemsize for array, _, rows in parts)
    pieces = sum(max(rows // (LANES // 8), 1) for _, _, rows in parts)
    return pl.pallas_call(
        functools.partial(load_kernel, len(parts), [start for _, start, _ in parts]),
        out_shape=[pltpu.VMEM((rows,) + array.shape[1:], array.dtype) for array, _, rows in parts],
        in_specs=[ANY] * (len(parts) + len(after)),
        out_specs=[VMEM] * len(parts),
        scratch_shapes=[pltpu.SemaphoreType.DMA((pieces,))],
        compiler_params=pltpu.CompilerParams(vmem_limit_bytes=MIB),
        cost_estimate=pl.CostEstimate(flops=0, bytes_accessed=2 * size, transcendentals=0),
        name=name,
    )(*[in_hbm(array) for array, _, _ in parts], *after)


def hold(name, value, after, flops=0):
    return pl.pallas_call(
        lambda *refs: None,
        out_shape=jax.ShapeDtypeStruct(value.shape, value.dtype),
        in_specs=[ANY] * (1 + len(after)),
        out_specs=ANY,
        input_output_aliases={0: 0},
        compiler_params=pltpu.CompilerParams(vmem_limit_bytes=MIB),
        cost_estimate=pl.CostEstimate(flops=flops, bytes_accessed=2000000, transcendentals=0),
        name=name,
    )(value, *after)


def join_kernel(picks, *refs):
    for pick, out in zip(picks, refs[-len(picks) :]):
        for target, (source, *entry) in enumerate(pick):
            out[target] = refs[source][entry[0]] if entry else refs[source][...]


def join(name, values, picks, shape, after=(), flops=0):
    return pl.pallas_call(
        functools.partial(join_kernel, picks),
        out_shape=[jax.ShapeDtypeStruct((len(pick),) + shape, values[0].dtype) for pick in picks],
        in_specs=[VMEM] * len(values) + [ANY] * len(after),
        out_specs=[VMEM] * len(picks),
        compiler_params=pltpu.CompilerParams(vmem_limit_bytes=2 * MIB),
        cost_estimate=pl.CostEstimate(flops=flops, bytes_accessed=2000000, transcendentals=0),
        name=name,
    )(*values, *after)


def add_lowrank(total, me, blocks, places, tokens):
    for block, owners in zip(blocks, places):
        depth = block.shape[-1]
        for i, k in enumerate(owners):
            start = pl.multiple_of((me[0] ^ k) * depth, depth)
            part = block[i] if len(block.shape) == 3 else block[...]
            total += lax.dot_general(part, tokens[:, pl.ds(start, depth)], NT, preferred_element_type=jnp.float32)
    return total


def lowrank_kernel(places, me, tokens, *refs):
    blocks, out = refs[: len(places)], refs[-1]
    before = refs[len(places)][...] if len(refs) > len(places) + 1 else jnp.zeros(out.shape, jnp.float32)
    out[...] = add_lowrank(before, me, blocks, places, tokens)


def partial_lowrank(name, me, tokens, blocks, places, before=()):
    return pl.pallas_call(
        functools.partial(lowrank_kernel, places),
        out_shape=jax.ShapeDtypeStruct((blocks[0].shape[-2], tokens.shape[0]), jnp.float32),
        in_specs=[SMEM] + [VMEM] * (1 + len(blocks) + len(before)),
        out_specs=VMEM,
        compiler_params=pltpu.CompilerParams(vmem_limit_bytes=2 * MIB),
        cost_estimate=pl.CostEstimate(flops=100000000, bytes_accessed=2000000, transcendentals=0),
        name=name,
    )(me, tokens, *blocks, *before)


def grads_kernel(owners, places, me, tokens, *refs):
    blocks = refs[: len(places)]
    before, cotangent, mask = refs[len(places) : len(places) + 3]
    outs, grads = refs[-1 - len(owners) : -1], refs[-1]
    total = add_lowrank(before[...], me, blocks, places, tokens)
    rank = total.shape[0]
    lowrank = total.astype(jnp.bfloat16) * mask[...].astype(jnp.bfloat16)
    turned = jnp.dot(lowrank, cotangent[...], preferred_element_type=jnp.float32)
    grads[...] = turned.T
    pack = LANES // rank
    share = outs[0].shape[1]
    for out, ks in zip(outs, owners):
        for i, k in enumerate(ks):
            start = pl.multiple_of((me[0] ^ k) * (share * pack), share * pack)
            for q in range(pack):
                rows = grads[pl.ds(start + q, share, stride=pack), :]
                out[i, :, q * rank : (q + 1) * rank] = rows.astype(jnp.bfloat16)


def packed_grads(me, owners, tokens, blocks, places, before, cotangent, mask):
    rank, width = blocks[0].shape[-2], cotangent.shape[1]
    share = width * rank // LANES // sum(len(ks) for ks in owners)
    return pl.pallas_call(
        functools.partial(grads_kernel, owners, places),
        out_shape=[jax.ShapeDtypeStruct((len(ks), share, LANES), jnp.bfloat16) for ks in owners],
        in_specs=[SMEM] + [VMEM] * (len(blocks) + 4),
        out_specs=[VMEM] * len(owners),
        scratch_shapes=[pltpu.VMEM((width, rank), jnp.float32)],
        compiler_params=pltpu.CompilerParams(vmem_limit_bytes=6 * MIB),
        cost_estimate=pl.CostEstimate(flops=100000000, bytes_accessed=2000000, transcendentals=0),
        name="grads",
    )(me, tokens, *blocks, before, cotangent, mask)


def features_kernel(places, count, me, *refs):
    arrays, weights = refs[:count], refs[count]
    keep, send, x, left, total = refs[-5:]
    n = len(places)
    share = arrays[0].shape[1]
    pitch = x.shape[1] // n
    for k, (source, entry) in enumerate(places):
        rows = arrays[source][entry]
        place = pl.multiple_of((me[0] ^ k) * pitch, pitch)
        for h in range(x.shape[0]):
            x[h, pl.ds(place, share), :] = rows[:, h * 128 : (h + 1) * 128].astype(jnp.float32)
    for j in range(share):
        for h in range(x.shape[0]):
            at = j * LANES + h * 128
            left[:, at : at + 128] = x[h, pl.ds(j, n, stride=pitch), :].astype(jnp.bfloat16)
    total[...] = jnp.dot(left[...], weights[...], preferred_element_type=jnp.float32)
    part = keep.shape[1]
    mine = pl.multiple_of((me[0] & 1) * part, part)
    partner = pl.multiple_of((1 - (me[0] & 1)) * part, part)
    keep[...] = total[:, pl.ds(mine, part)]
    send[...] = total[:, pl.ds(partner, part)].astype(jnp.bfloat16)


def partial_features(me, arrays, places, projection, after):
    n = len(places)
    share = arrays[0].shape[1]
    depth, width = projection.shape
    half = (n, width // 2)
    return pl.pallas_call(
        functools.partial(features_kernel, places, len(arrays)),
        out_shape=[jax.ShapeDtypeStruct(half, jnp.float32), jax.ShapeDtypeStruct(half, jnp.bfloat16)],
        in_specs=[SMEM] + [VMEM] * (len(arrays) + 1) + [ANY],
        out_specs=[VMEM, VMEM],
        scratch_shapes=[
            pltpu.VMEM((LANES // 128, n * max(share, 8), 128), jnp.float32),
            pltpu.VMEM((n, depth), jnp.bfloat16),
            pltpu.VMEM((n, width), jnp.float32),
        ],
        compiler_params=pltpu.CompilerParams(vmem_limit_bytes=4 * MIB),
        cost_estimate=pl.CostEstimate(flops=600000000, bytes_accessed=34000000, transcendentals=0),
        name="features",
    )(me, *arrays, in_vmem(projection), after)


def scores_kernel(me, targets, partner_targets, kept, *refs):
    mine, send = refs[-2:]
    features = kept[...]
    for arrived in refs[:-2]:
        features += arrived[...].astype(jnp.float32)
    count, half = features.shape
    start = pl.multiple_of((me[0] & 1) * half, half)
    high = lax.Precision.HIGHEST
    ones = jnp.ones((targets.shape[0], half), jnp.float32)
    squares = lax.dot_general(ones, features * features, NT, precision=high, preferred_element_type=jnp.float32)
    rest = jnp.zeros((targets.shape[0], mine.shape[1] - 2 * count), jnp.float32)
    for source, out in ((targets, mine), (partner_targets, send)):
        scale = lax.rsqrt(jnp.sum(source[...] * source[...], axis=1, keepdims=True) / PDIM + 1e-06)
        dots = lax.dot_general(
            source[:, pl.ds(start, half)], features, NT, precision=high, preferred_element_type=jnp.float32
        )
        parts = [dots * scale, squares] + ([rest] if rest.shape[1] else [])
        out[...] = jnp.concatenate(parts, axis=1)


def partial_scores(me, targets, partner_targets, kept, arrived):
    shape = jax.ShapeDtypeStruct((targets.shape[0], 128), jnp.float32)
    return pl.pallas_call(
        scores_kernel,
        out_shape=[shape, shape],
        in_specs=[SMEM] + [VMEM] * (3 + len(arrived)),
        out_specs=[VMEM, VMEM],
        compiler_params=pltpu.CompilerParams(vmem_limit_bytes=6 * MIB),
        name="partial_scores",
    )(me, targets, partner_targets, kept, *arrived)


def body(tokens, cotangent, response_loss_mask, adapter_down_weight, projection, targets):
    n = lax.axis_size("shard")
    far = n // NEAR
    me = lax.axis_index("shard").astype(jnp.int32).reshape(1)
    block = adapter_down_weight
    bits = [1 << i for i in range(n.bit_length() - 1)]

    whole = [(tokens, 0, tokens.shape[0]), (cotangent, 0, cotangent.shape[0])]
    whole += [(response_loss_mask.reshape(1, -1), 0, 1), (targets, 0, targets.shape[0])]
    tokens, cotangent, mask, targets = load("load_1", whole, (me,))
    order = [far - 1] + list(range(1, far - 1)) + [0]
    column = [swap(block, NEAR * d, n) for d in order[:-1]] + [block]
    across = [swap(value, 2, n) for value in column]
    places = [[[NEAR * d + k] for d in order] for k in range(NEAR)]
    blocks, owners = column + across[:1] + across[-1:], places[0] + places[2][:1] + places[2][-1:]
    total = partial_lowrank("lowrank_1", me, tokens, blocks, owners)
    picks = [[(i,) for i in range(far)]]
    (line,) = join("join_column", column, picks, block.shape, (total,))
    (gathered,) = join("join_across", across, picks, block.shape)
    other = [swap(line, 1, n), swap(gathered, 1, n)]
    total = partial_lowrank("lowrank_2", me, tokens, across[1:-1], places[2][1:-1], (total,))
    owners = [[k + 1 for part in side for k in part] for side in (places[0], places[2])]
    total = partial_lowrank("lowrank_3", me, tokens, other[:1], owners[:1], (total,))

    stages = [bits[i : i + 2] for i in range(2, len(bits), 2)] + [bits[:2]]
    left = span([b for stage in stages[1:] for b in stage])
    moves = span(stages[0])
    targets_of = [[m ^ r for r in left] for m in moves]
    rows = packed_grads(me, targets_of, tokens, other[1:], owners[1:], total, cotangent, mask)
    rows = list(rows)
    rows[-1] = hold("hold_rows", rows[-1], (), HIDE)
    arrays = [swap(array, m, n) for array, m in zip(rows[:0:-1], moves[:0:-1])] + [rows[0]]
    held = {(m, r): (a, i) for a, m in enumerate(moves[::-1]) for i, r in enumerate(left)}
    for number, stage in enumerate(stages[1:]):
        moves, left = span(stage), span([b for later in stages[number + 2 :] for b in later])
        pairs = [[(src, r ^ m) for src in sorted({s for s, _ in held}) for r in left] for m in moves]
        picks = [[held[pair] for pair in group] for group in pairs[1:]]
        sent = join(f"join_rows_{number}", arrays, picks, rows[0].shape[1:])
        came = [swap(array, m, n) for array, m in zip(sent[::-1], moves[:0:-1])]
        kept = {pair: (held[pair][0] + len(came), held[pair][1]) for pair in pairs[0]}
        for a, (m, group) in enumerate(zip(moves[:0:-1], pairs[:0:-1])):
            kept.update({(src ^ m, r ^ m): (a, i) for i, (src, r) in enumerate(group)})
        arrays, held = came + arrays, kept
    partner_targets = swap(targets, 1, n)

    places = [held[k, 0] for k in range(n)]
    kept, send = partial_features(me, arrays, places, projection, partner_targets)
    kept = kept + swap(send, 1, n).astype(jnp.float32)
    for stage in [bits[1:3]] + [[bit] for bit in bits[3:]]:
        half = kept.astype(jnp.bfloat16)
        arrived = [swap(half, m, n) for m in span(stage)[:0:-1]]
        if bits[-1] not in stage:
            for value in arrived:
                kept = kept + value.astype(jnp.float32)
    mine, send = partial_scores(me, targets, partner_targets, kept, arrived)
    total = mine + swap(send, 1, n)
    scale = lax.rsqrt(total[:, n : 2 * n] / PDIM + 1e-06)
    return (total[:, :n] * scale / PDIM).T


def solution(mesh):
    in_specs = (
        P(("groups", "shard"), None),
        P(("groups", "shard"), None),
        P(("groups", "shard")),
        P(None, "shard"),
        P("shard", None),
        P(("groups", "shard"), None),
    )
    out_specs = P("groups", "shard")
    return jax.shard_map(body, mesh=mesh, in_specs=in_specs, out_specs=out_specs, check_vma=False)
```
